32 devices in a mesh: gx: 4 (over z), gy: 2 (over x), gz: 4 (over y, core).
Axes of the slice: x: 2, y: 2, z: 4, core: 2. Of those that a mesh axis runs over, the one named last changes fastest.
Arguments:
- old_fields: float32 [2, 4, 64, 16, 1024], P(None, 'gy', 'gz', None, 'gx'), may hold values from -6 to 6
- old_coef: bfloat16 [4, 4, 64, 16, 1024], P(None, 'gy', 'gz', None, 'gx'), may hold values from 0.25 to 4
- held_slabs: int32 [4, 4, 4], P('gy', 'gz', 'gx'), may hold values from 0 to 3, as said below
Outputs:
- solution: float32 [64, 48, 1024], P('gz', 'gy', 'gx')
- residual: float32 [64, 48, 1024], P('gz', 'gy', 'gx')
The draws below stay inside these ranges and needn't reach their ends.
Inputs may be any that keep to these rules, and one draw needn't show every extreme that they name: `held_slabs`: in every column of bricks and for every p below 1, rows 4p to 4p + 3 hold the old slabs 3p, 3p + 1, 3p + 2 once each and one entry 3, which marks an empty slot.
All inputs are finite; a program needn't handle non-finite values.
Results may differ from the reference program's by a relative error of at most 0.0003.
Values may be sent and summed in bfloat16 or wider, within the bound.
No kernel may reach another device: no remote copies, remote signals or barrier semaphores. Data moves between devices by JAX's collectives and lax.ppermute only.
A program may use at most 64 MiB of HBM per device.

```python
import math
import jax
import jax.numpy as jnp

UNIT = 8
CZ = 16
CX = 256
SWEEPS = 4
SLOTS = 2
NX = 1024
NY = 48
NZ = 64
OLD_Y = 3
N_GX = 4
N_GY = 2
N_GZ = 4


def draw_held_slabs(key, part):
    pair_count = N_GY // 2
    slot_scores = jax.random.randint(key, (pair_count, N_GZ, N_GX, 4), 0, 1 << 20) * 4 + jnp.arange(4, dtype=jnp.int32)
    slot_order = jnp.argsort(slot_scores, axis=-1)
    slot_rank = jnp.argsort(slot_order, axis=-1).astype(jnp.int32)
    first_slab = (3 * jnp.arange(pair_count, dtype=jnp.int32))[:, None, None, None]
    slab_values = jnp.where(slot_rank < 3, first_slab + slot_rank, OLD_Y)
    slab_values = jnp.transpose(slab_values, (0, 3, 1, 2))
    return slab_values.reshape(2 * N_GY, N_GZ, N_GX).astype(jnp.int32)


def steps_of(own_key, dims, cuts, least, high):
    gain, own = 1.0, jax.random.fold_in(own_key, 6)
    for dim, blocks in cuts:
        draws = jnp.exp(jax.random.uniform(jax.random.fold_in(own, dim), (blocks,), jnp.float32, least / len(cuts), high / len(cuts)))
        gain = gain * jnp.repeat(draws, dims[dim] // blocks).reshape([-1 if axis == dim else 1 for axis in range(len(dims))])
    return gain


def noise(own_key, extent, deviation, most, pieces=(), kind=jnp.bfloat16):
    entries = deviation * jax.random.normal(own_key, extent, jnp.float32)
    if pieces:
        entries = entries * steps_of(own_key, extent, pieces, -0.22, 0.18)
    return jnp.clip(entries, -most, most).astype(kind)


def setup_inputs(seed: int = 0) -> dict:
    key_of = jax.random.split(jax.random.key(seed), 4)
    return {
        "old_fields": noise(key_of[0], (2, SLOTS * N_GY, NZ, 2 * UNIT, NX), 1.0, 6.0, ((1, 2), (2, 4), (4, 4)), jnp.float32),
        "old_coef": jnp.clip(jnp.exp(math.log(4.0) - 2.7725887 * jax.random.uniform(key_of[1], (4, SLOTS * N_GY, NZ, 2 * UNIT, NX), jnp.float32) ** steps_of(key_of[1], (4, SLOTS * N_GY, NZ, 2 * UNIT, NX), ((1, 2), (2, 4), (4, 4)), -0.2, 0.2)), 0.25, 4.0).astype(jnp.bfloat16),
        "held_slabs": draw_held_slabs(jax.random.fold_in(key_of[3], 71), 0),
    }


def chebyshev_weights(count):
    low_bound = 0.25
    high_bound = 2.0
    centre_value = 0.5 * (high_bound + low_bound)
    half_width = 0.5 * (high_bound - low_bound)
    ratio_value = centre_value / half_width
    damping = 1.0 / ratio_value
    first_list = [0.0]
    second_list = [1.0 / centre_value]
    for step_index in range(1, count):
        damping_next = 1.0 / (2.0 * ratio_value - damping)
        first_list.append(damping_next * damping)
        second_list.append(2.0 * damping_next / half_width)
        damping = damping_next
    return first_list, second_list


def assemble(old_array, held_slabs):
    field_count = old_array.shape[0]
    slot_total = old_array.shape[1]
    grouped = old_array.reshape(field_count, slot_total, N_GZ, CZ, 2 * UNIT, N_GX, CX)
    grouped = jnp.transpose(grouped, (1, 2, 5, 0, 3, 4, 6))
    slab_numbers = jnp.arange(OLD_Y, dtype=jnp.int32)
    slot_rows = jnp.arange(slot_total, dtype=jnp.int32)
    matches = held_slabs[None, :, :, :] == slab_numbers[:, None, None, None]
    holder_rows = jnp.sum(jnp.where(matches, slot_rows[None, :, None, None], 0), axis=1).astype(jnp.int32)
    column_z = jnp.arange(N_GZ, dtype=jnp.int32)[None, :, None]
    column_x = jnp.arange(N_GX, dtype=jnp.int32)[None, None, :]
    picked = grouped[holder_rows, column_z, column_x]
    picked = jnp.transpose(picked, (3, 1, 4, 0, 5, 2, 6))
    return picked.reshape(field_count, NZ, NY, NX)


def operator_apply(field, face_terms):
    cell_alpha, beta_x, upper_x, beta_y, upper_y, beta_z, upper_z = face_terms
    result = cell_alpha * field
    result = result + beta_x * (field - jnp.roll(field, 1, 2)) + upper_x * (field - jnp.roll(field, -1, 2))
    result = result + beta_y * (field - jnp.roll(field, 1, 1)) + upper_y * (field - jnp.roll(field, -1, 1))
    result = result + beta_z * (field - jnp.roll(field, 1, 0)) + upper_z * (field - jnp.roll(field, -1, 0))
    return result


def reference(old_fields, old_coef, held_slabs):
    grid_fields = assemble(old_fields, held_slabs)
    grid_coef = assemble(old_coef, held_slabs)
    solution = grid_fields[0]
    rhs_field = grid_fields[1]
    cell_alpha = grid_coef[0].astype(jnp.float32)
    beta_x = grid_coef[1].astype(jnp.float32)
    beta_y = grid_coef[2].astype(jnp.float32)
    beta_z = grid_coef[3].astype(jnp.float32)
    upper_x = jnp.roll(beta_x, -1, 2)
    upper_y = jnp.roll(beta_y, -1, 1)
    upper_z = jnp.roll(beta_z, -1, 0)
    face_terms = (cell_alpha, beta_x, upper_x, beta_y, upper_y, beta_z, upper_z)
    diagonal = cell_alpha + beta_x + upper_x + beta_y + upper_y + beta_z + upper_z
    inverse = 1.0 / diagonal
    first_list, second_list = chebyshev_weights(SWEEPS)
    residual = rhs_field - operator_apply(solution, face_terms)
    direction = jnp.zeros_like(solution)
    for sweep_index in range(SWEEPS):
        direction = first_list[sweep_index] * direction + second_list[sweep_index] * (inverse * residual)
        solution = solution + direction
        residual = residual - operator_apply(direction, face_terms)
    return solution, residual
```

```python
import functools

import jax
import jax.numpy as jnp
from jax import lax
from jax.experimental import pallas as pl
from jax.experimental.pallas import tpu as pltpu
from jax.sharding import PartitionSpec as P

SWEEPS = 4
LANES = 128
STRIP = 8
SHIFT = 4096.0
VMEM_LIMIT = 24 * 1024 * 1024


def chebyshev_weights(count):
    low_bound = 0.25
    high_bound = 2.0
    centre_value = 0.5 * (high_bound + low_bound)
    half_width = 0.5 * (high_bound - low_bound)
    ratio_value = centre_value / half_width
    damping = 1.0 / ratio_value
    first_list = [0.0]
    second_list = [1.0 / centre_value]
    for step_index in range(1, count):
        damping_next = 1.0 / (2.0 * ratio_value - damping)
        first_list.append(damping_next * damping)
        second_list.append(2.0 * damping_next / half_width)
        damping = damping_next
    return (first_list, second_list)


def shifted(value, axis, steps):
    count = lax.axis_size(axis)
    return lax.ppermute(value, axis, [(i, (i + steps) % count) for i in range(count)])


def swapped(value):
    return lax.ppermute(value, "gy", [(i, i ^ 1) for i in range(lax.axis_size("gy"))])


def row_ghosts(rows):
    if lax.axis_size("gy") == 2:
        return swapped(rows)
    return jnp.concatenate([shifted(rows[:1], "gy", 1), shifted(rows[1:], "gy", -1)])


def f32(*shape):
    return jax.ShapeDtypeStruct(shape, jnp.float32)


def call(kernel, outs, *operands):
    specs = [pl.BlockSpec(memory_space=pltpu.VMEM) for _ in operands]
    specs[0] = pl.BlockSpec(memory_space=pltpu.SMEM)
    return pl.pallas_call(
        kernel,
        out_shape=outs,
        in_specs=specs,
        out_specs=[pl.BlockSpec(memory_space=pltpu.VMEM) for _ in outs],
        compiler_params=pltpu.CompilerParams(vmem_limit_bytes=VMEM_LIMIT),
    )(*operands)


def lane_of(shape):
    return lax.broadcasted_iota(jnp.int32, shape, 1)


def row_of(shape):
    return lax.broadcasted_iota(jnp.int32, shape, 0)


def units_of(ids, half):
    first = 3 * (lax.axis_index("gy") // 2)
    a, b = ids[0, 0, 0] - first, ids[1, 0, 0] - first
    found = []
    for k in range(3):
        unit = 3 * half + k
        slab = unit // 2
        found.append((jnp.logical_or(a == slab, b == slab), jnp.where(a == slab, 0, 1), unit % 2))
    return found


def field_unit(fields, item, place, z):
    rows = fields.shape[3] // 2
    _, slot, part = place
    return fields[item, slot, z, pl.ds(pl.multiple_of(part * rows, rows), rows), :]


def coef_unit(coef, item, place, z):
    rows = coef.shape[3] // 2
    _, slot, part = place
    both = coef[item, slot, z].astype(jnp.float32)
    return jnp.where(part == 0, both[:rows], both[rows:])


def strips(fields, coef, item, place, planes):
    columns, rows = fields.shape[4], fields.shape[3] // 2
    group = lane_of((rows, LANES)) // STRIP
    low = jnp.zeros((rows, LANES), jnp.float32)
    high = jnp.zeros((rows, LANES), jnp.float32)
    for z in range(planes):
        if item < 2:
            cells = field_unit(fields, item, place, z)
        else:
            cells = coef_unit(coef, 2 * item - 4, place, z) + SHIFT * coef_unit(coef, 2 * item - 3, place, z)
        first, last = cells[:, :LANES], cells[:, columns - LANES :]
        turn = STRIP * z
        low = jnp.where(group == z, pltpu.roll(first, turn, 1) if turn else first, low)
        turn = (STRIP * z + STRIP) % LANES
        high = jnp.where(group == z, pltpu.roll(last, turn, 1) if turn else last, high)
    return low, high


def pack_kernel(ids, fields, coef, strip_out, start_out, rhs_out, coef_out):
    planes = fields.shape[2]
    places = units_of(ids, 1 - lax.axis_index("gy") % 2)
    for k, place in enumerate(places):
        for item in range(4):
            low, high = strips(fields, coef, item, place, planes)
            strip_out[0, item, k] = low
            strip_out[1, item, k] = high
        for z in range(planes):
            start_out[k, z] = field_unit(fields, 0, place, z)
            rhs_out[k, z] = field_unit(fields, 1, place, z)
        for part in range(4):
            for z in range(0, planes, 2):
                both = [coef_unit(coef, part, place, z + j) for j in range(2)]
                coef_out[part, k, z // 2] = jnp.concatenate(both).astype(jnp.bfloat16)


def strip_kernel(ids, fields, coef, strip_in, left, right):
    planes = fields.shape[2]
    for k, place in enumerate(units_of(ids, lax.axis_index("gy") % 2)):
        for item in range(4):
            low, high = strips(fields, coef, item, place, planes)
            left[item, k] = jnp.where(place[0], low, strip_in[0, item, k])
            right[item, k] = jnp.where(place[0], high, strip_in[1, item, k])


def gather_kernel(
    ids, fields, coef, start_in, coef_in, from_left, from_right, start, rhs_ghost, wide, up, down, rows_out
):
    _, _, planes, rows, columns = fields.shape
    rows //= 2
    lane = lane_of((rows, LANES))
    for k, place in enumerate(units_of(ids, lax.axis_index("gy") % 2)):
        at = slice(k * rows, (k + 1) * rows)
        for item in range(4):
            low, high = from_left[item, k], from_right[item, k]
            for z in range(planes):
                turn = (LANES - STRIP * z) % LANES
                right = pltpu.roll(high, turn, 1) if turn else high
                turn = (LANES - STRIP - STRIP * z) % LANES
                left = pltpu.roll(low, turn, 1) if turn else low
                ghost = jnp.where(lane < LANES // 2, right, left)
                if item == 0:
                    start[z, at, :columns] = jnp.where(place[0], field_unit(fields, 0, place, z), start_in[k, z])
                    start[z, at, columns:] = ghost
                elif item == 1:
                    rhs_ghost[z, at] = ghost
                else:
                    b = jnp.floor(ghost * 0.125) * (8.0 / SHIFT)
                    a = ghost - SHIFT * b
                    for part, value in ((2 * item - 4, a), (2 * item - 3, b)):
                        got = coef_in[part, k, z // 2].astype(jnp.float32)
                        got = got[rows:] if z % 2 else got[:rows]
                        own = coef_unit(coef, part, place, z)
                        wide[part, z, at, :columns] = jnp.where(place[0], own, got)
                        wide[part, z, at, columns:] = value
    last = 3 * rows - 1
    up[...] = start[planes - 1]
    down[0] = start[0]
    down[1] = wide[3, 0]
    for z in range(planes):
        rows_out[0, z : z + 1] = start[z, last : last + 1]
        rows_out[1, z : z + 1] = start[z, 0:1]
        rows_out[2, z : z + 1] = wide[2, z, 0:1]


def apply_plane(value, low_row, high_row, lower_flux, upper_flux, alpha, beta_x, beta_y, rim_row):
    rows, width = value.shape
    flux_x = beta_x * (value - pltpu.roll(value, 1, 1))
    row = row_of(value.shape)
    before = jnp.where(row == 0, low_row, pltpu.roll(value, 1, 0))
    flux_y = beta_y * (value - before)
    top = rim_row * (high_row - value[rows - 1 : rows])
    after = jnp.where(row == rows - 1, top, pltpu.roll(flux_y, rows - 1, 0))
    return (
        alpha * value
        + (flux_x - pltpu.roll(flux_x, width - 1, 1))
        + (flux_y - after)
        + (lower_flux - upper_flux)
    )


def sweep_kernel(stage, first, second, ids, wide, field, low_face, high_face, low_high_rows, rim_face, rim_rows, *refs):
    if stage == 0:
        fields, rhs_in, rhs_ghost, residual, inverse, direction, total, up, down, rows_out = refs
        places = units_of(ids, lax.axis_index("gy") % 2)
    elif stage < SWEEPS:
        old, inverse, sum_in, residual, direction, total, up, down, rows_out = refs
    else:
        old, residual = refs
    planes, rows, width = field.shape
    columns = width - LANES
    value, beta_z = field[0], wide[3, 0]
    lower = beta_z * (value - low_face[...])
    for z in range(planes):
        at = slice(z, z + 1)
        if z + 1 < planes:
            following, next_z = field[z + 1], wide[3, z + 1]
        else:
            following, next_z = high_face[0], rim_face[1]
        upper = next_z * (following - value)
        alpha, beta_x, beta_y = wide[0, z], wide[1, z], wide[2, z]
        rim_row = rim_rows[2, at]
        image = apply_plane(
            value, low_high_rows[0, at], low_high_rows[1, at], lower, upper, alpha, beta_x, beta_y, rim_row
        )
        if stage == 0:
            parts = [
                jnp.where(place[0], field_unit(fields, 1, place, z), rhs_in[k, z]) for k, place in enumerate(places)
            ]
            rhs = jnp.concatenate([jnp.concatenate(parts), rhs_ghost[z]], axis=1)
            left = rhs - image
            next_y = jnp.where(row_of(value.shape) == rows - 1, rim_row, pltpu.roll(beta_y, rows - 1, 0))
            factor = 1.0 / (alpha + beta_x + pltpu.roll(beta_x, width - 1, 1) + beta_y + next_y + beta_z + next_z)
            inverse[z] = factor
            step = second * (factor * left)
            total[z] = value[:, :columns] + step[:, :columns]
        elif stage < SWEEPS:
            left = old[z] - image
            step = first * value + second * (inverse[z] * left)
            total[z] = sum_in[z] + step[:, :columns]
        else:
            residual[z] = (old[z] - image)[:, :columns]
        if stage < SWEEPS:
            residual[z] = left
            direction[z] = step
            rows_out[0, at] = step[rows - 1 : rows]
            rows_out[1, at] = step[0:1]
            if z == 0:
                down[0] = step
            if z == planes - 1:
                up[...] = step
        value, lower, beta_z = following, upper, next_z


def local(old_fields, old_coef, held_slabs):
    _, _, planes, rows, columns = old_fields.shape
    half = rows // 2
    rows = 3 * half
    width = columns + LANES
    full, own = f32(planes, rows, width), f32(planes, rows, columns)
    unit = f32(3, planes, half, columns)
    strip_out, start_out, rhs_out, coef_out = call(
        pack_kernel,
        [
            f32(2, 4, 3, half, LANES),
            unit,
            unit,
            jax.ShapeDtypeStruct((4, 3, planes // 2, 2 * half, columns), jnp.bfloat16),
        ],
        held_slabs,
        old_fields,
        old_coef,
    )
    strip_in = swapped(strip_out)
    start_in, coef_in, rhs_in = swapped(start_out), swapped(coef_out), swapped(rhs_out)
    strip = f32(4, 3, half, LANES)
    left, right = call(strip_kernel, [strip, strip], held_slabs, old_fields, old_coef, strip_in)
    from_left, from_right = shifted(right, "gx", 1), shifted(left, "gx", -1)
    field, rhs_ghost, wide, up, down, rows_out = call(
        gather_kernel,
        [
            full,
            f32(planes, rows, LANES),
            f32(4, planes, rows, width),
            f32(rows, width),
            f32(2, rows, width),
            f32(3, planes, width),
        ],
        held_slabs,
        old_fields,
        old_coef,
        start_in,
        coef_in,
        from_left,
        from_right,
    )
    first_list, second_list = chebyshev_weights(SWEEPS)
    faces = [f32(rows, width), f32(1, rows, width), f32(2, planes, width)]
    rim_face = rim_rows = None
    for stage in range(SWEEPS + 1):
        low_face, high_face, low_high_rows = shifted(up, "gz", 1), shifted(down, "gz", -1), row_ghosts(rows_out)
        if stage == 0:
            rim_face, rim_rows = high_face, low_high_rows
        common = (held_slabs, wide, field, low_face, high_face, low_high_rows, rim_face, rim_rows)
        if stage == 0:
            residual, inverse, field, total, up, down, rows_out = call(
                functools.partial(sweep_kernel, stage, first_list[stage], second_list[stage]),
                [full, full, full, own] + faces,
                *common,
                old_fields,
                rhs_in,
                rhs_ghost,
            )
        elif stage < SWEEPS:
            residual, field, total, up, down, rows_out = call(
                functools.partial(sweep_kernel, stage, first_list[stage], second_list[stage]),
                [full, full, own] + faces,
                *common,
                residual,
                inverse,
                total,
            )
        else:
            (residual,) = call(functools.partial(sweep_kernel, stage, 0.0, 0.0), [own], *common, residual)
    return total, residual


def solution(mesh):
    in_specs = (
        P(None, "gy", "gz", None, "gx"),
        P(None, "gy", "gz", None, "gx"),
        P("gy", "gz", "gx"),
    )
    out_specs = (P("gz", "gy", "gx"), P("gz", "gy", "gx"))
    return jax.shard_map(local, mesh=mesh, in_specs=in_specs, out_specs=out_specs, check_vma=False)
```

```python
import functools

import jax
import jax.numpy as jnp
from jax import lax
from jax.experimental import pallas as pl
from jax.experimental.pallas import tpu as pltpu
from jax.sharding import PartitionSpec as P

SWEEPS = 4
LANES = 128
STRIP = 8
SHIFT = 4096.0
VMEM_LIMIT = 24 * 1024 * 1024


def chebyshev_weights(count):
    low_bound = 0.25
    high_bound = 2.0
    centre_value = 0.5 * (high_bound + low_bound)
    half_width = 0.5 * (high_bound - low_bound)
    ratio_value = centre_value / half_width
    damping = 1.0 / ratio_value
    first_list = [0.0]
    second_list = [1.0 / centre_value]
    for step_index in range(1, count):
        damping_next = 1.0 / (2.0 * ratio_value - damping)
        first_list.append(damping_next * damping)
        second_list.append(2.0 * damping_next / half_width)
        damping = damping_next
    return (first_list, second_list)


def shifted(value, axis, steps):
    count = lax.axis_size(axis)
    return lax.ppermute(value, axis, [(i, (i + steps) % count) for i in range(count)])


def swapped(value):
    return lax.ppermute(value, "gy", [(i, i ^ 1) for i in range(lax.axis_size("gy"))])


def row_ghosts(rows):
    if lax.axis_size("gy") == 2:
        return swapped(rows)
    return jnp.concatenate([shifted(rows[:1], "gy", 1), shifted(rows[1:], "gy", -1)])


def f32(*shape):
    return jax.ShapeDtypeStruct(shape, jnp.float32)


def call(kernel, outs, *operands, ids=False):
    specs = [pl.BlockSpec(memory_space=pltpu.VMEM) for _ in operands]
    if ids:
        specs[0] = pl.BlockSpec(memory_space=pltpu.SMEM)
    return pl.pallas_call(
        kernel,
        out_shape=outs,
        in_specs=specs,
        out_specs=[pl.BlockSpec(memory_space=pltpu.VMEM) for _ in outs],
        compiler_params=pltpu.CompilerParams(vmem_limit_bytes=VMEM_LIMIT),
    )(*operands)


def lane_of(shape):
    return lax.broadcasted_iota(jnp.int32, shape, 1)


def row_of(shape):
    return lax.broadcasted_iota(jnp.int32, shape, 0)


def units_of(ids, half):
    first = 3 * (lax.axis_index("gy") // 2)
    a, b = ids[0] - first, ids[1] - first
    found = []
    for k in range(3):
        unit = 3 * half + k
        slab = unit // 2
        found.append((jnp.logical_or(a == slab, b == slab), jnp.where(a == slab, 0, 1), unit % 2))
    return found


def field_unit(fields, item, place, z):
    rows = fields.shape[3] // 2
    _, slot, part = place
    return fields[item, slot, z, pl.ds(pl.multiple_of(part * rows, rows), rows), :]


def coef_unit(coef, item, place, z):
    rows = coef.shape[3] // 2
    _, slot, part = place
    both = coef[item, slot, z].astype(jnp.float32)
    return jnp.where(part == 0, both[:rows], both[rows:])


def strips(fields, coef, item, place, planes):
    columns, rows = fields.shape[4], fields.shape[3] // 2
    group = lane_of((rows, LANES)) // STRIP
    low = jnp.zeros((rows, LANES), jnp.float32)
    high = jnp.zeros((rows, LANES), jnp.float32)
    for z in range(planes):
        if item < 2:
            cells = field_unit(fields, item, place, z)
        else:
            cells = coef_unit(coef, 2 * item - 4, place, z) + SHIFT * coef_unit(coef, 2 * item - 3, place, z)
        first, last = cells[:, :LANES], cells[:, columns - LANES :]
        turn = STRIP * z
        low = jnp.where(group == z, pltpu.roll(first, turn, 1) if turn else first, low)
        turn = (STRIP * z + STRIP) % LANES
        high = jnp.where(group == z, pltpu.roll(last, turn, 1) if turn else last, high)
    return low, high


def take_kernel(ids, fields, start_out, sems):
    rows = fields.shape[3] // 2
    copies = []
    for k, (_, slot, part) in enumerate(units_of(ids, 1 - lax.axis_index("gy") % 2)):
        source = fields.at[0, slot, :, pl.ds(pl.multiple_of(part * rows, rows), rows), :]
        copies.append(pltpu.make_async_copy(source, start_out.at[k], sems.at[k]))
    for copy in copies:
        copy.start()
    for copy in copies:
        copy.wait()


def edge_kernel(ids, fields, coef, strip_out):
    planes = fields.shape[2]
    for k, place in enumerate(units_of(ids, 1 - lax.axis_index("gy") % 2)):
        for item in range(4):
            low, high = strips(fields, coef, item, place, planes)
            strip_out[0, item, k] = low
            strip_out[1, item, k] = high


def coef_kernel(first, ids, coef, _, out):
    planes = coef.shape[2]
    for k, place in enumerate(units_of(ids, 1 - lax.axis_index("gy") % 2)):
        for part in range(2):
            for z in range(0, planes, 2):
                both = [coef_unit(coef, first + part, place, z + j) for j in range(2)]
                out[part, k, z // 2] = jnp.concatenate(both).astype(jnp.bfloat16)


def rhs_kernel(ids, fields, _, out):
    for k, place in enumerate(units_of(ids, 1 - lax.axis_index("gy") % 2)):
        for z in range(fields.shape[2]):
            out[k, z] = field_unit(fields, 1, place, z)


def strip_kernel(ids, fields, coef, strip_in, left, right):
    planes = fields.shape[2]
    for k, place in enumerate(units_of(ids, lax.axis_index("gy") % 2)):
        for item in range(4):
            low, high = strips(fields, coef, item, place, planes)
            left[item, k] = jnp.where(place[0], low, strip_in[0, item, k])
            right[item, k] = jnp.where(place[0], high, strip_in[1, item, k])


def ghost_columns(from_left, from_right, item, k, z):
    low, high = from_left[item, k], from_right[item, k]
    turn = (LANES - STRIP * z) % LANES
    right = pltpu.roll(high, turn, 1) if turn else high
    turn = (LANES - STRIP - STRIP * z) % LANES
    left = pltpu.roll(low, turn, 1) if turn else low
    return jnp.where(lane_of(low.shape) < LANES // 2, right, left)


def coef_gather(coef, coef_in, item, place, k, z):
    rows = coef.shape[3] // 2
    got = coef_in[item % 2, k, z // 2].astype(jnp.float32)
    got = got[rows:] if z % 2 else got[:rows]
    return jnp.where(place[0], coef_unit(coef, item, place, z), got)


def gather_kernel(
    ids, fields, coef, start_in, coef_in, from_left, from_right, start, rhs_ghost, wide, ghosts, up, down, rows_out
):
    _, _, planes, rows, columns = fields.shape
    rows //= 2
    for k, place in enumerate(units_of(ids, lax.axis_index("gy") % 2)):
        at = slice(k * rows, (k + 1) * rows)
        for z in range(planes):
            start[z, at, :columns] = jnp.where(place[0], field_unit(fields, 0, place, z), start_in[k, z])
            start[z, at, columns:] = ghost_columns(from_left, from_right, 0, k, z)
            rhs_ghost[z, at] = ghost_columns(from_left, from_right, 1, k, z)
            for item in (2, 3):
                both = ghost_columns(from_left, from_right, item, k, z)
                b = jnp.floor(both * 0.125) * (8.0 / SHIFT)
                a = both - SHIFT * b
                if item == 2:
                    ghosts[0, z, at], ghosts[1, z, at] = a, b
                else:
                    wide[0, z, at, columns:], wide[1, z, at, columns:] = a, b
            for part in (0, 1):
                wide[part, z, at, :columns] = coef_gather(coef, coef_in, part + 2, place, k, z)
    last = 3 * rows - 1
    up[...] = start[planes - 1]
    down[0] = start[0]
    down[1] = wide[1, 0]
    for z in range(planes):
        rows_out[0, z : z + 1] = start[z, last : last + 1]
        rows_out[1, z : z + 1] = start[z, 0:1]
        rows_out[2, z : z + 1] = wide[0, z, 0:1]


def spread_kernel(ids, coef, coef_in, ghosts, wide):
    planes, columns, rows = coef.shape[2], coef.shape[4], coef.shape[3] // 2
    for part in (0, 1):
        wide[part, :, :, columns:] = ghosts[part]
        for k, place in enumerate(units_of(ids, lax.axis_index("gy") % 2)):
            at = slice(k * rows, (k + 1) * rows)
            for z in range(planes):
                wide[part, z, at, :columns] = coef_gather(coef, coef_in, part, place, k, z)


def image_plane(value, low_row, high_row, lower_flux, upper_flux, alpha, beta_x, beta_y, rim_row):
    rows, width = value.shape
    flux_x = beta_x * (value - pltpu.roll(value, 1, 1))
    row = row_of(value.shape)
    before = jnp.where(row == 0, 0.0 if low_row is None else low_row, pltpu.roll(value, 1, 0))
    flux_y = beta_y * (value - before)
    last = value[rows - 1 : rows]
    top = rim_row * (-last if high_row is None else high_row - last)
    after = jnp.where(row == rows - 1, top, pltpu.roll(flux_y, rows - 1, 0))
    return (
        alpha * value
        + (flux_x - pltpu.roll(flux_x, width - 1, 1))
        + (flux_y - after)
        + (lower_flux - upper_flux)
    )


def images(plane, wide_ax, wide_yz, rim_face, rim_rows, low_face=None, high_face=None, ghost_rows=None):
    planes = wide_ax.shape[1]
    (value, *others), beta_z = plane(0), wide_yz[1, 0]
    lower = beta_z * (value if low_face is None else value - low_face[...])
    for z in range(planes):
        at = slice(z, z + 1)
        if z + 1 < planes:
            (following, *next_others), next_z = plane(z + 1), wide_yz[1, z + 1]
            upper = next_z * (following - value)
        else:
            following, next_others, next_z = None, None, rim_face[1]
            upper = next_z * (-value if high_face is None else high_face[0] - value)
        low_row, high_row = (None, None) if ghost_rows is None else (ghost_rows[0, at], ghost_rows[1, at])
        image = image_plane(
            value, low_row, high_row, lower, upper, wide_ax[0, z], wide_ax[1, z], wide_yz[0, z], rim_rows[2, at]
        )
        yield z, (value, *others), image, beta_z, next_z
        value, others, lower, beta_z = following, next_others, upper, next_z


def first_kernel(
    wide_ax, wide_yz, field, low_face, high_face, ghost_rows, image_out, inverse
):
    _, rows, width = field.shape
    for z, (value,), image, beta_z, next_z in images(
        lambda z: (field[z],), wide_ax, wide_yz, high_face, ghost_rows, low_face, high_face, ghost_rows
    ):
        image_out[z] = image
        beta_x, beta_y = wide_ax[1, z], wide_yz[0, z]
        rim_row = ghost_rows[2, z : z + 1]
        next_y = jnp.where(row_of(value.shape) == rows - 1, rim_row, pltpu.roll(beta_y, rows - 1, 0))
        next_x = pltpu.roll(beta_x, width - 1, 1)
        inverse[z] = 1.0 / (wide_ax[0, z] + beta_x + next_x + beta_y + next_y + beta_z + next_z)


def store_faces(direction, up, down, rows_out):
    planes, rows, _ = direction.shape
    up[...] = direction[planes - 1]
    down[0] = direction[0]
    for z in range(planes):
        rows_out[0, z : z + 1] = direction[z, rows - 1 : rows]
        rows_out[1, z : z + 1] = direction[z, 0:1]


def start_kernel(
    second, ids, fields, rhs_in, rhs_ghost, image, inverse, start, residual, direction, total, up, down, rows_out
):
    planes, _, _ = start.shape
    columns = fields.shape[4]
    places = units_of(ids, lax.axis_index("gy") % 2)
    for z in range(planes):
        parts = [jnp.where(place[0], field_unit(fields, 1, place, z), rhs_in[k, z]) for k, place in enumerate(places)]
        left = jnp.concatenate([jnp.concatenate(parts), rhs_ghost[z]], axis=1) - image[z]
        step = second * (inverse[z] * left)
        residual[z] = left
        direction[z] = step
        total[z] = start[z, :, :columns] + step[:, :columns]
    store_faces(direction, up, down, rows_out)


def halo_flux(z, wide_yz, rim_face, rim_rows, low_face, high_face, ghost_rows):
    _, planes, rows, width = wide_yz.shape
    at, row = slice(z, z + 1), row_of((rows, width))
    top = jnp.where(row == rows - 1, rim_rows[2, at] * ghost_rows[1, at], 0.0)
    flux = jnp.where(row == 0, wide_yz[0, z, 0:1] * ghost_rows[0, at], top)
    if z == 0:
        flux = flux + wide_yz[1, 0] * low_face[...]
    if z == planes - 1:
        flux = flux + rim_face[1] * high_face[0]
    return flux


def inner_kernel(weights, wide_ax, wide_yz, rim_face, rim_rows, field, old, inverse, sum_in, *refs):
    before, first, second = weights
    rims = rim_face, rim_rows
    halo = refs[:3] if before else None
    if second:
        residual, direction, total = refs[-3:]
    else:
        residual, total = refs[-2:]
    columns = total.shape[2]

    def plane(z):
        if not before:
            return field[z], old[z], sum_in[z]
        flux = halo_flux(z, wide_yz, *rims, *halo)
        step = before * (inverse[z] * flux)
        return field[z] + step, old[z] + flux, sum_in[z] + step[:, :columns]

    for z, (value, left, done), image, _, _ in images(plane, wide_ax, wide_yz, *rims):
        left = left - image
        if second:
            step = first * value + second * (inverse[z] * left)
            residual[z] = left
            direction[z] = step
            total[z] = done + step[:, :columns]
        else:
            residual[z] = left[:, :columns]
            total[z] = done


def faces_kernel(second, wide_yz, rim_face, rim_rows, low_face, high_face, ghost_rows, inverse, direction, up, down, rows_out):
    halo = wide_yz, rim_face, rim_rows, low_face, high_face, ghost_rows
    planes, rows, _ = direction.shape
    for z, out in ((0, down.at[0]), (planes - 1, up)):
        out[...] = direction[z] + second * (inverse[z] * halo_flux(z, *halo))
    for z in range(planes):
        at = slice(z, z + 1)
        for edge, row, out in ((0, 0, 1), (1, rows - 1, 0)):
            line = slice(row, row + 1)
            if z == 0:
                rows_out[out, at] = down[0, line]
            elif z == planes - 1:
                rows_out[out, at] = up[line]
            else:
                beta = rim_rows[2, at] if edge else wide_yz[0, z, line]
                flux = beta * ghost_rows[edge, at]
                rows_out[out, at] = direction[z, line] + second * (inverse[z, line] * flux)


def last_kernel(wide_yz, rim_face, rim_rows, low_face, high_face, ghost_rows, partial, residual):
    planes, _, columns = residual.shape
    for z in range(planes):
        flux = halo_flux(z, wide_yz, rim_face, rim_rows, low_face, high_face, ghost_rows)
        residual[z] = partial[z] + flux[:, :columns]


def local(old_fields, old_coef, held_slabs):
    _, _, planes, rows, columns = old_fields.shape
    half = rows // 2
    rows = 3 * half
    width = columns + LANES
    full, own = f32(planes, rows, width), f32(planes, rows, columns)
    unit = f32(3, planes, half, columns)
    ids = held_slabs.reshape(2)
    start_out = pl.pallas_call(
        take_kernel,
        out_shape=unit,
        in_specs=[pl.BlockSpec(memory_space=pltpu.SMEM), pl.BlockSpec(memory_space=pl.ANY)],
        out_specs=pl.BlockSpec(memory_space=pltpu.VMEM),
        scratch_shapes=[pltpu.SemaphoreType.DMA((3,))],
    )(ids, old_fields)
    start_in = swapped(start_out)
    coef_units = jax.ShapeDtypeStruct((2, 3, planes // 2, 2 * half, columns), jnp.bfloat16)
    (strip_out,) = call(edge_kernel, [f32(2, 4, 3, half, LANES)], ids, old_fields, old_coef, ids=True)
    strip_in = swapped(strip_out)
    (coef_yz,) = call(functools.partial(coef_kernel, 2), [coef_units], ids, old_coef, strip_out, ids=True)
    yz_in = swapped(coef_yz)
    (coef_ax,) = call(functools.partial(coef_kernel, 0), [coef_units], ids, old_coef, coef_yz, ids=True)
    ax_in = swapped(coef_ax)
    strip = f32(4, 3, half, LANES)
    left, right = call(strip_kernel, [strip, strip], ids, old_fields, old_coef, strip_in, ids=True)
    from_left, from_right = shifted(right, "gx", 1), shifted(left, "gx", -1)
    coef_full = f32(2, planes, rows, width)
    field, rhs_ghost, wide_yz, ghosts, up, down, rows_out = call(
        gather_kernel,
        [
            full,
            f32(planes, rows, LANES),
            coef_full,
            f32(2, planes, rows, LANES),
            f32(rows, width),
            f32(2, rows, width),
            f32(3, planes, width),
        ],
        ids,
        old_fields,
        old_coef,
        start_in,
        yz_in,
        from_left,
        from_right,
        ids=True,
    )
    low_face, rim_face, rim_rows = shifted(up, "gz", 1), shifted(down, "gz", -1), row_ghosts(rows_out)
    (rhs_out,) = call(rhs_kernel, [unit], ids, old_fields, rows_out, ids=True)
    rhs_in = swapped(rhs_out)
    (wide_ax,) = call(spread_kernel, [coef_full], ids, old_coef, ax_in, ghosts, ids=True)
    image, inverse = call(first_kernel, [full, full], wide_ax, wide_yz, field, low_face, rim_face, rim_rows)
    first_list, second_list = chebyshev_weights(SWEEPS)
    faces = [f32(rows, width), f32(1, rows, width), f32(2, planes, width)]
    residual, direction, total, up, down, rows_out = call(
        functools.partial(start_kernel, second_list[0]),
        [full, full, own] + faces,
        ids,
        old_fields,
        rhs_in,
        rhs_ghost,
        image,
        inverse,
        field,
        ids=True,
    )
    rims, halo = (rim_face, rim_rows), ()
    for stage in range(1, SWEEPS + 1):
        before = second_list[stage - 1] if halo else 0.0
        last = stage == SWEEPS
        weights = (before, 0.0, 0.0) if last else (before, first_list[stage], second_list[stage])
        arrived = halo
        halo = shifted(up, "gz", 1), shifted(down, "gz", -1), row_ghosts(rows_out)
        state = call(
            functools.partial(inner_kernel, weights),
            [own, own] if last else [full, full, own],
            wide_ax,
            wide_yz,
            *rims,
            direction,
            residual,
            inverse,
            total,
            *arrived,
        )
        if last:
            residual, total = state
            (residual,) = call(last_kernel, [own], wide_yz, *rims, *halo, residual)
        else:
            residual, direction, total = state
            up, down, rows_out = call(
                functools.partial(faces_kernel, second_list[stage]), faces, wide_yz, *rims, *halo, inverse, direction
            )
    return total, residual


def solution(mesh):
    in_specs = (
        P(None, "gy", "gz", None, "gx"),
        P(None, "gy", "gz", None, "gx"),
        P("gy", "gz", "gx"),
    )
    out_specs = (P("gz", "gy", "gx"), P("gz", "gy", "gx"))
    return jax.shard_map(local, mesh=mesh, in_specs=in_specs, out_specs=out_specs, check_vma=False)
```

```python
import functools

import jax
import jax.numpy as jnp
from jax import lax
from jax.experimental import pallas as pl
from jax.experimental.pallas import tpu as pltpu
from jax.sharding import PartitionSpec as P

SWEEPS = 4
LANES = 128
STRIP = 8
SHIFT = 4096.0
VMEM_LIMIT = 24 * 1024 * 1024


def chebyshev_weights(count):
    low_bound = 0.25
    high_bound = 2.0
    centre_value = 0.5 * (high_bound + low_bound)
    half_width = 0.5 * (high_bound - low_bound)
    ratio_value = centre_value / half_width
    damping = 1.0 / ratio_value
    first_list = [0.0]
    second_list = [1.0 / centre_value]
    for step_index in range(1, count):
        damping_next = 1.0 / (2.0 * ratio_value - damping)
        first_list.append(damping_next * damping)
        second_list.append(2.0 * damping_next / half_width)
        damping = damping_next
    return (first_list, second_list)


def shifted(value, axis, steps):
    count = lax.axis_size(axis)
    return lax.ppermute(value, axis, [(i, (i + steps) % count) for i in range(count)])


def swapped(value):
    return lax.ppermute(value, "gy", [(i, i ^ 1) for i in range(lax.axis_size("gy"))])


def row_ghosts(rows):
    if lax.axis_size("gy") == 2:
        return swapped(rows)
    return jnp.concatenate([shifted(rows[:1], "gy", 1), shifted(rows[1:], "gy", -1)])


def f32(*shape):
    return jax.ShapeDtypeStruct(shape, jnp.float32)


def call(kernel, outs, *operands, ids=False):
    specs = [pl.BlockSpec(memory_space=pltpu.VMEM) for _ in operands]
    if ids:
        specs[0] = pl.BlockSpec(memory_space=pltpu.SMEM)
    return pl.pallas_call(
        kernel,
        out_shape=outs,
        in_specs=specs,
        out_specs=[pl.BlockSpec(memory_space=pltpu.VMEM) for _ in outs],
        compiler_params=pltpu.CompilerParams(vmem_limit_bytes=VMEM_LIMIT),
    )(*operands)


def lane_of(shape):
    return lax.broadcasted_iota(jnp.int32, shape, 1)


def row_of(shape):
    return lax.broadcasted_iota(jnp.int32, shape, 0)


def units_of(ids, half):
    first = 3 * (lax.axis_index("gy") // 2)
    a, b = ids[0] - first, ids[1] - first
    found = []
    for k in range(3):
        unit = 3 * half + k
        slab = unit // 2
        found.append((jnp.logical_or(a == slab, b == slab), jnp.where(a == slab, 0, 1), unit % 2))
    return found


def field_unit(fields, item, place, z):
    rows = fields.shape[3] // 2
    _, slot, part = place
    return fields[item, slot, z, pl.ds(pl.multiple_of(part * rows, rows), rows), :]


def coef_unit(coef, item, place, z):
    rows = coef.shape[3] // 2
    _, slot, part = place
    both = coef[item, slot, z].astype(jnp.float32)
    return jnp.where(part == 0, both[:rows], both[rows:])


def strips(fields, coef, item, place, planes):
    columns, rows = fields.shape[4], fields.shape[3] // 2
    group = lane_of((rows, LANES)) // STRIP
    low = jnp.zeros((rows, LANES), jnp.float32)
    high = jnp.zeros((rows, LANES), jnp.float32)
    for z in range(planes):
        if item < 2:
            cells = field_unit(fields, item, place, z)
        else:
            cells = coef_unit(coef, 2 * item - 4, place, z) + SHIFT * coef_unit(coef, 2 * item - 3, place, z)
        first, last = cells[:, :LANES], cells[:, columns - LANES :]
        turn = STRIP * z
        low = jnp.where(group == z, pltpu.roll(first, turn, 1) if turn else first, low)
        turn = (STRIP * z + STRIP) % LANES
        high = jnp.where(group == z, pltpu.roll(last, turn, 1) if turn else last, high)
    return low, high


def brick_rows(ids, half, unit_rows):
    first = 3 * (lax.axis_index("gy") // 2)
    a, b = ids[0] - first, ids[1] - first
    found = []
    for j in range(3):
        slab = jnp.where(half == 0, j // 2, 1 + (j + 1) // 2)
        row = jnp.where((j + half) % 2 == 0, 0, 2 * unit_rows - 1)
        found.append((jnp.logical_or(a == slab, b == slab), jnp.where(a == slab, 0, 1), row))
    return found


def field_row(fields, place, z):
    last = fields.shape[3] - 1
    _, slot, row = place
    return jnp.where(row == 0, fields[0, slot, z, 0:1], fields[0, slot, z, last : last + 1])


PLANES_AT, ROWS_AT = 12, 18


def edge_kernel(ids, fields_in, coef_in, fields, coef, out, sems):
    copies = []
    for item in range(2):
        for slot in range(2):
            at = len(copies)
            copies.append(pltpu.make_async_copy(fields_in.at[item, slot], fields.at[item, slot], sems.at[at]))
    for part in range(4):
        at = len(copies)
        copies.append(pltpu.make_async_copy(coef_in.at[part], coef.at[part], sems.at[at]))
    for copy in copies:
        copy.start()
    for copy in copies:
        copy.wait()
    planes, unit_rows = fields.shape[2], fields.shape[3] // 2
    half = 1 - lax.axis_index("gy") % 2
    for k, place in enumerate(units_of(ids, half)):
        for item in range(4):
            low, high = strips(fields, coef, item, place, planes)
            out[3 * item + k] = jnp.concatenate([low, high], axis=1)
        for e, z in enumerate((0, planes - 1)):
            out[PLANES_AT + 3 * e + k] = field_unit(fields, 0, place, z)
    for j, place in enumerate(brick_rows(ids, half, unit_rows)):
        for z in range(planes):
            at = ROWS_AT + j * (planes // unit_rows) + z // unit_rows
            line = z % unit_rows
            out[at, line : line + 1] = field_row(fields, place, z)
    at = ROWS_AT + 3 * (planes // unit_rows)
    for k, place in enumerate(units_of(ids, half)):
        for z in range(planes):
            out[at + k * planes + z] = coef_unit(coef, 2, place, z) + SHIFT * coef_unit(coef, 3, place, z)


def coef_kernel(first, ids, coef, _, out):
    planes = coef.shape[2]
    for k, place in enumerate(units_of(ids, 1 - lax.axis_index("gy") % 2)):
        for part in range(2):
            for z in range(0, planes, 2):
                both = [coef_unit(coef, first + part, place, z + j) for j in range(2)]
                out[part, k, z // 2] = jnp.concatenate(both).astype(jnp.bfloat16)


def partial_kernel(ids, fields, coef, _, out, own, start_own, *refs):
    start_out, partial = refs[:3], refs[3]
    _, slots, planes, rows, columns = fields.shape
    lane, row = lane_of((rows, columns)), row_of((rows, columns))
    for slot in range(slots):
        value, lower = fields[0, slot, 0], 0.0
        for z in range(planes):
            alpha, beta_x, beta_y = (coef[part, slot, z].astype(jnp.float32) for part in range(3))
            flux_x = jnp.where(lane == 0, 0.0, beta_x * (value - pltpu.roll(value, 1, 1)))
            flux_y = jnp.where(row == 0, 0.0, beta_y * (value - pltpu.roll(value, 1, 0)))
            image = (
                alpha * value
                + (flux_x - pltpu.roll(flux_x, columns - 1, 1))
                + (flux_y - pltpu.roll(flux_y, rows - 1, 0))
                + lower
            )
            if z + 1 < planes:
                following = fields[0, slot, z + 1]
                lower = coef[3, slot, z + 1].astype(jnp.float32) * (following - value)
                image = image - lower
                value = following
            partial[slot, z] = fields[1, slot, z] - image
    half_rows = rows // 2
    half = lax.axis_index("gy") % 2
    for theirs, side in ((True, 1 - half), (False, half)):
        for k, place in enumerate(units_of(ids, side)):
            held, slot, part = place
            at = pl.ds(pl.multiple_of(part * half_rows, half_rows), half_rows)
            line = slice(k * half_rows, (k + 1) * half_rows)
            for z in range(planes):
                left = jnp.where(held, partial[slot, z, at, :], 0.0)
                start = jnp.where(held, field_unit(fields, 0, place, z), 0.0)
                if theirs:
                    out[k, z], start_out[k][z] = left, start
                else:
                    own[z, line], start_own[z, line] = left, start


def strip_kernel(ids, fields, coef, edge_in, left, right):
    planes = fields.shape[2]
    for k, place in enumerate(units_of(ids, lax.axis_index("gy") % 2)):
        for item in range(4):
            low, high = strips(fields, coef, item, place, planes)
            got = edge_in[3 * item + k]
            left[item, k] = jnp.where(place[0], low, got[:, :LANES])
            right[item, k] = jnp.where(place[0], high, got[:, LANES:])


def parted(both):
    second = jnp.floor(both * 0.125) * (8.0 / SHIFT)
    return both - SHIFT * second, second


def ghost_columns(from_left, from_right, item, k, z):
    low, high = from_left[item, k], from_right[item, k]
    turn = (LANES - STRIP * z) % LANES
    right = pltpu.roll(high, turn, 1) if turn else high
    turn = (LANES - STRIP - STRIP * z) % LANES
    left = pltpu.roll(low, turn, 1) if turn else low
    return jnp.where(lane_of(low.shape) < LANES // 2, right, left)


def coef_gather(coef, coef_in, item, place, k, z):
    rows = coef.shape[3] // 2
    got = coef_in[item % 2, k, z // 2].astype(jnp.float32)
    got = got[rows:] if z % 2 else got[:rows]
    return jnp.where(place[0], coef_unit(coef, item, place, z), got)


def gather_kernel(
    ids, fields, coef, edge_in, left, right, from_left, from_right,
    edge_start, rhs_ghost, wide, ghosts, own_rows, up, down, rows_out,
):
    _, _, planes, rows, columns = fields.shape
    rows //= 2
    half = lax.axis_index("gy") % 2
    for k, place in enumerate(units_of(ids, half)):
        at = slice(k * rows, (k + 1) * rows)
        for z in range(planes):
            edge_start[z, at, :LANES] = ghost_columns(right, left, 0, k, z)
            edge_start[z, at, LANES:] = ghost_columns(from_left, from_right, 0, k, z)
            rhs_ghost[z, at] = ghost_columns(from_left, from_right, 1, k, z)
            for item in (2, 3):
                both = ghost_columns(from_left, from_right, item, k, z)
                a, b = parted(both)
                if item == 2:
                    ghosts[0, z, at], ghosts[1, z, at] = a, b
                else:
                    wide[0, z, at, columns:], wide[1, z, at, columns:] = a, b
            got = parted(edge_in[ROWS_AT + 3 * (planes // rows) + k * planes + z])
            for part in (0, 1):
                wide[part, z, at, :columns] = jnp.where(place[0], coef_unit(coef, part + 2, place, z), got[part])
        for e, (z, out) in enumerate(((0, down.at[0]), (planes - 1, up))):
            own = field_unit(fields, 0, place, z)
            out[at, :columns] = jnp.where(place[0], own, edge_in[PLANES_AT + 3 * e + k])
            out[at, columns:] = edge_start[z, at, LANES:]
    down[1] = wide[1, 0]
    for j, place in enumerate(brick_rows(ids, half, rows)):
        for z in range(planes):
            at = ROWS_AT + j * (planes // rows) + z // rows
            line = z % rows
            own_rows[j, z : z + 1] = jnp.where(place[0], field_row(fields, place, z), edge_in[at, line : line + 1])
    last = 3 * rows - 1
    for z in range(planes):
        line = slice(z, z + 1)
        for out, row, j, known in ((0, last, 2, half == 1), (1, 0, 0, half == 0)):
            edge = edge_start[z, row : row + 1]
            middle = jnp.concatenate([edge[:, :LANES]] * (columns // LANES), axis=1)
            rows_out[out, line, :columns] = jnp.where(known, own_rows[j, line], middle)
            rows_out[out, line, columns:] = edge[:, LANES:]
        rows_out[2, line] = wide[0, z, 0:1]


def spread_kernel(ids, coef, coef_in, ghosts, wide):
    planes, columns, rows = coef.shape[2], coef.shape[4], coef.shape[3] // 2
    for part in (0, 1):
        wide[part, :, :, columns:] = ghosts[part]
        for k, place in enumerate(units_of(ids, lax.axis_index("gy") % 2)):
            at = slice(k * rows, (k + 1) * rows)
            for z in range(planes):
                wide[part, z, at, :columns] = coef_gather(coef, coef_in, part, place, k, z)


def image_plane(value, low_row, high_row, lower_flux, upper_flux, alpha, beta_x, beta_y, rim_row):
    rows, width = value.shape
    flux_x = beta_x * (value - pltpu.roll(value, 1, 1))
    row = row_of(value.shape)
    before = jnp.where(row == 0, 0.0 if low_row is None else low_row, pltpu.roll(value, 1, 0))
    flux_y = beta_y * (value - before)
    top = 0.0
    if rim_row is not None:
        last = value[rows - 1 : rows]
        top = rim_row * (-last if high_row is None else high_row - last)
    after = jnp.where(row == rows - 1, top, pltpu.roll(flux_y, rows - 1, 0))
    return (
        alpha * value
        + (flux_x - pltpu.roll(flux_x, width - 1, 1))
        + (flux_y - after)
        + (lower_flux - upper_flux)
    )


def images(plane, coef, planes, rim_face, rim_row, low_face=None, high_face=None, ghost_row=None):
    (value, *others), beta_z = plane(0), coef(3, 0)
    lower = beta_z * (value if low_face is None else value - low_face)
    for z in range(planes):
        if z + 1 < planes:
            (following, *next_others), next_z = plane(z + 1), coef(3, z + 1)
            upper = next_z * (following - value)
        else:
            following, next_others, next_z = None, None, rim_face
            upper = next_z * (-value if high_face is None else high_face - value)
        low_row, high_row = (None, None) if ghost_row is None else (ghost_row(0, z), ghost_row(1, z))
        image = image_plane(value, low_row, high_row, lower, upper, coef(0, z), coef(1, z), coef(2, z), rim_row(z))
        yield z, (value, *others), image
        value, others, lower, beta_z = following, next_others, upper, next_z


def edges(value):
    columns = value.shape[1] - LANES
    own = jnp.where(lane_of((value.shape[0], LANES)) < LANES // 2, value[:, :LANES], value[:, columns - LANES : columns])
    return jnp.concatenate([own, value[:, columns:]], axis=1)


def first_kernel(
    wide_ax, wide_yz, edge_start, rhs_ghost, own_rows, up, down, partial, low_face, high_face, extra, inverse
):
    planes, rows, width = extra.shape
    columns = width - LANES
    unit_rows = rows // 3
    even = lax.axis_index("gy") % 2 == 0

    def coef(part, z):
        return wide_ax[part, z] if part < 2 else wide_yz[part - 2, z]

    def ring(part, z):
        return edges(coef(part, z))

    lane, row = lane_of((rows, columns)), row_of((rows, columns))
    inner = jnp.where(even, 2 * unit_rows, unit_rows)
    for z, (value,), image in images(
        lambda z: (edge_start[z],),
        ring,
        planes,
        edges(high_face[1]),
        lambda z: None,
        edges(low_face[...]),
        edges(high_face[0]),
    ):
        flux = ring(1, z) * (value - pltpu.roll(value, 1, 1))
        gain = jnp.where(lane == 0, -flux[:, :columns], 0.0)
        far = jnp.where(lane == columns - 1, pltpu.roll(flux, LANES - 1, 1)[:, :columns], 0.0)
        gain = gain + far
        if z == 0:
            gain = gain - (wide_yz[1, 0] * (down[0] - low_face[...]))[:, :columns]
        if z == planes - 1:
            gain = gain + (high_face[1] * (high_face[0] - up[...]))[:, :columns]
        beta_y = wide_yz[0, z]
        at = slice(z, z + 1)
        between = jnp.where(even, own_rows[2, at] - own_rows[1, at], own_rows[1, at] - own_rows[0, at])
        beta = jnp.where(even, beta_y[2 * unit_rows : 2 * unit_rows + 1], beta_y[unit_rows : unit_rows + 1])
        between = beta[:, :columns] * between
        gain = gain + jnp.where(row == inner, -between, jnp.where(row == inner - 1, between, 0.0))
        low = jnp.where(even, beta_y[0:1, :columns] * own_rows[0, at], 0.0)
        gain = gain - jnp.where(row == 0, low, 0.0)
        extra[z, :, :columns] = gain + partial[z]
        extra[z, :, columns:] = rhs_ghost[z] - image[:, LANES:]
        beta_x, beta_z = wide_ax[1, z], wide_yz[1, z]
        next_z = wide_yz[1, z + 1] if z + 1 < planes else high_face[1]
        next_y = jnp.where(row_of((rows, width)) == rows - 1, 0.0, pltpu.roll(beta_y, rows - 1, 0))
        next_x = pltpu.roll(beta_x, width - 1, 1)
        inverse[z] = 1.0 / (wide_ax[0, z] + beta_x + next_x + beta_y + next_y + beta_z + next_z)


def store_faces(direction, up, down, rows_out):
    planes, rows, _ = direction.shape
    up[...] = direction[planes - 1]
    down[0] = direction[0]
    for z in range(planes):
        rows_out[0, z : z + 1] = direction[z, rows - 1 : rows]
        rows_out[1, z : z + 1] = direction[z, 0:1]


def start_kernel(
    second, partial_in, extra, part_inverse, start, wide_yz, own_last, ghost_rows,
    inverse, residual, direction, total, up, down, rows_out,
):
    planes, rows, width = extra.shape
    columns = total.shape[2]
    even = lax.axis_index("gy") % 2 == 0
    row = row_of((rows, width))
    ghost = lane_of((1, width)) >= columns
    for z in range(planes):
        at = slice(z, z + 1)
        known = jnp.concatenate([partial_in[k, z] for k in range(3)])
        left = extra[z] + jnp.concatenate([known, jnp.zeros((rows, width - columns), jnp.float32)], axis=1)
        rim = ghost_rows[2, at]
        low = jnp.where(jnp.logical_or(ghost, even), wide_yz[0, z, 0:1] * ghost_rows[0, at], 0.0)
        high = rim * (ghost_rows[1, at] - own_last[0, at])
        high = jnp.where(jnp.logical_and(jnp.logical_not(ghost), even), 0.0, high)
        left = left + jnp.where(row == 0, low, jnp.where(row == rows - 1, high, 0.0))
        factor = part_inverse[z]
        last = factor[rows - 1 : rows]
        factor = jnp.where(row == rows - 1, last / (1.0 + rim * last), factor)
        step = second * (factor * left)
        inverse[z] = factor
        residual[z] = left
        direction[z] = step
        total[z] = start[z] + step[:, :columns]
    store_faces(direction, up, down, rows_out)


def halo_flux(z, wide_yz, rim_face, rim_rows, low_face, high_face, ghost_rows):
    _, planes, rows, width = wide_yz.shape
    at, row = slice(z, z + 1), row_of((rows, width))
    top = jnp.where(row == rows - 1, rim_rows[2, at] * ghost_rows[1, at], 0.0)
    flux = jnp.where(row == 0, wide_yz[0, z, 0:1] * ghost_rows[0, at], top)
    if z == 0:
        flux = flux + wide_yz[1, 0] * low_face[...]
    if z == planes - 1:
        flux = flux + rim_face[1] * high_face[0]
    return flux


def inner_kernel(number, weights, wide_ax, wide_yz, rim_face, rim_rows, field, old, inverse, sum_in, *refs):
    before, first, second = weights
    rims = rim_face, rim_rows
    halo, piece = (refs[:3], refs[3]) if before else (None, None)
    if second:
        residual, direction, total = refs[-3:]
    else:
        residual, total = refs[-2:]
    _, rows, columns = total.shape

    def plane(z):
        if not before:
            return field[z], old[z], sum_in[z]
        flux = halo_flux(z, wide_yz, *rims, *halo)
        step = before * (inverse[z] * flux)
        got = [jnp.zeros_like(piece[z])] * 3
        got[number - 2] = piece[z]
        return field[z] + step, old[z] + flux, sum_in[z] + step[:, :columns] + jnp.concatenate(got)

    def coef(part, z):
        return wide_ax[part, z] if part < 2 else wide_yz[part - 2, z]

    planes = wide_ax.shape[1]
    for z, (value, left, done), image in images(
        plane, coef, planes, rim_face[1], lambda z: rim_rows[2, z : z + 1]
    ):
        left = left - image
        if second:
            step = first * value + second * (inverse[z] * left)
            residual[z] = left
            direction[z] = step
            total[z] = done + step[:, :columns]
        else:
            residual[z] = left[:, :columns]
            total[z] = done


def faces_kernel(second, wide_yz, rim_face, rim_rows, low_face, high_face, ghost_rows, inverse, direction, up, down, rows_out):
    halo = wide_yz, rim_face, rim_rows, low_face, high_face, ghost_rows
    planes, rows, _ = direction.shape
    for z, out in ((0, down.at[0]), (planes - 1, up)):
        out[...] = direction[z] + second * (inverse[z] * halo_flux(z, *halo))
    for z in range(planes):
        at = slice(z, z + 1)
        for edge, row, out in ((0, 0, 1), (1, rows - 1, 0)):
            line = slice(row, row + 1)
            if z == 0:
                rows_out[out, at] = down[0, line]
            elif z == planes - 1:
                rows_out[out, at] = up[line]
            else:
                beta = rim_rows[2, at] if edge else wide_yz[0, z, line]
                flux = beta * ghost_rows[edge, at]
                rows_out[out, at] = direction[z, line] + second * (inverse[z, line] * flux)


def last_kernel(wide_yz, rim_face, rim_rows, low_face, high_face, ghost_rows, partial, residual):
    planes, _, columns = residual.shape
    for z in range(planes):
        flux = halo_flux(z, wide_yz, rim_face, rim_rows, low_face, high_face, ghost_rows)
        residual[z] = partial[z] + flux[:, :columns]


def local(old_fields, old_coef, held_slabs):
    _, slots, planes, rows, columns = old_fields.shape
    half = rows // 2
    rows = 3 * half
    width = columns + LANES
    full, own = f32(planes, rows, width), f32(planes, rows, columns)
    ids = held_slabs.reshape(2)
    vmem = pl.BlockSpec(memory_space=pltpu.VMEM)
    fields, coef, edge_out = pl.pallas_call(
        edge_kernel,
        out_shape=[
            f32(*old_fields.shape),
            jax.ShapeDtypeStruct(old_coef.shape, old_coef.dtype),
            f32(ROWS_AT + 3 * (planes // half) + 3 * planes, half, columns),
        ],
        in_specs=[pl.BlockSpec(memory_space=pltpu.SMEM)] + [pl.BlockSpec(memory_space=pltpu.HBM)] * 2,
        out_specs=[vmem] * 3,
        scratch_shapes=[pltpu.SemaphoreType.DMA((8,))],
        compiler_params=pltpu.CompilerParams(vmem_limit_bytes=VMEM_LIMIT),
    )(ids, *(pltpu.with_memory_space_constraint(array, pltpu.HBM) for array in (old_fields, old_coef)))
    edge_in = swapped(edge_out)
    coef_units = jax.ShapeDtypeStruct((2, 3, planes // 2, 2 * half, columns), jnp.bfloat16)
    (coef_ax,) = call(functools.partial(coef_kernel, 0), [coef_units], ids, coef, edge_out, ids=True)
    ax_in = swapped(coef_ax)
    third = f32(planes, half, columns)
    partial_out, partial, start_own, *start_out, _ = call(
        partial_kernel,
        [f32(3, planes, half, columns), own, own, third, third, third, f32(slots, planes, 2 * half, columns)],
        ids,
        fields,
        coef,
        coef_ax,
        ids=True,
    )
    partial_in = swapped(partial_out)
    strip = f32(4, 3, half, LANES)
    left, right = call(strip_kernel, [strip, strip], ids, fields, coef, edge_in, ids=True)
    from_left, from_right = shifted(right, "gx", 1), shifted(left, "gx", -1)
    coef_full = f32(2, planes, rows, width)
    edge_start, rhs_ghost, wide_yz, ghosts, own_rows, up, down, rows_out = call(
        gather_kernel,
        [
            f32(planes, rows, 2 * LANES),
            f32(planes, rows, LANES),
            coef_full,
            f32(2, planes, rows, LANES),
            f32(3, planes, columns),
            f32(rows, width),
            f32(2, rows, width),
            f32(3, planes, width),
        ],
        ids,
        fields,
        coef,
        edge_in,
        left,
        right,
        from_left,
        from_right,
        ids=True,
    )
    low_face, rim_face, rim_rows = shifted(up, "gz", 1), shifted(down, "gz", -1), row_ghosts(rows_out)
    (wide_ax,) = call(spread_kernel, [coef_full], ids, coef, ax_in, ghosts, ids=True)
    extra, part_inverse = call(
        first_kernel,
        [full, full],
        wide_ax,
        wide_yz,
        edge_start,
        rhs_ghost,
        own_rows,
        up,
        down,
        partial,
        low_face,
        rim_face,
    )
    pieces = [swapped(units) for units in start_out]
    first_list, second_list = chebyshev_weights(SWEEPS)
    faces = [f32(rows, width), f32(1, rows, width), f32(2, planes, width)]
    inverse, residual, direction, total, up, down, rows_out = call(
        functools.partial(start_kernel, second_list[0]),
        [full, full, full, own] + faces,
        partial_in,
        extra,
        part_inverse,
        start_own,
        wide_yz,
        rows_out,
        rim_rows,
    )
    rims, halo = (rim_face, rim_rows), ()
    for stage in range(1, SWEEPS + 1):
        before = second_list[stage - 1] if halo else 0.0
        last = stage == SWEEPS
        weights = (before, 0.0, 0.0) if last else (before, first_list[stage], second_list[stage])
        arrived = (*halo, pieces[stage - 2]) if halo else ()
        halo = shifted(up, "gz", 1), shifted(down, "gz", -1), row_ghosts(rows_out)
        state = call(
            functools.partial(inner_kernel, stage, weights),
            [own, own] if last else [full, full, own],
            wide_ax,
            wide_yz,
            *rims,
            direction,
            residual,
            inverse,
            total,
            *arrived,
        )
        if last:
            residual, total = state
            (residual,) = call(last_kernel, [own], wide_yz, *rims, *halo, residual)
        else:
            residual, direction, total = state
            up, down, rows_out = call(
                functools.partial(faces_kernel, second_list[stage]), faces, wide_yz, *rims, *halo, inverse, direction
            )
    return total, residual


def solution(mesh):
    in_specs = (
        P(None, "gy", "gz", None, "gx"),
        P(None, "gy", "gz", None, "gx"),
        P("gy", "gz", "gx"),
    )
    out_specs = (P("gz", "gy", "gx"), P("gz", "gy", "gx"))
    return jax.shard_map(local, mesh=mesh, in_specs=in_specs, out_specs=out_specs, check_vma=False)
```

```python
import functools

import jax
import jax.numpy as jnp
from jax import lax
from jax.experimental import pallas as pl
from jax.experimental.pallas import tpu as pltpu
from jax.sharding import PartitionSpec as P

SWEEPS = 4
LANES = 128
STRIP = 8
SHIFT = 4096.0
VMEM_LIMIT = 24 * 1024 * 1024


def chebyshev_weights(count):
    low_bound = 0.25
    high_bound = 2.0
    centre_value = 0.5 * (high_bound + low_bound)
    half_width = 0.5 * (high_bound - low_bound)
    ratio_value = centre_value / half_width
    damping = 1.0 / ratio_value
    first_list = [0.0]
    second_list = [1.0 / centre_value]
    for step_index in range(1, count):
        damping_next = 1.0 / (2.0 * ratio_value - damping)
        first_list.append(damping_next * damping)
        second_list.append(2.0 * damping_next / half_width)
        damping = damping_next
    return (first_list, second_list)


def shifted(value, axis, steps):
    count = lax.axis_size(axis)
    return lax.ppermute(value, axis, [(i, (i + steps) % count) for i in range(count)])


def swapped(value):
    return lax.ppermute(value, "gy", [(i, i ^ 1) for i in range(lax.axis_size("gy"))])


def row_ghosts(rows):
    if lax.axis_size("gy") == 2:
        return swapped(rows)
    return jnp.concatenate([shifted(rows[:1], "gy", 1), shifted(rows[1:], "gy", -1)])


def f32(*shape):
    return jax.ShapeDtypeStruct(shape, jnp.float32)


def call(kernel, outs, *operands, ids=False, sent=False):
    out_specs = [pl.BlockSpec(memory_space=pltpu.VMEM) for _ in outs]
    scratch = []
    if sent:
        out_specs = [pl.BlockSpec(memory_space=pltpu.HBM) for _ in outs]
        scratch = [pltpu.VMEM(out.shape, out.dtype) for out in outs] + [pltpu.SemaphoreType.DMA((4,)) for _ in outs]
    specs = [pl.BlockSpec(memory_space=pltpu.VMEM) for _ in operands]
    if ids:
        specs[0] = pl.BlockSpec(memory_space=pltpu.SMEM)
    return pl.pallas_call(
        kernel,
        out_shape=outs,
        in_specs=specs,
        out_specs=out_specs,
        scratch_shapes=scratch,
        compiler_params=pltpu.CompilerParams(vmem_limit_bytes=VMEM_LIMIT),
    )(*operands)


def lane_of(shape):
    return lax.broadcasted_iota(jnp.int32, shape, 1)


def row_of(shape):
    return lax.broadcasted_iota(jnp.int32, shape, 0)


def units_of(ids, half, numbers=(0, 1, 2)):
    first = 3 * (lax.axis_index("gy") // 2)
    a, b = ids[0] - first, ids[1] - first
    found = []
    for k in numbers:
        unit = (3 * half + k) % 6
        slab = unit // 2
        found.append((jnp.logical_or(a == slab, b == slab), jnp.where(a == slab, 0, 1), unit % 2))
    return found


def field_unit(fields, item, place, z):
    rows = fields.shape[3] // 2
    _, slot, part = place
    return fields[item, slot, z, pl.ds(pl.multiple_of(part * rows, rows), rows), :]


def coef_unit(coef, item, place, z):
    rows = coef.shape[3] // 2
    _, slot, part = place
    both = coef[item, slot, z].astype(jnp.float32)
    return jnp.where(part == 0, both[:rows], both[rows:])


def strips(fields, coef, item, place, planes):
    columns, rows = fields.shape[4], fields.shape[3] // 2
    group = lane_of((rows, LANES)) // STRIP
    low = jnp.zeros((rows, LANES), jnp.float32)
    high = jnp.zeros((rows, LANES), jnp.float32)
    for z in range(planes):
        if item < 2:
            cells = field_unit(fields, item, place, z)
        else:
            cells = coef_unit(coef, 2 * item - 4, place, z) + SHIFT * coef_unit(coef, 2 * item - 3, place, z)
        first, last = cells[:, :LANES], cells[:, columns - LANES :]
        turn = STRIP * z
        low = jnp.where(group == z, pltpu.roll(first, turn, 1) if turn else first, low)
        turn = (STRIP * z + STRIP) % LANES
        high = jnp.where(group == z, pltpu.roll(last, turn, 1) if turn else last, high)
    return low, high


def outer_strips(fields, coef, item, ids, half, planes):
    found = []
    for place in units_of(ids, half, (3, 5)):
        found.append([jnp.where(place[0], side, 0.0) for side in strips(fields, coef, item, place, planes)])
    above = row_of(found[0][0].shape) < found[0][0].shape[0] // 2
    return [jnp.where(above, high, low) for high, low in zip(*found)]


def outer_row(fields, ids, half, z):
    last = fields.shape[3] - 1
    (above_held, above_slot, _), (below_held, below_slot, _) = units_of(ids, half, (3, 5))
    above = jnp.where(above_held, fields[0, above_slot, z, 0:1], 0.0)
    below = jnp.where(below_held, fields[0, below_slot, z, last : last + 1], 0.0)
    return jnp.where(half == 0, below, above)


def brick_rows(ids, half, unit_rows):
    first = 3 * (lax.axis_index("gy") // 2)
    a, b = ids[0] - first, ids[1] - first
    found = []
    for j in range(3):
        slab = jnp.where(half == 0, j // 2, 1 + (j + 1) // 2)
        row = jnp.where((j + half) % 2 == 0, 0, 2 * unit_rows - 1)
        found.append((jnp.logical_or(a == slab, b == slab), jnp.where(a == slab, 0, 1), row))
    return found


def field_row(fields, place, z):
    last = fields.shape[3] - 1
    _, slot, row = place
    return jnp.where(row == 0, fields[0, slot, z, 0:1], fields[0, slot, z, last : last + 1])


PLANES_AT, ROWS_AT = 12, 18
FIRST_PAIRS = 16
NEXT_PAIRS = 45
PIECES = (1, 8, 15)
CODE_BITS = 20
ADDED_AT = (2, 4)


def pieces_at(stage):
    return [number for number, at in enumerate(ADDED_AT) if at == stage]


def power_of_two(number):
    size, result = jnp.abs(number), jnp.ones(number.shape, jnp.float32)
    for bit in range(7):
        factor = jnp.where(number < 0, 2.0 ** -(1 << bit), 2.0 ** (1 << bit))
        result = result * jnp.where((size >> bit) & 1 == 1, factor, 1.0)
    return result


def exponents_of(tops):
    return (jnp.floor(jnp.log2(jnp.maximum(tops, 1e-30)) + 0.001) + 1.0).astype(jnp.int32)


def encoded(tiles, factors, first):
    codes, limit = [], float((1 << CODE_BITS) - 1)
    for j, tile in enumerate(tiles):
        scaled = jnp.floor(tile * factors[:, first + j : first + j + 1] + 0.5)
        codes.append(jnp.clip(scaled, -limit, limit).astype(jnp.int32) + (1 << CODE_BITS))
    a, b, c = codes
    return a | (c & 0x7FF) << 21, b | (c >> 11) << 21


def decoded(words, scales, first):
    a, b = (word & 0x1FFFFF for word in words)
    c = lax.shift_right_logical(words[0], 21) | (lax.shift_right_logical(words[1], 21) << 11)
    tiles = []
    for j, code in enumerate((a, b, c)):
        tiles.append((code - (1 << CODE_BITS)).astype(jnp.float32) * scales[:, first + j : first + j + 1])
    return tiles


def scales_of(exponents):
    return power_of_two(exponents - CODE_BITS)


def piece_rows(piece, scales, number, z):
    at = 2 * (z - PIECES[number])
    if not 0 <= at < piece.shape[0]:
        return 0.0
    return jnp.concatenate(decoded((piece[at], piece[at + 1]), scales, 3 * (z - 1)))


def pair_at(ids, half, number, planes):
    unit = number % (3 * planes)
    part = 2 if number < 3 * planes else 0
    return part, unit // planes, unit % planes, units_of(ids, half)[unit // planes]


def pair_tile(ids, coef, half, number):
    part, _, z, place = pair_at(ids, half, number, coef.shape[2])
    return coef_unit(coef, part, place, z) + SHIFT * coef_unit(coef, part + 1, place, z)


def rim_at(planes, unit_rows):
    planes_at = ROWS_AT + 3 * (planes // unit_rows)
    outer_at = planes_at + 3 + planes // unit_rows
    return planes_at, planes_at + 3, outer_at, outer_at + 2 + 2 * (planes // unit_rows)


def beyond(fields, coef, ids, half, pairs, strip_out, row_out):
    planes = fields.shape[2]
    if pairs > 1:
        return
    for j, item in enumerate((0, 3)):
        strip_out(j, *outer_strips(fields, coef, item, ids, half, planes))
    (above,) = units_of(ids, half, (3,))
    for z in range(planes):
        row_out(0, z, outer_row(fields, ids, half, z))
        row_out(1, z, jnp.where(above[0], first_row(coef, above, z), 0.0))


def first_row(coef, place, z):
    rows = coef.shape[3] // 2
    both = coef[2, place[1], z].astype(jnp.float32)
    return jnp.where(place[2] == 0, both[0:1], both[rows : rows + 1])


def edge_kernel(pairs, ids_in, fields_in, coef_in, fields, coef, out, ids, sems):
    copies = [pltpu.make_async_copy(ids_in, ids, sems.at[0])]
    for item in range(2):
        for slot in range(2):
            at = len(copies)
            copies.append(pltpu.make_async_copy(fields_in.at[item, slot], fields.at[item, slot], sems.at[at]))
    for part in range(4):
        at = len(copies)
        copies.append(pltpu.make_async_copy(coef_in.at[part], coef.at[part], sems.at[at]))
    for copy in copies:
        copy.start()
    planes, unit_rows = fields.shape[2], fields.shape[3] // 2
    half = 1 - lax.axis_index("gy") % 2
    for copy in copies[:5]:
        copy.wait()
    for item in range(4):
        if item == 2:
            for copy in copies[5:]:
                copy.wait()
        for k, place in enumerate(units_of(ids, half)):
            low, high = strips(fields, coef, item, place, planes)
            out[3 * item + k] = jnp.concatenate([low, high], axis=1)
            if item < 2:
                out[PLANES_AT + 3 * item + k] = field_unit(fields, 0, place, item * (planes - 1))
    for j, place in enumerate(brick_rows(ids, half, unit_rows)):
        for z in range(planes):
            at = ROWS_AT + j * (planes // unit_rows) + z // unit_rows
            line = z % unit_rows
            out[at, line : line + 1] = field_row(fields, place, z)
    faces_at, lines_at, beyond_at, pairs_at = rim_at(planes, unit_rows)

    def strip_out(j, low, high):
        out[beyond_at + j] = jnp.concatenate([low, high], axis=1)

    def row_out(j, z, value):
        line = z % unit_rows
        out[beyond_at + 2 + j * (planes // unit_rows) + z // unit_rows, line : line + 1] = value

    beyond(fields, coef, ids, half, pairs, strip_out, row_out)
    places = units_of(ids, half)
    for k, place in enumerate(places):
        out[faces_at + k] = coef_unit(coef, 3, place, 0)
    for z in range(planes):
        line = z % unit_rows
        out[lines_at + z // unit_rows, line : line + 1] = first_row(coef, places[0], z)
    for number in range(FIRST_PAIRS):
        out[pairs_at + number] = pair_tile(ids, coef, half, number)


def coef_kernel(first, ids, coef, _, out):
    for number in range(out.shape[0]):
        out[number] = pair_tile(ids, coef, 1 - lax.axis_index("gy") % 2, first + number)


def outer_at(planes):
    return 6 * planes - FIRST_PAIRS - NEXT_PAIRS


def line_at(planes, unit_rows, edge, z):
    at = outer_at(planes) + 6 + edge * (planes // unit_rows) + z // unit_rows
    return at, slice(z % unit_rows, z % unit_rows + 1)


def partial_kernel(ids, fields, coef, _, out, middle, own, start_own, *refs):
    start_out, partial = refs[:-1], refs[-1]
    _, slots, planes, rows, columns = fields.shape
    lane, row = lane_of((rows, columns)), row_of((rows, columns))
    for slot in range(slots):
        value, lower = fields[0, slot, 0], 0.0
        for z in range(planes):
            alpha, beta_x, beta_y = (coef[part, slot, z].astype(jnp.float32) for part in range(3))
            flux_x = jnp.where(lane == 0, 0.0, beta_x * (value - pltpu.roll(value, 1, 1)))
            flux_y = jnp.where(row == 0, 0.0, beta_y * (value - pltpu.roll(value, 1, 0)))
            image = (
                alpha * value
                + (flux_x - pltpu.roll(flux_x, columns - 1, 1))
                + (flux_y - pltpu.roll(flux_y, rows - 1, 0))
                + lower
            )
            if z + 1 < planes:
                following = fields[0, slot, z + 1]
                lower = coef[3, slot, z + 1].astype(jnp.float32) * (following - value)
                image = image - lower
                value = following
            partial[slot, z] = fields[1, slot, z] - image
    half_rows = rows // 2
    half = lax.axis_index("gy") % 2
    for number in range(outer_at(planes)):
        out[number] = pair_tile(ids, coef, 1 - half, FIRST_PAIRS + NEXT_PAIRS + number)
    places = units_of(ids, half)
    for z in range(planes):
        for k, place in enumerate(places):
            held, slot, part = place
            at = pl.ds(pl.multiple_of(part * half_rows, half_rows), half_rows)
            line = slice(k * half_rows, (k + 1) * half_rows)
            own[z, line] = jnp.where(held, partial[slot, z, at, :], 0.0)
            start_own[z, line] = jnp.where(held, field_unit(fields, 0, place, z), 0.0)
    lane = lane_of((half_rows, columns))
    places = units_of(ids, 1 - half)
    tops = jnp.zeros((half_rows, columns), jnp.float32)
    shares = []
    for z in range(planes):
        lefts, starts = [], []
        for k, place in enumerate(places):
            held, slot, part = place
            at = pl.ds(pl.multiple_of(part * half_rows, half_rows), half_rows)
            lefts.append(jnp.where(held, partial[slot, z, at, :], 0.0))
            starts.append(jnp.where(held, field_unit(fields, 0, place, z), 0.0))
            if k != 1:
                row = 0 if k == 0 else half_rows - 1
                at_line, line_in = line_at(planes, half_rows, k // 2, z)
                out[at_line, line_in] = lefts[k][row : row + 1]
            if z % (planes - 1) == 0:
                out[outer_at(planes) + 3 * (z > 0) + k] = lefts[k]
        if z % (planes - 1) == 0:
            continue
        piece = sum(z >= end for end in PIECES[1:])
        shares.append((lefts, 3 * (z - 1), middle, 2 * (z - 1)))
        shares.append((starts, LANES + 3 * (z - 1), start_out[piece], 2 * (z - PIECES[piece])))
        for tiles, first, _, _ in shares[-2:]:
            for j, tile in enumerate(tiles):
                tops = jnp.where(lane == first + j, jnp.max(jnp.abs(tile), axis=1, keepdims=True), tops)
    exponents = exponents_of(tops)
    factors = power_of_two(CODE_BITS - exponents)
    for tiles, first, target, at in shares:
        target[at], target[at + 1] = encoded(tiles, factors, first)
    middle[2 * (planes - 2)] = exponents


def strip_kernel(pairs, ids, fields, coef, edge_in, left, right, outer_rows):
    planes, unit_rows = fields.shape[2], fields.shape[3] // 2
    half = lax.axis_index("gy") % 2
    for k, place in enumerate(units_of(ids, half)):
        for item in range(4):
            low, high = strips(fields, coef, item, place, planes)
            got = edge_in[3 * item + k]
            left[3 * item + k] = jnp.where(place[0], low, got[:, :LANES])
            right[3 * item + k] = jnp.where(place[0], high, got[:, LANES:])
    beyond_at = rim_at(planes, unit_rows)[2]

    def strip_out(j, low, high):
        got = edge_in[beyond_at + j]
        left[12 + j], right[12 + j] = low + got[:, :LANES], high + got[:, LANES:]

    def row_out(j, z, value):
        line = z % unit_rows
        got = edge_in[beyond_at + 2 + j * (planes // unit_rows) + z // unit_rows, line : line + 1]
        outer_rows[j, z : z + 1] = value + got

    if pairs > 1:
        outer_rows[...] = jnp.zeros_like(outer_rows)
        left[12:14] = jnp.zeros_like(left[12:14])
        right[12:14] = jnp.zeros_like(right[12:14])
    beyond(fields, coef, ids, half, pairs, strip_out, row_out)


def parted(both):
    second = jnp.floor(both * 0.125) * (8.0 / SHIFT)
    return both - SHIFT * second, second


def ghost_columns(from_left, from_right, item, k, z):
    low, high = from_left[3 * item + k], from_right[3 * item + k]
    turn = (LANES - STRIP * z) % LANES
    right = pltpu.roll(high, turn, 1) if turn else high
    turn = (LANES - STRIP - STRIP * z) % LANES
    left = pltpu.roll(low, turn, 1) if turn else low
    return jnp.where(lane_of(low.shape) < LANES // 2, right, left)


def gather_kernel(
    pairs, ids, fields, coef, edge_in, left, right, outer_rows, from_left, from_right,
    edge_start, rhs_ghost, ghosts, own_rows, up, down, rows_out, beyond_rows,
):
    _, _, planes, rows, columns = fields.shape
    rows //= 2
    half = lax.axis_index("gy") % 2
    for k, place in enumerate(units_of(ids, half)):
        at = slice(k * rows, (k + 1) * rows)
        for z in range(planes):
            edge_start[z, at, :LANES] = ghost_columns(right, left, 0, k, z)
            edge_start[z, at, LANES:] = ghost_columns(from_left, from_right, 0, k, z)
            rhs_ghost[z, at] = ghost_columns(from_left, from_right, 1, k, z)
            for item in (2, 3):
                both = ghost_columns(from_left, from_right, item, k, z)
                part = 2 * item - 4
                ghosts[part, z, at], ghosts[part + 1, z, at] = parted(both)
        for e, (z, out) in enumerate(((0, down.at[0]), (planes - 1, up))):
            own = field_unit(fields, 0, place, z)
            out[at, :columns] = jnp.where(place[0], own, edge_in[PLANES_AT + 3 * e + k])
            out[at, columns:] = edge_start[z, at, LANES:]
    faces_at, lines_at, _, _ = rim_at(planes, rows)
    places = units_of(ids, half)
    for k, place in enumerate(places):
        at = slice(k * rows, (k + 1) * rows)
        down[1, at, :columns] = jnp.where(place[0], coef_unit(coef, 3, place, 0), edge_in[faces_at + k])
    down[1, :, columns:] = ghosts[3, 0]
    for j, place in enumerate(brick_rows(ids, half, rows)):
        for z in range(planes):
            at = ROWS_AT + j * (planes // rows) + z // rows
            line = z % rows
            own_rows[j, z : z + 1] = jnp.where(place[0], field_row(fields, place, z), edge_in[at, line : line + 1])
    last = 3 * rows - 1
    for z in range(planes):
        line = slice(z, z + 1)
        for out, row, j, known in ((0, last, 2, half == 1), (1, 0, 0, half == 0)):
            edge = edge_start[z, row : row + 1]
            middle = jnp.concatenate([edge[:, :LANES]] * (columns // LANES), axis=1)
            rows_out[out, line, :columns] = jnp.where(known, own_rows[j, line], middle)
            rows_out[out, line, columns:] = edge[:, LANES:]
        got = edge_in[lines_at + z // rows, z % rows : z % rows + 1]
        rows_out[2, line, :columns] = jnp.where(places[0][0], first_row(coef, places[0], z), got)
        rows_out[2, line, columns:] = ghosts[2, z, 0:1]
        if pairs > 1:
            continue
        own = ghost_columns(right, left, 4, 0, z)
        ghost = ghost_columns(from_left, from_right, 4, 0, z)
        for out, row, known in ((0, rows - 1, half == 0), (1, 0, half == 1)):
            edge = own[row : row + 1]
            middle = jnp.concatenate([edge] * (columns // LANES), axis=1)
            beyond_rows[out, line, :columns] = jnp.where(known, outer_rows[0, line], middle)
            beyond_rows[out, line, columns:] = ghost[row : row + 1]
        beyond_rows[2, line, :columns] = outer_rows[1, line]
        beyond_rows[2, line, columns:] = parted(ghost_columns(from_left, from_right, 4, 1, z)[0:1])[0]
    if pairs > 1:
        beyond_rows[...] = jnp.zeros_like(beyond_rows)


def spread_kernel(ids, coef, edge_in, pairs, more_pairs, ghosts, wide_ax, wide_yz):
    planes, columns, rows = coef.shape[2], coef.shape[4], coef.shape[3] // 2
    pairs_at = rim_at(planes, rows)[3]
    for part in (0, 1):
        wide_ax[part, :, :, columns:] = ghosts[part]
        wide_yz[part, :, :, columns:] = ghosts[2 + part]
    for number in range(6 * planes):
        part, k, z, place = pair_at(ids, lax.axis_index("gy") % 2, number, planes)
        at = slice(k * rows, (k + 1) * rows)
        place_in = number - FIRST_PAIRS
        if place_in < 0:
            got = edge_in[pairs_at + number]
        elif place_in < pairs.shape[0]:
            got = pairs[place_in]
        else:
            got = more_pairs[place_in - pairs.shape[0]]
        for j, value in enumerate(parted(got)):
            out = wide_yz if part else wide_ax
            out[j, z, at, :columns] = jnp.where(place[0], coef_unit(coef, part + j, place, z), value)


def image_plane(value, lower_flux, upper_flux, alpha, beta_x, beta_y, rim_row):
    rows, width = value.shape
    flux_x = beta_x * (value - pltpu.roll(value, 1, 1))
    row = row_of(value.shape)
    before = jnp.where(row == 0, 0.0, pltpu.roll(value, 1, 0))
    flux_y = beta_y * (value - before)
    top = 0.0 if rim_row is None else -rim_row * value[rows - 1 : rows]
    after = jnp.where(row == rows - 1, top, pltpu.roll(flux_y, rows - 1, 0))
    return (
        alpha * value
        + (flux_x - pltpu.roll(flux_x, width - 1, 1))
        + (flux_y - after)
        + (lower_flux - upper_flux)
    )


def images(plane, coef, planes, rim_face, rim_row):
    (value, *others), beta_z = plane(0), coef(3, 0)
    lower = beta_z * value
    for z in range(planes):
        if z + 1 < planes:
            (following, *next_others), next_z = plane(z + 1), coef(3, z + 1)
            upper = next_z * (following - value)
        else:
            following, next_others, next_z = None, None, rim_face
            upper = 0.0 if rim_face is None else -rim_face * value
        image = image_plane(value, lower, upper, coef(0, z), coef(1, z), coef(2, z), rim_row(z))
        yield z, (value, *others), image
        value, others, lower, beta_z = following, next_others, upper, next_z


def edges(value):
    columns = value.shape[1] - LANES
    own = jnp.where(lane_of((value.shape[0], LANES)) < LANES // 2, value[:, :LANES], value[:, columns - LANES : columns])
    return jnp.concatenate([own, value[:, columns:]], axis=1)


def first_kernel(
    wide_ax, wide_yz, edge_start, rhs_ghost, own_rows, down, partial, extra, inverse
):
    planes, rows, width = extra.shape
    columns = width - LANES
    unit_rows = rows // 3
    even = lax.axis_index("gy") % 2 == 0

    def coef(part, z):
        return wide_ax[part, z] if part < 2 else wide_yz[part - 2, z]

    def ring(part, z):
        return edges(coef(part, z))

    lane, row = lane_of((rows, columns)), row_of((rows, columns))
    inner = jnp.where(even, 2 * unit_rows, unit_rows)
    for z, (value,), image in images(
        lambda z: (edge_start[z],),
        ring,
        planes,
        None,
        lambda z: None,
    ):
        flux = ring(1, z) * (value - pltpu.roll(value, 1, 1))
        gain = jnp.where(lane == 0, -flux[:, :columns], 0.0)
        far = jnp.where(lane == columns - 1, pltpu.roll(flux, LANES - 1, 1)[:, :columns], 0.0)
        gain = gain + far
        if z == 0:
            gain = gain - (wide_yz[1, 0] * down[0])[:, :columns]
        beta_y = wide_yz[0, z]
        at = slice(z, z + 1)
        between = jnp.where(even, own_rows[2, at] - own_rows[1, at], own_rows[1, at] - own_rows[0, at])
        beta = jnp.where(even, beta_y[2 * unit_rows : 2 * unit_rows + 1], beta_y[unit_rows : unit_rows + 1])
        between = beta[:, :columns] * between
        gain = gain + jnp.where(row == inner, -between, jnp.where(row == inner - 1, between, 0.0))
        low = jnp.where(even, beta_y[0:1, :columns] * own_rows[0, at], 0.0)
        gain = gain - jnp.where(row == 0, low, 0.0)
        extra[z, :, :columns] = gain + partial[z]
        extra[z, :, columns:] = rhs_ghost[z] - image[:, LANES:]
        beta_x, beta_z = wide_ax[1, z], wide_yz[1, z]
        next_z = wide_yz[1, z + 1] if z + 1 < planes else 0.0
        next_y = jnp.where(row_of((rows, width)) == rows - 1, 0.0, pltpu.roll(beta_y, rows - 1, 0))
        next_x = pltpu.roll(beta_x, width - 1, 1)
        inverse[z] = 1.0 / (wide_ax[0, z] + beta_x + next_x + beta_y + next_y + beta_z + next_z)


def start_rows(
    z, line, known, extra, part_inverse, wide_yz, own_up, own_last, low_face, high_face, ghost_rows
):
    planes, rows, width = extra.shape
    columns = known.shape[1]
    even = lax.axis_index("gy") % 2 == 0
    row = row_of((known.shape[0], width)) + line.start
    ghost = lane_of((1, width)) >= columns
    at = slice(z, z + 1)
    left = extra[z, line] + jnp.concatenate([known, jnp.zeros((known.shape[0], width - columns), jnp.float32)], axis=1)
    factor = part_inverse[z, line]
    if z == 0:
        left = left + wide_yz[1, 0, line] * low_face[line]
    if z == planes - 1:
        rim = high_face[1, line]
        left = left + rim * (high_face[0, line] - own_up[line])
        factor = factor / (1.0 + rim * factor)
    if line.start == 0:
        low = jnp.where(jnp.logical_or(ghost, even), wide_yz[0, z, 0:1] * ghost_rows[0, at], 0.0)
        left = left + jnp.where(row == 0, low, 0.0)
    if line.stop == rows:
        rim = ghost_rows[2, at]
        high = rim * (ghost_rows[1, at] - own_last[0, at])
        high = jnp.where(jnp.logical_and(jnp.logical_not(ghost), even), 0.0, high)
        left = left + jnp.where(row == rows - 1, high, 0.0)
        last = factor[factor.shape[0] - 1 :]
        factor = jnp.where(row == rows - 1, last / (1.0 + rim * last), factor)
    return left, factor


def partner_plane(z, planes, outer, middle=None, scales=None):
    if 0 < z < planes - 1:
        return jnp.concatenate(decoded((middle[2 * z - 2], middle[2 * z - 1]), scales, 3 * (z - 1)))
    return jnp.concatenate([outer[outer_at(planes) + 3 * (z > 0) + k] for k in range(3)])


def start_faces_kernel(second, outer, *refs):
    rest, (up, down, rows_out) = refs[:-3], refs[-3:]
    planes, rows, _ = rest[0].shape

    def step(z, line, known):
        left, factor = start_rows(z, line, known, *rest)
        return second * (factor * left)

    down[0] = step(0, slice(0, rows), partner_plane(0, planes, outer))
    up[...] = step(planes - 1, slice(0, rows), partner_plane(planes - 1, planes, outer))
    for z in range(planes):
        at = slice(z, z + 1)
        if z == 0:
            first, last = down[0, 0:1], down[0, rows - 1 : rows]
        elif z == planes - 1:
            first, last = up[0:1], up[rows - 1 : rows]
        else:
            lines = [outer[line_at(planes, outer.shape[1], edge, z)] for edge in range(2)]
            first, last = step(z, slice(0, 1), lines[0]), step(z, slice(rows - 1, rows), lines[1])
        rows_out[0, at], rows_out[1, at] = last, first


def start_kernel(second, outer, middle, start, *refs):
    own_down, *rest, inverse, residual, direction, total, start_scales = refs
    own_up = rest[3]
    planes, rows, _ = rest[0].shape
    columns = total.shape[2]
    scales = scales_of(middle[2 * (planes - 2)])
    start_scales[...] = scales[:, LANES:]
    for z in range(planes):
        known = partner_plane(z, planes, outer, middle, scales)
        left, factor = start_rows(z, slice(0, rows), known, *rest)
        step = second * (factor * left)
        inverse[z] = factor
        residual[z] = left
        direction[z] = step
        known = {0: own_down, planes - 1: own_up}.get(z)
        total[z] = (start[z] if known is None else known[:, :columns]) + step[:, :columns]


def halo_flux(z, wide_yz, rim_face, rim_rows, low_face, high_face, ghost_rows):
    _, planes, rows, width = wide_yz.shape
    at, row = slice(z, z + 1), row_of((rows, width))
    top = jnp.where(row == rows - 1, rim_rows[2, at] * ghost_rows[1, at], 0.0)
    flux = jnp.where(row == 0, wide_yz[0, z, 0:1] * ghost_rows[0, at], top)
    if z == 0:
        flux = flux + wide_yz[1, 0] * low_face[...]
    if z == planes - 1:
        flux = flux + rim_face[1] * high_face[0]
    return flux


def piecewise(source, target, sems):
    planes, pieces = source.shape[0], sems.shape[0]
    depth = planes // pieces
    copies = []
    for z in range(planes):
        if z % depth == depth - 1:
            at = pl.ds(z + 1 - depth, depth)
            copies.append(pltpu.make_async_copy(source.at[at], target.at[at], sems.at[z // depth]))
            copies[-1].start()
        yield
    for copy in copies:
        copy.wait()


def inner_kernel(weights, stage, wide_ax, wide_yz, rim_face, rim_rows, field, old, inverse, sum_in, *refs):
    before, first, second = weights
    rims = rim_face, rim_rows
    halo = refs[:3]
    if second:
        residual, direction, total = refs[-3:]
    else:
        residual, total = refs[-2:]
    planes, rows, columns = total.shape

    def plane(z):
        if not before:
            return field[z], old[z], sum_in[z]
        flux = halo_flux(z, wide_yz, *rims, *halo)
        step = before * (inverse[z] * flux)
        done = sum_in[z] + step[:, :columns]
        for place, number in enumerate(pieces_at(stage)):
            done = done + piece_rows(refs[4 + place], refs[3], number, z)
        return field[z] + step, old[z] + flux, done

    def coef(part, z):
        return wide_ax[part, z] if part < 2 else wide_yz[part - 2, z]

    for z, (value, left, done), image in images(
        plane, coef, planes, rim_face[1], lambda z: rim_rows[2, z : z + 1]
    ):
        left = left - image
        if second:
            step = first * value + second * (inverse[z] * left)
            residual[z] = left
            direction[z] = step
            total[z] = done + step[:, :columns]
        else:
            residual[z] = left[:, :columns]
            total[z] = done


def faces_kernel(second, wide_yz, rim_face, rim_rows, low_face, high_face, ghost_rows, inverse, direction, up, down, rows_out):
    halo = wide_yz, rim_face, rim_rows, low_face, high_face, ghost_rows
    planes, rows, _ = direction.shape
    for z, out in ((0, down.at[0]), (planes - 1, up)):
        out[...] = direction[z] + second * (inverse[z] * halo_flux(z, *halo))
    for z in range(planes):
        at = slice(z, z + 1)
        for edge, row, out in ((0, 0, 1), (1, rows - 1, 0)):
            line = slice(row, row + 1)
            if z == 0:
                rows_out[out, at] = down[0, line]
            elif z == planes - 1:
                rows_out[out, at] = up[line]
            else:
                beta = rim_rows[2, at] if edge else wide_yz[0, z, line]
                flux = beta * ghost_rows[edge, at]
                rows_out[out, at] = direction[z, line] + second * (inverse[z, line] * flux)


def last_kernel(wide_yz, rim_face, rim_rows, low_face, high_face, ghost_rows, partial, total, *refs):
    total_out, residual_out, whole, residual, total_sems, residual_sems = refs[-6:]
    planes, rows, columns = residual.shape
    copies = piecewise(whole, total_out, total_sems)
    for z in range(planes):
        done = total[z]
        for place, number in enumerate(pieces_at(SWEEPS + 1)):
            done = done + piece_rows(refs[1 + place], refs[0], number, z)
        whole[z] = done
        next(copies)
    more = piecewise(residual, residual_out, residual_sems)
    for z in range(planes):
        flux = halo_flux(z, wide_yz, rim_face, rim_rows, low_face, high_face, ghost_rows)
        residual[z] = partial[z] + flux[:, :columns]
        next(more)
    list(copies)
    list(more)


def local(old_fields, old_coef, held_slabs):
    _, slots, planes, rows, columns = old_fields.shape
    half = rows // 2
    rows = 3 * half
    width = columns + LANES
    full, own = f32(planes, rows, width), f32(planes, rows, columns)
    ids = held_slabs.reshape(2)
    vmem = pl.BlockSpec(memory_space=pltpu.VMEM)
    pairs = lax.axis_size("gy") // 2
    fields, coef, edge_out = pl.pallas_call(
        functools.partial(edge_kernel, pairs),
        out_shape=[
            f32(*old_fields.shape),
            jax.ShapeDtypeStruct(old_coef.shape, old_coef.dtype),
            f32(rim_at(planes, half)[3] + FIRST_PAIRS, half, columns),
        ],
        in_specs=[pl.BlockSpec(memory_space=pltpu.HBM)] * 3,
        out_specs=[vmem] * 3,
        scratch_shapes=[pltpu.SMEM((2,), jnp.int32), pltpu.SemaphoreType.DMA((9,))],
        compiler_params=pltpu.CompilerParams(vmem_limit_bytes=VMEM_LIMIT),
    )(*(pltpu.with_memory_space_constraint(array, pltpu.HBM) for array in (ids, old_fields, old_coef)))
    edge_in = swapped(edge_out)
    (pairs_out,) = call(
        functools.partial(coef_kernel, FIRST_PAIRS), [f32(NEXT_PAIRS, half, columns)], ids, coef, edge_out, ids=True
    )
    pairs_in = swapped(pairs_out)
    outer_out, middle, partial, start_own, *start_out, _ = call(
        partial_kernel,
        [
            f32(outer_at(planes) + 6 + 2 * (planes // half), half, columns),
            jax.ShapeDtypeStruct((2 * (planes - 2) + 1, half, columns), jnp.int32),
            own,
            own,
            *(
                jax.ShapeDtypeStruct((2 * (end - start), half, columns), jnp.int32)
                for start, end in zip(PIECES, PIECES[1:])
            ),
            f32(slots, planes, 2 * half, columns),
        ],
        ids,
        fields,
        coef,
        pairs_out,
        ids=True,
    )
    outer_in, middle_in = swapped(outer_out), swapped(middle)
    strip = f32(14, half, LANES)
    left, right, outer_rows = call(
        functools.partial(strip_kernel, pairs),
        [strip, strip, f32(2, planes, columns)],
        ids,
        fields,
        coef,
        edge_in,
        ids=True,
    )
    from_left, from_right = shifted(right, "gx", 1), shifted(left, "gx", -1)
    coef_full = f32(2, planes, rows, width)
    edge_start, rhs_ghost, ghosts, own_rows, up, down, rows_out, rim_rows = call(
        functools.partial(gather_kernel, pairs),
        [
            f32(planes, rows, 2 * LANES),
            f32(planes, rows, LANES),
            f32(4, planes, rows, LANES),
            f32(3, planes, columns),
            f32(rows, width),
            f32(2, rows, width),
            f32(3, planes, width),
            f32(3, planes, width),
        ],
        ids,
        fields,
        coef,
        edge_in,
        left,
        right,
        outer_rows,
        from_left,
        from_right,
        ids=True,
    )
    low_face, rim_face = shifted(up, "gz", 1), shifted(down, "gz", -1)
    if pairs > 1:
        rim_rows = row_ghosts(rows_out)
    wide_ax, wide_yz = call(
        spread_kernel, [coef_full, coef_full], ids, coef, edge_in, pairs_in, outer_in, ghosts, ids=True
    )
    extra, part_inverse = call(
        first_kernel, [full, full], wide_ax, wide_yz, edge_start, rhs_ghost, own_rows, down, partial
    )
    first_list, second_list = chebyshev_weights(SWEEPS)
    faces = [f32(rows, width), f32(1, rows, width), f32(2, planes, width)]
    down_start = down[0]
    rest = extra, part_inverse, wide_yz, up, rows_out, low_face, rim_face, rim_rows
    up, down, rows_out = call(functools.partial(start_faces_kernel, second_list[0]), faces, outer_in, *rest)
    inverse, residual, direction, total, scales = call(
        functools.partial(start_kernel, second_list[0]), [full, full, full, own, f32(half, LANES)], outer_in, middle_in, start_own, down_start, *rest
    )
    rims, halo, pieces = (rim_face, rim_rows), (), [swapped(units) for units in start_out]
    for stage in range(1, SWEEPS + 1):
        before = second_list[stage - 1] if halo else 0.0
        last = stage == SWEEPS
        weights = (before, 0.0, 0.0) if last else (before, first_list[stage], second_list[stage])
        arrived = (*halo, scales, *(pieces[number] for number in pieces_at(stage))) if halo else ()
        halo = shifted(up, "gz", 1), shifted(down, "gz", -1), row_ghosts(rows_out)
        residual, *state = call(
            functools.partial(inner_kernel, weights, stage),
            [own, own] if last else [full, full, own],
            wide_ax,
            wide_yz,
            *rims,
            direction,
            residual,
            inverse,
            total,
            *arrived,
        )
        if last:
            more = (pieces[number] for number in pieces_at(SWEEPS + 1))
            return tuple(call(last_kernel, [own, own], wide_yz, *rims, *halo, residual, *state, scales, *more, sent=True))
        direction, total = state
        up, down, rows_out = call(
            functools.partial(faces_kernel, second_list[stage]), faces, wide_yz, *rims, *halo, inverse, direction
        )


def solution(mesh):
    in_specs = (
        P(None, "gy", "gz", None, "gx"),
        P(None, "gy", "gz", None, "gx"),
        P("gy", "gz", "gx"),
    )
    out_specs = (P("gz", "gy", "gx"), P("gz", "gy", "gx"))
    return jax.shard_map(local, mesh=mesh, in_specs=in_specs, out_specs=out_specs, check_vma=False)
```

```python
import functools

import jax
import jax.numpy as jnp
from jax import lax
from jax.experimental import pallas as pl
from jax.experimental.pallas import tpu as pltpu
from jax.sharding import PartitionSpec as P

SWEEPS = 4
LANES = 128
STRIP = SWEEPS + 1
STRIPS_AT = (0, 3, 5, 7, 10)
SHIFT = 4096.0
VMEM_LIMIT = 24 * 1024 * 1024


def chebyshev_weights(count):
    low_bound = 0.25
    high_bound = 2.0
    centre_value = 0.5 * (high_bound + low_bound)
    half_width = 0.5 * (high_bound - low_bound)
    ratio_value = centre_value / half_width
    damping = 1.0 / ratio_value
    first_list = [0.0]
    second_list = [1.0 / centre_value]
    for step_index in range(1, count):
        damping_next = 1.0 / (2.0 * ratio_value - damping)
        first_list.append(damping_next * damping)
        second_list.append(2.0 * damping_next / half_width)
        damping = damping_next
    return (first_list, second_list)


def shifted(value, axis, steps):
    count = lax.axis_size(axis)
    return lax.ppermute(value, axis, [(i, (i + steps) % count) for i in range(count)])


def swapped(value):
    return lax.ppermute(value, "gy", [(i, i ^ 1) for i in range(lax.axis_size("gy"))])


def row_ghosts(rows):
    if lax.axis_size("gy") == 2:
        return swapped(rows)
    return jnp.concatenate([shifted(rows[:1], "gy", 1), shifted(rows[1:], "gy", -1)])


def f32(*shape):
    return jax.ShapeDtypeStruct(shape, jnp.float32)


def call(kernel, outs, *operands, ids=False, sent=False):
    out_specs = [pl.BlockSpec(memory_space=pltpu.VMEM) for _ in outs]
    scratch = []
    if sent:
        out_specs = [pl.BlockSpec(memory_space=pltpu.HBM) for _ in outs]
        scratch = [pltpu.VMEM(out.shape, out.dtype) for out in outs] + [pltpu.SemaphoreType.DMA((4,)) for _ in outs]
    specs = [pl.BlockSpec(memory_space=pltpu.VMEM) for _ in operands]
    if ids:
        specs[0] = pl.BlockSpec(memory_space=pltpu.SMEM)
    return pl.pallas_call(
        kernel,
        out_shape=outs,
        in_specs=specs,
        out_specs=out_specs,
        scratch_shapes=scratch,
        compiler_params=pltpu.CompilerParams(vmem_limit_bytes=VMEM_LIMIT),
    )(*operands)


def lane_of(shape):
    return lax.broadcasted_iota(jnp.int32, shape, 1)


def row_of(shape):
    return lax.broadcasted_iota(jnp.int32, shape, 0)


def units_of(ids, half, numbers=(0, 1, 2)):
    first = 3 * (lax.axis_index("gy") // 2)
    a, b = ids[0] - first, ids[1] - first
    found = []
    for k in numbers:
        unit = (3 * half + k) % 6
        slab = unit // 2
        found.append((jnp.logical_or(a == slab, b == slab), jnp.where(a == slab, 0, 1), unit % 2))
    return found


def field_unit(fields, item, place, z):
    rows = fields.shape[3] // 2
    _, slot, part = place
    return fields[item, slot, z, pl.ds(pl.multiple_of(part * rows, rows), rows), :]


def coef_unit(coef, item, place, z):
    rows = coef.shape[3] // 2
    _, slot, part = place
    both = coef[item, slot, z].astype(jnp.float32)
    return jnp.where(part == 0, both[:rows], both[rows:])


def strip_at(item, k, z, planes):
    group = k * planes + z
    return STRIPS_AT[item] + group // (LANES // STRIP), STRIP * (group % (LANES // STRIP))


def strips(fields, coef, item, ids, half, pairs, store):
    planes, columns, rows = fields.shape[2], fields.shape[4], fields.shape[3] // 2
    lane, row = lane_of((rows, LANES)), row_of((rows, columns))
    numbers = (0, 1, 2, 3, 5) if pairs == 1 and item in (0, 3) else (0, 1, 2)
    places = units_of(ids, half, numbers)

    def cells(place, z):
        if item < 2:
            found = field_unit(fields, item, place, z)
        else:
            found = coef_unit(coef, 2 * item - 4, place, z) + SHIFT * coef_unit(coef, 2 * item - 3, place, z)
        return jnp.where(place[0], found, 0.0)

    tiles = {at: [jnp.zeros((rows, LANES), jnp.float32)] * 2 for at in range(STRIPS_AT[item], STRIPS_AT[item + 1])}
    for k in range(min(len(places), 4)):
        for z in range(planes):
            value = cells(places[k], z)
            if k == 3:
                value = jnp.where(row < rows // 2, value, cells(places[4], z))
            at, first = strip_at(item, k, z, planes)
            inside = jnp.logical_and(lane >= first, lane < first + STRIP)
            for side, start, turn in ((0, 0, first), (1, columns - LANES, (first + STRIP) % LANES)):
                part = value[:, start : start + LANES]
                part = pltpu.roll(part, turn, 1) if turn else part
                tiles[at][side] = jnp.where(inside, part, tiles[at][side])
    for at, (low, high) in tiles.items():
        store(at, low, high)


def outer_row(fields, ids, half, z):
    last = fields.shape[3] - 1
    (above_held, above_slot, _), (below_held, below_slot, _) = units_of(ids, half, (3, 5))
    above = jnp.where(above_held, fields[0, above_slot, z, 0:1], 0.0)
    below = jnp.where(below_held, fields[0, below_slot, z, last : last + 1], 0.0)
    return jnp.where(half == 0, below, above)


def brick_rows(ids, half, unit_rows):
    first = 3 * (lax.axis_index("gy") // 2)
    a, b = ids[0] - first, ids[1] - first
    found = []
    for j in range(3):
        slab = jnp.where(half == 0, j // 2, 1 + (j + 1) // 2)
        row = jnp.where((j + half) % 2 == 0, 0, 2 * unit_rows - 1)
        found.append((jnp.logical_or(a == slab, b == slab), jnp.where(a == slab, 0, 1), row))
    return found


def field_row(fields, place, z):
    last = fields.shape[3] - 1
    _, slot, row = place
    return jnp.where(row == 0, fields[0, slot, z, 0:1], fields[0, slot, z, last : last + 1])


PLANES_AT, ROWS_AT = 10, 16
FIRST_PAIRS = 20
NEXT_PAIRS = 43
PIECES = (1, 7, 15)
CODE_BITS = 20
ADDED_AT = (2, 4)


def pieces_at(stage):
    return [number for number, at in enumerate(ADDED_AT) if at == stage]


def power_of_two(number):
    size, result = jnp.abs(number), jnp.ones(number.shape, jnp.float32)
    for bit in range(7):
        factor = jnp.where(number < 0, 2.0 ** -(1 << bit), 2.0 ** (1 << bit))
        result = result * jnp.where((size >> bit) & 1 == 1, factor, 1.0)
    return result


def exponents_of(tops):
    return (jnp.floor(jnp.log2(jnp.maximum(tops, 1e-30)) + 0.001) + 1.0).astype(jnp.int32)


def encoded(tiles, factors, first):
    codes, limit = [], float((1 << CODE_BITS) - 1)
    for j, tile in enumerate(tiles):
        scaled = jnp.floor(tile * factors[:, first + j : first + j + 1] + 0.5)
        codes.append(jnp.clip(scaled, -limit, limit).astype(jnp.int32) + (1 << CODE_BITS))
    a, b, c = codes
    return a | (c & 0x7FF) << 21, b | (c >> 11) << 21


def decoded(words, scales, first):
    a, b = (word & 0x1FFFFF for word in words)
    c = lax.shift_right_logical(words[0], 21) | (lax.shift_right_logical(words[1], 21) << 11)
    tiles = []
    for j, code in enumerate((a, b, c)):
        tiles.append((code - (1 << CODE_BITS)).astype(jnp.float32) * scales[:, first + j : first + j + 1])
    return tiles


def scales_of(exponents):
    return power_of_two(exponents - CODE_BITS)


def piece_rows(piece, scales, number, z):
    at = 2 * (z - PIECES[number])
    if not 0 <= at < piece.shape[0]:
        return 0.0
    return jnp.concatenate(decoded((piece[at], piece[at + 1]), scales, 3 * (z - 1)))


def pair_order(planes):
    rest = [(2, k, z) for k in (1, 2) for z in range(1, planes)]
    return (
        [(2, 0, z) for z in range(planes)]
        + [(2, 1, 0), (2, 2, 0)]
        + rest
        + [(0, k, z) for k in range(3) for z in range(planes)]
    )


def pair_tile(ids, coef, half, number):
    part, k, z = pair_order(coef.shape[2])[number]
    place = units_of(ids, half)[k]
    return coef_unit(coef, part, place, z) + SHIFT * coef_unit(coef, part + 1, place, z)


def beyond_at(planes, unit_rows):
    start = ROWS_AT + 3 * (planes // unit_rows)
    return start, start + 2 * (planes // unit_rows)


def beyond(fields, coef, ids, half, pairs, row_out):
    if pairs > 1:
        return
    (above,) = units_of(ids, half, (3,))
    for z in range(fields.shape[2]):
        row_out(0, z, outer_row(fields, ids, half, z))
        row_out(1, z, jnp.where(above[0], first_row(coef, above, z), 0.0))


def first_row(coef, place, z):
    rows = coef.shape[3] // 2
    both = coef[2, place[1], z].astype(jnp.float32)
    return jnp.where(place[2] == 0, both[0:1], both[rows : rows + 1])


def edge_kernel(pairs, ids_in, fields_in, coef_in, fields, coef, out, ids, sems):
    copies = [pltpu.make_async_copy(ids_in, ids, sems.at[0])]
    for item in range(2):
        for slot in range(2):
            at = len(copies)
            copies.append(pltpu.make_async_copy(fields_in.at[item, slot], fields.at[item, slot], sems.at[at]))
    for part in range(4):
        at = len(copies)
        copies.append(pltpu.make_async_copy(coef_in.at[part], coef.at[part], sems.at[at]))
    for copy in copies:
        copy.start()
    planes, unit_rows = fields.shape[2], fields.shape[3] // 2
    half = 1 - lax.axis_index("gy") % 2
    for copy in copies[:5]:
        copy.wait()
    def strip_out(at, low, high):
        out[at] = jnp.concatenate([low, high], axis=1)

    for item in range(4):
        if item == 2:
            for copy in copies[5:]:
                copy.wait()
        strips(fields, coef, item, ids, half, pairs, strip_out)
        if item < 2:
            for k, place in enumerate(units_of(ids, half)):
                out[PLANES_AT + 3 * item + k] = field_unit(fields, 0, place, item * (planes - 1))
    for j, place in enumerate(brick_rows(ids, half, unit_rows)):
        for z in range(planes):
            at = ROWS_AT + j * (planes // unit_rows) + z // unit_rows
            line = z % unit_rows
            out[at, line : line + 1] = field_row(fields, place, z)
    rows_at, pairs_at = beyond_at(planes, unit_rows)

    def row_out(j, z, value):
        line = z % unit_rows
        out[rows_at + j * (planes // unit_rows) + z // unit_rows, line : line + 1] = value

    beyond(fields, coef, ids, half, pairs, row_out)
    for number in range(FIRST_PAIRS):
        out[pairs_at + number] = pair_tile(ids, coef, half, number)


def coef_kernel(first, ids, coef, _, out):
    for number in range(out.shape[0]):
        out[number] = pair_tile(ids, coef, 1 - lax.axis_index("gy") % 2, first + number)


def outer_at(planes):
    return 6 * planes - FIRST_PAIRS - NEXT_PAIRS


def line_at(planes, unit_rows, edge, z):
    at = outer_at(planes) + 6 + edge * (planes // unit_rows) + z // unit_rows
    return at, slice(z % unit_rows, z % unit_rows + 1)


def partial_kernel(ids, fields, coef, _, out, middle, own, start_own, *refs):
    start_out, partial = refs[:-1], refs[-1]
    _, slots, planes, rows, columns = fields.shape
    lane, row = lane_of((rows, columns)), row_of((rows, columns))
    for slot in range(slots):
        value, lower = fields[0, slot, 0], 0.0
        for z in range(planes):
            alpha, beta_x, beta_y = (coef[part, slot, z].astype(jnp.float32) for part in range(3))
            flux_x = jnp.where(lane == 0, 0.0, beta_x * (value - pltpu.roll(value, 1, 1)))
            flux_y = jnp.where(row == 0, 0.0, beta_y * (value - pltpu.roll(value, 1, 0)))
            image = (
                alpha * value
                + (flux_x - pltpu.roll(flux_x, columns - 1, 1))
                + (flux_y - pltpu.roll(flux_y, rows - 1, 0))
                + lower
            )
            if z + 1 < planes:
                following = fields[0, slot, z + 1]
                lower = coef[3, slot, z + 1].astype(jnp.float32) * (following - value)
                image = image - lower
                value = following
            partial[slot, z] = fields[1, slot, z] - image
    half_rows = rows // 2
    half = lax.axis_index("gy") % 2
    for number in range(outer_at(planes)):
        out[number] = pair_tile(ids, coef, 1 - half, FIRST_PAIRS + NEXT_PAIRS + number)
    places = units_of(ids, half)
    for z in range(planes):
        for k, place in enumerate(places):
            held, slot, part = place
            at = pl.ds(pl.multiple_of(part * half_rows, half_rows), half_rows)
            line = slice(k * half_rows, (k + 1) * half_rows)
            own[z, line] = jnp.where(held, partial[slot, z, at, :], 0.0)
            start_own[z, line] = jnp.where(held, field_unit(fields, 0, place, z), 0.0)
    lane = lane_of((half_rows, columns))
    places = units_of(ids, 1 - half)
    tops = jnp.zeros((half_rows, columns), jnp.float32)
    shares = []
    for z in range(planes):
        lefts, starts = [], []
        for k, place in enumerate(places):
            held, slot, part = place
            at = pl.ds(pl.multiple_of(part * half_rows, half_rows), half_rows)
            lefts.append(jnp.where(held, partial[slot, z, at, :], 0.0))
            starts.append(jnp.where(held, field_unit(fields, 0, place, z), 0.0))
            if k != 1:
                row = 0 if k == 0 else half_rows - 1
                at_line, line_in = line_at(planes, half_rows, k // 2, z)
                out[at_line, line_in] = lefts[k][row : row + 1]
            if z % (planes - 1) == 0:
                out[outer_at(planes) + 3 * (z > 0) + k] = lefts[k]
        if z % (planes - 1) == 0:
            continue
        piece = sum(z >= end for end in PIECES[1:])
        shares.append((lefts, 3 * (z - 1), middle, 2 * (z - 1)))
        shares.append((starts, LANES + 3 * (z - 1), start_out[piece], 2 * (z - PIECES[piece])))
        for tiles, first, _, _ in shares[-2:]:
            for j, tile in enumerate(tiles):
                tops = jnp.where(lane == first + j, jnp.max(jnp.abs(tile), axis=1, keepdims=True), tops)
    exponents = exponents_of(tops)
    factors = power_of_two(CODE_BITS - exponents)
    for tiles, first, target, at in shares:
        target[at], target[at + 1] = encoded(tiles, factors, first)
    middle[2 * (planes - 2)] = exponents


def strip_kernel(pairs, ids, fields, coef, edge_in, left, right, outer_rows):
    planes, unit_rows = fields.shape[2], fields.shape[3] // 2
    half = lax.axis_index("gy") % 2

    def strip_out(at, low, high):
        got = edge_in[at]
        left[at], right[at] = low + got[:, :LANES], high + got[:, LANES:]

    for item in range(4):
        strips(fields, coef, item, ids, half, pairs, strip_out)
    rows_at, _ = beyond_at(planes, unit_rows)

    def row_out(j, z, value):
        line = z % unit_rows
        got = edge_in[rows_at + j * (planes // unit_rows) + z // unit_rows, line : line + 1]
        outer_rows[j, z : z + 1] = value + got

    if pairs > 1:
        outer_rows[...] = jnp.zeros_like(outer_rows)
    beyond(fields, coef, ids, half, pairs, row_out)


def parted(both):
    second = jnp.floor(both * 0.125) * (8.0 / SHIFT)
    return both - SHIFT * second, second


def ghost_columns(from_left, from_right, item, k, z, planes):
    at, first = strip_at(item, k, z, planes)
    low, high = from_left[at], from_right[at]
    turn = (LANES - first) % LANES
    right = pltpu.roll(high, turn, 1) if turn else high
    turn = (LANES - STRIP - first) % LANES
    left = pltpu.roll(low, turn, 1) if turn else low
    lane = lane_of(low.shape)
    return jnp.where(lane < STRIP, right, jnp.where(lane >= LANES - STRIP, left, 1.0))


def gather_kernel(
    pairs, ids, fields, coef, edge_in, left, right, outer_rows, from_left, from_right,
    edge_start, rhs_ghost, ghosts, own_rows, up, down, rows_out, beyond_rows,
):
    _, _, planes, rows, columns = fields.shape
    rows //= 2
    half = lax.axis_index("gy") % 2
    for k, place in enumerate(units_of(ids, half)):
        at = slice(k * rows, (k + 1) * rows)
        for z in range(planes):
            edge_start[z, at, :LANES] = ghost_columns(right, left, 0, k, z, planes)
            edge_start[z, at, LANES:] = ghost_columns(from_left, from_right, 0, k, z, planes)
            rhs_ghost[z, at] = ghost_columns(from_left, from_right, 1, k, z, planes)
            for item in (2, 3):
                both = ghost_columns(from_left, from_right, item, k, z, planes)
                part = 2 * item - 4
                ghosts[part, z, at], ghosts[part + 1, z, at] = parted(both)
        for e, (z, out) in enumerate(((0, down.at[0]), (planes - 1, up))):
            own = field_unit(fields, 0, place, z)
            out[at, :columns] = jnp.where(place[0], own, edge_in[PLANES_AT + 3 * e + k])
            out[at, columns:] = edge_start[z, at, LANES:]
    _, pairs_at = beyond_at(planes, rows)
    places = units_of(ids, half)
    for k, place in enumerate(places):
        at = slice(k * rows, (k + 1) * rows)
        down[1, at, :columns] = jnp.where(
            place[0], coef_unit(coef, 3, place, 0), parted(edge_in[pairs_at + (planes - 1 + k if k else 0)])[1]
        )
    down[1, :, columns:] = ghosts[3, 0]
    for j, place in enumerate(brick_rows(ids, half, rows)):
        for z in range(planes):
            at = ROWS_AT + j * (planes // rows) + z // rows
            line = z % rows
            own_rows[j, z : z + 1] = jnp.where(place[0], field_row(fields, place, z), edge_in[at, line : line + 1])
    last = 3 * rows - 1
    for z in range(planes):
        line = slice(z, z + 1)
        for out, row, j, known in ((0, last, 2, half == 1), (1, 0, 0, half == 0)):
            edge = edge_start[z, row : row + 1]
            middle = jnp.concatenate([edge[:, :LANES]] * (columns // LANES), axis=1)
            rows_out[out, line, :columns] = jnp.where(known, own_rows[j, line], middle)
            rows_out[out, line, columns:] = edge[:, LANES:]
        got = parted(edge_in[pairs_at + z, 0:1])[0]
        rows_out[2, line, :columns] = jnp.where(places[0][0], first_row(coef, places[0], z), got)
        rows_out[2, line, columns:] = ghosts[2, z, 0:1]
        if pairs > 1:
            continue
        own = ghost_columns(right, left, 0, 3, z, planes)
        ghost = ghost_columns(from_left, from_right, 0, 3, z, planes)
        for out, row, known in ((0, rows - 1, half == 0), (1, 0, half == 1)):
            edge = own[row : row + 1]
            middle = jnp.concatenate([edge] * (columns // LANES), axis=1)
            beyond_rows[out, line, :columns] = jnp.where(known, outer_rows[0, line], middle)
            beyond_rows[out, line, columns:] = ghost[row : row + 1]
        beyond_rows[2, line, :columns] = outer_rows[1, line]
        beyond_rows[2, line, columns:] = parted(ghost_columns(from_left, from_right, 3, 3, z, planes)[0:1])[0]
    if pairs > 1:
        beyond_rows[...] = jnp.zeros_like(beyond_rows)


def spread_kernel(ids, coef, edge_in, pairs, more_pairs, ghosts, wide_ax, wide_yz):
    planes, columns, rows = coef.shape[2], coef.shape[4], coef.shape[3] // 2
    places, pairs_at = units_of(ids, lax.axis_index("gy") % 2), beyond_at(planes, rows)[1]
    for part in (0, 1):
        wide_ax[part, :, :, columns:] = ghosts[part]
        wide_yz[part, :, :, columns:] = ghosts[2 + part]
    for number, (part, k, z) in enumerate(pair_order(planes)):
        place = places[k]
        at = slice(k * rows, (k + 1) * rows)
        place_in = number - FIRST_PAIRS
        if place_in < 0:
            got = edge_in[pairs_at + number]
        elif place_in < pairs.shape[0]:
            got = pairs[place_in]
        else:
            got = more_pairs[place_in - pairs.shape[0]]
        for j, value in enumerate(parted(got)):
            out = wide_yz if part else wide_ax
            out[j, z, at, :columns] = jnp.where(place[0], coef_unit(coef, part + j, place, z), value)


def image_plane(value, lower_flux, upper_flux, alpha, beta_x, beta_y, rim_row):
    rows, width = value.shape
    flux_x = beta_x * (value - pltpu.roll(value, 1, 1))
    row = row_of(value.shape)
    before = jnp.where(row == 0, 0.0, pltpu.roll(value, 1, 0))
    flux_y = beta_y * (value - before)
    top = 0.0 if rim_row is None else -rim_row * value[rows - 1 : rows]
    after = jnp.where(row == rows - 1, top, pltpu.roll(flux_y, rows - 1, 0))
    return (
        alpha * value
        + (flux_x - pltpu.roll(flux_x, width - 1, 1))
        + (flux_y - after)
        + (lower_flux - upper_flux)
    )


def images(plane, coef, planes, rim_face, rim_row):
    (value, *others), beta_z = plane(0), coef(3, 0)
    lower = beta_z * value
    for z in range(planes):
        if z + 1 < planes:
            (following, *next_others), next_z = plane(z + 1), coef(3, z + 1)
            upper = next_z * (following - value)
        else:
            following, next_others, next_z = None, None, rim_face
            upper = 0.0 if rim_face is None else -rim_face * value
        image = image_plane(value, lower, upper, coef(0, z), coef(1, z), coef(2, z), rim_row(z))
        yield z, (value, *others), image
        value, others, lower, beta_z = following, next_others, upper, next_z


def edges(value):
    columns = value.shape[1] - LANES
    own = jnp.where(lane_of((value.shape[0], LANES)) < LANES // 2, value[:, :LANES], value[:, columns - LANES : columns])
    return jnp.concatenate([own, value[:, columns:]], axis=1)


def first_kernel(
    wide_ax, wide_yz, edge_start, rhs_ghost, own_rows, down, partial, extra, inverse
):
    planes, rows, width = extra.shape
    columns = width - LANES
    unit_rows = rows // 3
    even = lax.axis_index("gy") % 2 == 0

    def coef(part, z):
        return wide_ax[part, z] if part < 2 else wide_yz[part - 2, z]

    def ring(part, z):
        return edges(coef(part, z))

    lane, row = lane_of((rows, columns)), row_of((rows, columns))
    inner = jnp.where(even, 2 * unit_rows, unit_rows)
    for z, (value,), image in images(
        lambda z: (edge_start[z],),
        ring,
        planes,
        None,
        lambda z: None,
    ):
        flux = ring(1, z) * (value - pltpu.roll(value, 1, 1))
        gain = jnp.where(lane == 0, -flux[:, :columns], 0.0)
        far = jnp.where(lane == columns - 1, pltpu.roll(flux, LANES - 1, 1)[:, :columns], 0.0)
        gain = gain + far
        if z == 0:
            gain = gain - (wide_yz[1, 0] * down[0])[:, :columns]
        beta_y = wide_yz[0, z]
        at = slice(z, z + 1)
        between = jnp.where(even, own_rows[2, at] - own_rows[1, at], own_rows[1, at] - own_rows[0, at])
        beta = jnp.where(even, beta_y[2 * unit_rows : 2 * unit_rows + 1], beta_y[unit_rows : unit_rows + 1])
        between = beta[:, :columns] * between
        gain = gain + jnp.where(row == inner, -between, jnp.where(row == inner - 1, between, 0.0))
        low = jnp.where(even, beta_y[0:1, :columns] * own_rows[0, at], 0.0)
        gain = gain - jnp.where(row == 0, low, 0.0)
        extra[z, :, :columns] = gain + partial[z]
        extra[z, :, columns:] = rhs_ghost[z] - image[:, LANES:]
        beta_x, beta_z = wide_ax[1, z], wide_yz[1, z]
        next_z = wide_yz[1, z + 1] if z + 1 < planes else 0.0
        next_y = jnp.where(row_of((rows, width)) == rows - 1, 0.0, pltpu.roll(beta_y, rows - 1, 0))
        next_x = pltpu.roll(beta_x, width - 1, 1)
        inverse[z] = 1.0 / (wide_ax[0, z] + beta_x + next_x + beta_y + next_y + beta_z + next_z)


def start_rows(
    z, line, known, extra, part_inverse, wide_yz, own_up, own_last, low_face, high_face, ghost_rows
):
    planes, rows, width = extra.shape
    columns = known.shape[1]
    even = lax.axis_index("gy") % 2 == 0
    row = row_of((known.shape[0], width)) + line.start
    ghost = lane_of((1, width)) >= columns
    at = slice(z, z + 1)
    left = extra[z, line] + jnp.concatenate([known, jnp.zeros((known.shape[0], width - columns), jnp.float32)], axis=1)
    factor = part_inverse[z, line]
    if z == 0:
        left = left + wide_yz[1, 0, line] * low_face[line]
    if z == planes - 1:
        rim = high_face[1, line]
        left = left + rim * (high_face[0, line] - own_up[line])
        factor = factor / (1.0 + rim * factor)
    if line.start == 0:
        low = jnp.where(jnp.logical_or(ghost, even), wide_yz[0, z, 0:1] * ghost_rows[0, at], 0.0)
        left = left + jnp.where(row == 0, low, 0.0)
    if line.stop == rows:
        rim = ghost_rows[2, at]
        high = rim * (ghost_rows[1, at] - own_last[0, at])
        high = jnp.where(jnp.logical_and(jnp.logical_not(ghost), even), 0.0, high)
        left = left + jnp.where(row == rows - 1, high, 0.0)
        last = factor[factor.shape[0] - 1 :]
        factor = jnp.where(row == rows - 1, last / (1.0 + rim * last), factor)
    return left, factor


def partner_plane(z, planes, outer, middle=None, scales=None):
    if 0 < z < planes - 1:
        return jnp.concatenate(decoded((middle[2 * z - 2], middle[2 * z - 1]), scales, 3 * (z - 1)))
    return jnp.concatenate([outer[outer_at(planes) + 3 * (z > 0) + k] for k in range(3)])


def start_faces_kernel(second, outer, *refs):
    rest, (up, down, rows_out) = refs[:-3], refs[-3:]
    planes, rows, _ = rest[0].shape

    def step(z, line, known):
        left, factor = start_rows(z, line, known, *rest)
        return second * (factor * left)

    down[0] = step(0, slice(0, rows), partner_plane(0, planes, outer))
    up[...] = step(planes - 1, slice(0, rows), partner_plane(planes - 1, planes, outer))
    for z in range(planes):
        at = slice(z, z + 1)
        if z == 0:
            first, last = down[0, 0:1], down[0, rows - 1 : rows]
        elif z == planes - 1:
            first, last = up[0:1], up[rows - 1 : rows]
        else:
            lines = [outer[line_at(planes, outer.shape[1], edge, z)] for edge in range(2)]
            first, last = step(z, slice(0, 1), lines[0]), step(z, slice(rows - 1, rows), lines[1])
        rows_out[0, at], rows_out[1, at] = last, first


def start_kernel(second, outer, middle, start, *refs):
    own_down, *rest, inverse, residual, direction, total, start_scales = refs
    own_up = rest[3]
    planes, rows, _ = rest[0].shape
    columns = total.shape[2]
    scales = scales_of(middle[2 * (planes - 2)])
    start_scales[...] = scales[:, LANES:]
    for z in range(planes):
        known = partner_plane(z, planes, outer, middle, scales)
        left, factor = start_rows(z, slice(0, rows), known, *rest)
        step = second * (factor * left)
        inverse[z] = factor
        residual[z] = left
        direction[z] = step
        known = {0: own_down, planes - 1: own_up}.get(z)
        total[z] = (start[z] if known is None else known[:, :columns]) + step[:, :columns]


def halo_flux(z, wide_yz, rim_face, rim_rows, low_face, high_face, ghost_rows):
    _, planes, rows, width = wide_yz.shape
    at, row = slice(z, z + 1), row_of((rows, width))
    top = jnp.where(row == rows - 1, rim_rows[2, at] * ghost_rows[1, at], 0.0)
    flux = jnp.where(row == 0, wide_yz[0, z, 0:1] * ghost_rows[0, at], top)
    if z == 0:
        flux = flux + wide_yz[1, 0] * low_face[...]
    if z == planes - 1:
        flux = flux + rim_face[1] * high_face[0]
    return flux


def piecewise(source, target, sems):
    planes, pieces = source.shape[0], sems.shape[0]
    depth = planes // pieces
    copies = []
    for z in range(planes):
        if z % depth == depth - 1:
            at = pl.ds(z + 1 - depth, depth)
            copies.append(pltpu.make_async_copy(source.at[at], target.at[at], sems.at[z // depth]))
            copies[-1].start()
        yield
    for copy in copies:
        copy.wait()


def inner_kernel(weights, stage, wide_ax, wide_yz, rim_face, rim_rows, field, old, inverse, sum_in, *refs):
    before, first, second = weights
    rims = rim_face, rim_rows
    halo = refs[:3]
    if second:
        residual, direction, total = refs[-3:]
    else:
        residual, total = refs[-2:]
    planes, rows, columns = total.shape

    def plane(z):
        if not before:
            return field[z], old[z], sum_in[z]
        flux = halo_flux(z, wide_yz, *rims, *halo)
        step = before * (inverse[z] * flux)
        done = sum_in[z] + step[:, :columns]
        for place, number in enumerate(pieces_at(stage)):
            done = done + piece_rows(refs[4 + place], refs[3], number, z)
        return field[z] + step, old[z] + flux, done

    def coef(part, z):
        return wide_ax[part, z] if part < 2 else wide_yz[part - 2, z]

    for z, (value, left, done), image in images(
        plane, coef, planes, rim_face[1], lambda z: rim_rows[2, z : z + 1]
    ):
        left = left - image
        if second:
            step = first * value + second * (inverse[z] * left)
            residual[z] = left
            direction[z] = step
            total[z] = done + step[:, :columns]
        else:
            residual[z] = left[:, :columns]
            total[z] = done


def faces_kernel(second, wide_yz, rim_face, rim_rows, low_face, high_face, ghost_rows, inverse, direction, up, down, rows_out):
    halo = wide_yz, rim_face, rim_rows, low_face, high_face, ghost_rows
    planes, rows, _ = direction.shape
    for z, out in ((0, down.at[0]), (planes - 1, up)):
        out[...] = direction[z] + second * (inverse[z] * halo_flux(z, *halo))
    for z in range(planes):
        at = slice(z, z + 1)
        for edge, row, out in ((0, 0, 1), (1, rows - 1, 0)):
            line = slice(row, row + 1)
            if z == 0:
                rows_out[out, at] = down[0, line]
            elif z == planes - 1:
                rows_out[out, at] = up[line]
            else:
                beta = rim_rows[2, at] if edge else wide_yz[0, z, line]
                flux = beta * ghost_rows[edge, at]
                rows_out[out, at] = direction[z, line] + second * (inverse[z, line] * flux)


def last_kernel(wide_yz, rim_face, rim_rows, low_face, high_face, ghost_rows, partial, total, *refs):
    total_out, residual_out, whole, residual, total_sems, residual_sems = refs[-6:]
    planes, rows, columns = residual.shape
    copies = piecewise(whole, total_out, total_sems)
    for z in range(planes):
        done = total[z]
        for place, number in enumerate(pieces_at(SWEEPS + 1)):
            done = done + piece_rows(refs[1 + place], refs[0], number, z)
        whole[z] = done
        next(copies)
    more = piecewise(residual, residual_out, residual_sems)
    for z in range(planes):
        flux = halo_flux(z, wide_yz, rim_face, rim_rows, low_face, high_face, ghost_rows)
        residual[z] = partial[z] + flux[:, :columns]
        next(more)
    list(copies)
    list(more)


def local(old_fields, old_coef, held_slabs):
    _, slots, planes, rows, columns = old_fields.shape
    half = rows // 2
    rows = 3 * half
    width = columns + LANES
    full, own = f32(planes, rows, width), f32(planes, rows, columns)
    ids = held_slabs.reshape(2)
    vmem = pl.BlockSpec(memory_space=pltpu.VMEM)
    pairs = lax.axis_size("gy") // 2
    fields, coef, edge_out = pl.pallas_call(
        functools.partial(edge_kernel, pairs),
        out_shape=[
            f32(*old_fields.shape),
            jax.ShapeDtypeStruct(old_coef.shape, old_coef.dtype),
            f32(beyond_at(planes, half)[1] + FIRST_PAIRS, half, columns),
        ],
        in_specs=[pl.BlockSpec(memory_space=pltpu.HBM)] * 3,
        out_specs=[vmem] * 3,
        scratch_shapes=[pltpu.SMEM((2,), jnp.int32), pltpu.SemaphoreType.DMA((9,))],
        compiler_params=pltpu.CompilerParams(vmem_limit_bytes=VMEM_LIMIT),
    )(*(pltpu.with_memory_space_constraint(array, pltpu.HBM) for array in (ids, old_fields, old_coef)))
    edge_in = swapped(edge_out)
    (pairs_out,) = call(
        functools.partial(coef_kernel, FIRST_PAIRS), [f32(NEXT_PAIRS, half, columns)], ids, coef, edge_out, ids=True
    )
    pairs_in = swapped(pairs_out)
    outer_out, middle, partial, start_own, *start_out, _ = call(
        partial_kernel,
        [
            f32(outer_at(planes) + 6 + 2 * (planes // half), half, columns),
            jax.ShapeDtypeStruct((2 * (planes - 2) + 1, half, columns), jnp.int32),
            own,
            own,
            *(
                jax.ShapeDtypeStruct((2 * (end - start), half, columns), jnp.int32)
                for start, end in zip(PIECES, PIECES[1:])
            ),
            f32(slots, planes, 2 * half, columns),
        ],
        ids,
        fields,
        coef,
        pairs_out,
        ids=True,
    )
    outer_in, middle_in = swapped(outer_out), swapped(middle)
    strip = f32(STRIPS_AT[-1], half, LANES)
    left, right, outer_rows = call(
        functools.partial(strip_kernel, pairs),
        [strip, strip, f32(2, planes, columns)],
        ids,
        fields,
        coef,
        edge_in,
        ids=True,
    )
    from_left, from_right = shifted(right, "gx", 1), shifted(left, "gx", -1)
    coef_full = f32(2, planes, rows, width)
    edge_start, rhs_ghost, ghosts, own_rows, up, down, rows_out, rim_rows = call(
        functools.partial(gather_kernel, pairs),
        [
            f32(planes, rows, 2 * LANES),
            f32(planes, rows, LANES),
            f32(4, planes, rows, LANES),
            f32(3, planes, columns),
            f32(rows, width),
            f32(2, rows, width),
            f32(3, planes, width),
            f32(3, planes, width),
        ],
        ids,
        fields,
        coef,
        edge_in,
        left,
        right,
        outer_rows,
        from_left,
        from_right,
        ids=True,
    )
    low_face, rim_face = shifted(up, "gz", 1), shifted(down, "gz", -1)
    if pairs > 1:
        rim_rows = row_ghosts(rows_out)
    wide_ax, wide_yz = call(
        spread_kernel, [coef_full, coef_full], ids, coef, edge_in, pairs_in, outer_in, ghosts, ids=True
    )
    extra, part_inverse = call(
        first_kernel, [full, full], wide_ax, wide_yz, edge_start, rhs_ghost, own_rows, down, partial
    )
    first_list, second_list = chebyshev_weights(SWEEPS)
    faces = [f32(rows, width), f32(1, rows, width), f32(2, planes, width)]
    down_start = down[0]
    rest = extra, part_inverse, wide_yz, up, rows_out, low_face, rim_face, rim_rows
    up, down, rows_out = call(functools.partial(start_faces_kernel, second_list[0]), faces, outer_in, *rest)
    inverse, residual, direction, total, scales = call(
        functools.partial(start_kernel, second_list[0]), [full, full, full, own, f32(half, LANES)], outer_in, middle_in, start_own, down_start, *rest
    )
    rims, halo, pieces = (rim_face, rim_rows), (), [swapped(units) for units in start_out]
    for stage in range(1, SWEEPS + 1):
        before = second_list[stage - 1] if halo else 0.0
        last = stage == SWEEPS
        weights = (before, 0.0, 0.0) if last else (before, first_list[stage], second_list[stage])
        arrived = (*halo, scales, *(pieces[number] for number in pieces_at(stage))) if halo else ()
        halo = shifted(up, "gz", 1), shifted(down, "gz", -1), row_ghosts(rows_out)
        residual, *state = call(
            functools.partial(inner_kernel, weights, stage),
            [own, own] if last else [full, full, own],
            wide_ax,
            wide_yz,
            *rims,
            direction,
            residual,
            inverse,
            total,
            *arrived,
        )
        if last:
            more = (pieces[number] for number in pieces_at(SWEEPS + 1))
            return tuple(call(last_kernel, [own, own], wide_yz, *rims, *halo, residual, *state, scales, *more, sent=True))
        direction, total = state
        up, down, rows_out = call(
            functools.partial(faces_kernel, second_list[stage]), faces, wide_yz, *rims, *halo, inverse, direction
        )


def solution(mesh):
    in_specs = (
        P(None, "gy", "gz", None, "gx"),
        P(None, "gy", "gz", None, "gx"),
        P("gy", "gz", "gx"),
    )
    out_specs = (P("gz", "gy", "gx"), P("gz", "gy", "gx"))
    return jax.shard_map(local, mesh=mesh, in_specs=in_specs, out_specs=out_specs, check_vma=False)
```

```python
import functools

import jax
import jax.numpy as jnp
from jax import lax
from jax.experimental import pallas as pl
from jax.experimental.pallas import tpu as pltpu
from jax.sharding import PartitionSpec as P

SWEEPS = 4
LANES = 128
STRIP = SWEEPS + 1
STRIPS_AT = (0, 3, 5, 7, 10)
SHIFT = 4096.0
VMEM_LIMIT = 24 * 1024 * 1024


def chebyshev_weights(count):
    low_bound = 0.25
    high_bound = 2.0
    centre_value = 0.5 * (high_bound + low_bound)
    half_width = 0.5 * (high_bound - low_bound)
    ratio_value = centre_value / half_width
    damping = 1.0 / ratio_value
    first_list = [0.0]
    second_list = [1.0 / centre_value]
    for step_index in range(1, count):
        damping_next = 1.0 / (2.0 * ratio_value - damping)
        first_list.append(damping_next * damping)
        second_list.append(2.0 * damping_next / half_width)
        damping = damping_next
    return (first_list, second_list)


def shifted(value, axis, steps):
    count = lax.axis_size(axis)
    return lax.ppermute(value, axis, [(i, (i + steps) % count) for i in range(count)])


def swapped(value):
    return lax.ppermute(value, "gy", [(i, i ^ 1) for i in range(lax.axis_size("gy"))])


def row_ghosts(rows):
    if lax.axis_size("gy") == 2:
        return swapped(rows)
    return jnp.concatenate([shifted(rows[:1], "gy", 1), shifted(rows[1:], "gy", -1)])


def f32(*shape):
    return jax.ShapeDtypeStruct(shape, jnp.float32)


def call(kernel, outs, *operands, ids=False, sent=False):
    out_specs = [pl.BlockSpec(memory_space=pltpu.VMEM) for _ in outs]
    scratch = []
    if sent:
        out_specs = [pl.BlockSpec(memory_space=pltpu.HBM) for _ in outs]
        scratch = [pltpu.VMEM(out.shape, out.dtype) for out in outs] + [pltpu.SemaphoreType.DMA((4,)) for _ in outs]
    specs = [pl.BlockSpec(memory_space=pltpu.VMEM) for _ in operands]
    if ids:
        specs[0] = pl.BlockSpec(memory_space=pltpu.SMEM)
    return pl.pallas_call(
        kernel,
        out_shape=outs,
        in_specs=specs,
        out_specs=out_specs,
        scratch_shapes=scratch,
        compiler_params=pltpu.CompilerParams(vmem_limit_bytes=VMEM_LIMIT),
    )(*operands)


def lane_of(shape):
    return lax.broadcasted_iota(jnp.int32, shape, 1)


def row_of(shape):
    return lax.broadcasted_iota(jnp.int32, shape, 0)


def units_of(ids, half, numbers=(0, 1, 2)):
    first = 3 * (lax.axis_index("gy") // 2)
    a, b = ids[0] - first, ids[1] - first
    found = []
    for k in numbers:
        unit = (3 * half + k) % 6
        slab = unit // 2
        found.append((jnp.logical_or(a == slab, b == slab), jnp.where(a == slab, 0, 1), unit % 2))
    return found


def field_unit(fields, item, place, z):
    rows = fields.shape[3] // 2
    _, slot, part = place
    return fields[item, slot, z, pl.ds(pl.multiple_of(part * rows, rows), rows), :]


def coef_unit(coef, item, place, z):
    rows = coef.shape[3] // 2
    _, slot, part = place
    both = coef[item, slot, z].astype(jnp.float32)
    return jnp.where(part == 0, both[:rows], both[rows:])


def strip_at(item, k, z, planes):
    group = k * planes + z
    return STRIPS_AT[item] + group // (LANES // STRIP), STRIP * (group % (LANES // STRIP))


def strips(fields, coef, item, ids, half, pairs, store):
    planes, columns, rows = fields.shape[2], fields.shape[4], fields.shape[3] // 2
    lane, row = lane_of((rows, LANES)), row_of((rows, columns))
    numbers = (0, 1, 2, 3, 5) if pairs == 1 and item in (0, 3) else (0, 1, 2)
    places = units_of(ids, half, numbers)

    def cells(place, z):
        if item < 2:
            found = field_unit(fields, item, place, z)
        else:
            found = coef_unit(coef, 2 * item - 4, place, z) + SHIFT * coef_unit(coef, 2 * item - 3, place, z)
        return jnp.where(place[0], found, 0.0)

    tiles = {at: [jnp.zeros((rows, LANES), jnp.float32)] * 2 for at in range(STRIPS_AT[item], STRIPS_AT[item + 1])}
    for k in range(min(len(places), 4)):
        for z in range(planes):
            value = cells(places[k], z)
            if k == 3:
                value = jnp.where(row < rows // 2, value, cells(places[4], z))
            at, first = strip_at(item, k, z, planes)
            inside = jnp.logical_and(lane >= first, lane < first + STRIP)
            for side, start, turn in ((0, 0, first), (1, columns - LANES, (first + STRIP) % LANES)):
                part = value[:, start : start + LANES]
                part = pltpu.roll(part, turn, 1) if turn else part
                tiles[at][side] = jnp.where(inside, part, tiles[at][side])
    for at, (low, high) in tiles.items():
        store(at, low, high)


def outer_row(fields, ids, half, z):
    last = fields.shape[3] - 1
    (above_held, above_slot, _), (below_held, below_slot, _) = units_of(ids, half, (3, 5))
    above = jnp.where(above_held, fields[0, above_slot, z, 0:1], 0.0)
    below = jnp.where(below_held, fields[0, below_slot, z, last : last + 1], 0.0)
    return jnp.where(half == 0, below, above)


def brick_rows(ids, half, unit_rows):
    first = 3 * (lax.axis_index("gy") // 2)
    a, b = ids[0] - first, ids[1] - first
    found = []
    for j in range(3):
        slab = jnp.where(half == 0, j // 2, 1 + (j + 1) // 2)
        row = jnp.where((j + half) % 2 == 0, 0, 2 * unit_rows - 1)
        found.append((jnp.logical_or(a == slab, b == slab), jnp.where(a == slab, 0, 1), row))
    return found


def field_row(fields, place, z):
    last = fields.shape[3] - 1
    _, slot, row = place
    return jnp.where(row == 0, fields[0, slot, z, 0:1], fields[0, slot, z, last : last + 1])


PLANES_AT, ROWS_AT = 10, 16
FIRST_PAIRS = 20
NEXT_PAIRS = 43
PIECES = (1, 7, 15)
CODE_BITS = 20
ADDED_AT = (2, 4)


def pieces_at(stage):
    return [number for number, at in enumerate(ADDED_AT) if at == stage]


def power_of_two(number):
    size, result = jnp.abs(number), jnp.ones(number.shape, jnp.float32)
    for bit in range(7):
        factor = jnp.where(number < 0, 2.0 ** -(1 << bit), 2.0 ** (1 << bit))
        result = result * jnp.where((size >> bit) & 1 == 1, factor, 1.0)
    return result


def exponents_of(tops):
    return (jnp.floor(jnp.log2(jnp.maximum(tops, 1e-30)) + 0.001) + 1.0).astype(jnp.int32)


def encoded(tiles, factors, first):
    codes, limit = [], float((1 << CODE_BITS) - 1)
    for j, tile in enumerate(tiles):
        scaled = jnp.floor(tile * factors[:, first + j : first + j + 1] + 0.5)
        codes.append(jnp.clip(scaled, -limit, limit).astype(jnp.int32) + (1 << CODE_BITS))
    a, b, c = codes
    return a | (c & 0x7FF) << 21, b | (c >> 11) << 21


def decoded(words, scales, first):
    a, b = (word & 0x1FFFFF for word in words)
    c = lax.shift_right_logical(words[0], 21) | (lax.shift_right_logical(words[1], 21) << 11)
    tiles = []
    for j, code in enumerate((a, b, c)):
        tiles.append((code - (1 << CODE_BITS)).astype(jnp.float32) * scales[:, first + j : first + j + 1])
    return tiles


def scales_of(exponents):
    return power_of_two(exponents - CODE_BITS)


def piece_rows(piece, scales, number, z):
    at = 2 * (z - PIECES[number])
    if not 0 <= at < piece.shape[0]:
        return 0.0
    return jnp.concatenate(decoded((piece[at], piece[at + 1]), scales, 3 * (z - 1)))


def pair_order(planes):
    rest = [(2, k, z) for k in (1, 2) for z in range(1, planes)]
    return (
        [(2, 0, z) for z in range(planes)]
        + [(2, 1, 0), (2, 2, 0)]
        + rest
        + [(0, k, z) for k in range(3) for z in range(planes)]
    )


def pair_tile(ids, coef, half, number):
    part, k, z = pair_order(coef.shape[2])[number]
    place = units_of(ids, half)[k]
    return jnp.where(place[0], coef_unit(coef, part, place, z) + SHIFT * coef_unit(coef, part + 1, place, z), 0.0)


def beyond_at(planes, unit_rows):
    start = ROWS_AT + 3 * (planes // unit_rows)
    return start, start + 2 * (planes // unit_rows)


def beyond(fields, coef, ids, half, pairs, row_out):
    if pairs > 1:
        return
    (above,) = units_of(ids, half, (3,))
    for z in range(fields.shape[2]):
        row_out(0, z, outer_row(fields, ids, half, z))
        row_out(1, z, jnp.where(above[0], first_row(coef, above, z), 0.0))


def first_row(coef, place, z):
    rows = coef.shape[3] // 2
    both = coef[2, place[1], z].astype(jnp.float32)
    return jnp.where(place[2] == 0, both[0:1], both[rows : rows + 1])


def edge_kernel(pairs, ids_in, fields_in, coef_in, fields, coef, out, ids, sems):
    copies = [pltpu.make_async_copy(ids_in, ids, sems.at[0])]
    for item in range(2):
        for slot in range(2):
            at = len(copies)
            copies.append(pltpu.make_async_copy(fields_in.at[item, slot], fields.at[item, slot], sems.at[at]))
    for part in range(4):
        at = len(copies)
        copies.append(pltpu.make_async_copy(coef_in.at[part], coef.at[part], sems.at[at]))
    for copy in copies:
        copy.start()
    planes, unit_rows = fields.shape[2], fields.shape[3] // 2
    half = 1 - lax.axis_index("gy") % 2
    for copy in copies[:5]:
        copy.wait()
    def strip_out(at, low, high):
        out[at] = jnp.concatenate([low, high], axis=1)

    for item in range(4):
        if item == 2:
            for copy in copies[5:]:
                copy.wait()
        strips(fields, coef, item, ids, half, pairs, strip_out)
        if item < 2:
            for k, place in enumerate(units_of(ids, half)):
                out[PLANES_AT + 3 * item + k] = field_unit(fields, 0, place, item * (planes - 1))
    for j, place in enumerate(brick_rows(ids, half, unit_rows)):
        for z in range(planes):
            at = ROWS_AT + j * (planes // unit_rows) + z // unit_rows
            line = z % unit_rows
            out[at, line : line + 1] = field_row(fields, place, z)
    rows_at, pairs_at = beyond_at(planes, unit_rows)

    def row_out(j, z, value):
        line = z % unit_rows
        out[rows_at + j * (planes // unit_rows) + z // unit_rows, line : line + 1] = value

    beyond(fields, coef, ids, half, pairs, row_out)
    for number in range(FIRST_PAIRS):
        out[pairs_at + number] = pair_tile(ids, coef, half, number)


def coef_kernel(first, ids, coef, _, out):
    for number in range(out.shape[0]):
        out[number] = pair_tile(ids, coef, 1 - lax.axis_index("gy") % 2, first + number)


def outer_at(planes):
    return 6 * planes - FIRST_PAIRS - NEXT_PAIRS


def line_at(planes, unit_rows, edge, z):
    at = outer_at(planes) + 6 + edge * (planes // unit_rows) + z // unit_rows
    return at, slice(z % unit_rows, z % unit_rows + 1)


def partial_kernel(ids, fields, coef, _, out, middle, own, start_own, *refs):
    start_out, partial = refs[:-1], refs[-1]
    _, slots, planes, rows, columns = fields.shape
    lane, row = lane_of((rows, columns)), row_of((rows, columns))
    for slot in range(slots):
        value, lower = fields[0, slot, 0], 0.0
        for z in range(planes):
            alpha, beta_x, beta_y = (coef[part, slot, z].astype(jnp.float32) for part in range(3))
            flux_x = jnp.where(lane == 0, 0.0, beta_x * (value - pltpu.roll(value, 1, 1)))
            flux_y = jnp.where(row == 0, 0.0, beta_y * (value - pltpu.roll(value, 1, 0)))
            image = (
                alpha * value
                + (flux_x - pltpu.roll(flux_x, columns - 1, 1))
                + (flux_y - pltpu.roll(flux_y, rows - 1, 0))
                + lower
            )
            if z + 1 < planes:
                following = fields[0, slot, z + 1]
                lower = coef[3, slot, z + 1].astype(jnp.float32) * (following - value)
                image = image - lower
                value = following
            partial[slot, z] = fields[1, slot, z] - image
    half_rows = rows // 2
    half = lax.axis_index("gy") % 2
    for number in range(outer_at(planes)):
        out[number] = pair_tile(ids, coef, 1 - half, FIRST_PAIRS + NEXT_PAIRS + number)
    places = units_of(ids, half)
    for z in range(planes):
        for k, place in enumerate(places):
            held, slot, part = place
            at = pl.ds(pl.multiple_of(part * half_rows, half_rows), half_rows)
            line = slice(k * half_rows, (k + 1) * half_rows)
            own[z, line] = jnp.where(held, partial[slot, z, at, :], 0.0)
            start_own[z, line] = jnp.where(held, field_unit(fields, 0, place, z), 0.0)
    lane = lane_of((half_rows, columns))
    places = units_of(ids, 1 - half)
    tops = jnp.zeros((half_rows, columns), jnp.float32)
    shares = []
    for z in range(planes):
        lefts, starts = [], []
        for k, place in enumerate(places):
            held, slot, part = place
            at = pl.ds(pl.multiple_of(part * half_rows, half_rows), half_rows)
            lefts.append(jnp.where(held, partial[slot, z, at, :], 0.0))
            starts.append(jnp.where(held, field_unit(fields, 0, place, z), 0.0))
            if k != 1:
                row = 0 if k == 0 else half_rows - 1
                at_line, line_in = line_at(planes, half_rows, k // 2, z)
                out[at_line, line_in] = lefts[k][row : row + 1]
            if z % (planes - 1) == 0:
                out[outer_at(planes) + 3 * (z > 0) + k] = lefts[k]
        if z % (planes - 1) == 0:
            continue
        piece = sum(z >= end for end in PIECES[1:])
        shares.append((lefts, 3 * (z - 1), middle, 2 * (z - 1)))
        shares.append((starts, LANES + 3 * (z - 1), start_out[piece], 2 * (z - PIECES[piece])))
        for tiles, first, _, _ in shares[-2:]:
            for j, tile in enumerate(tiles):
                tops = jnp.where(lane == first + j, jnp.max(jnp.abs(tile), axis=1, keepdims=True), tops)
    exponents = exponents_of(tops)
    factors = power_of_two(CODE_BITS - exponents)
    for tiles, first, target, at in shares:
        target[at], target[at + 1] = encoded(tiles, factors, first)
    middle[2 * (planes - 2)] = exponents


def strip_kernel(pairs, ids, fields, coef, edge_in, left, right, outer_rows):
    planes, unit_rows = fields.shape[2], fields.shape[3] // 2
    half = lax.axis_index("gy") % 2

    def strip_out(at, low, high):
        got = edge_in[at]
        left[at], right[at] = low + got[:, :LANES], high + got[:, LANES:]

    for item in range(4):
        strips(fields, coef, item, ids, half, pairs, strip_out)
    rows_at, _ = beyond_at(planes, unit_rows)

    def row_out(j, z, value):
        line = z % unit_rows
        got = edge_in[rows_at + j * (planes // unit_rows) + z // unit_rows, line : line + 1]
        outer_rows[j, z : z + 1] = value + got

    if pairs > 1:
        outer_rows[...] = jnp.zeros_like(outer_rows)
    beyond(fields, coef, ids, half, pairs, row_out)


def parted(both):
    second = jnp.floor(both * 0.125) * (8.0 / SHIFT)
    return both - SHIFT * second, second


def ghost_columns(from_left, from_right, item, k, z, planes):
    at, first = strip_at(item, k, z, planes)
    low, high = from_left[at], from_right[at]
    turn = (LANES - first) % LANES
    right = pltpu.roll(high, turn, 1) if turn else high
    turn = (LANES - STRIP - first) % LANES
    left = pltpu.roll(low, turn, 1) if turn else low
    lane = lane_of(low.shape)
    return jnp.where(lane < STRIP, right, jnp.where(lane >= LANES - STRIP, left, 1.0))


def gather_kernel(
    pairs, ids, fields, coef, edge_in, left, right, outer_rows, from_left, from_right,
    edge_start, rhs_ghost, ghosts, own_rows, up, down, rows_out, beyond_rows,
):
    _, _, planes, rows, columns = fields.shape
    rows //= 2
    half = lax.axis_index("gy") % 2
    for k, place in enumerate(units_of(ids, half)):
        at = slice(k * rows, (k + 1) * rows)
        for z in range(planes):
            edge_start[z, at, :LANES] = ghost_columns(right, left, 0, k, z, planes)
            edge_start[z, at, LANES:] = ghost_columns(from_left, from_right, 0, k, z, planes)
            rhs_ghost[z, at] = ghost_columns(from_left, from_right, 1, k, z, planes)
            for item in (2, 3):
                both = ghost_columns(from_left, from_right, item, k, z, planes)
                part = 2 * item - 4
                ghosts[part, z, at], ghosts[part + 1, z, at] = parted(both)
        for e, (z, out) in enumerate(((0, down.at[0]), (planes - 1, up))):
            own = field_unit(fields, 0, place, z)
            out[at, :columns] = jnp.where(place[0], own, edge_in[PLANES_AT + 3 * e + k])
            out[at, columns:] = edge_start[z, at, LANES:]
    _, pairs_at = beyond_at(planes, rows)
    places = units_of(ids, half)
    for k, place in enumerate(places):
        at = slice(k * rows, (k + 1) * rows)
        down[1, at, :columns] = jnp.where(
            place[0], coef_unit(coef, 3, place, 0), parted(edge_in[pairs_at + (planes - 1 + k if k else 0)])[1]
        )
    down[1, :, columns:] = ghosts[3, 0]
    for j, place in enumerate(brick_rows(ids, half, rows)):
        for z in range(planes):
            at = ROWS_AT + j * (planes // rows) + z // rows
            line = z % rows
            own_rows[j, z : z + 1] = jnp.where(place[0], field_row(fields, place, z), edge_in[at, line : line + 1])
    last = 3 * rows - 1
    for z in range(planes):
        line = slice(z, z + 1)
        for out, row, j, known in ((0, last, 2, half == 1), (1, 0, 0, half == 0)):
            edge = edge_start[z, row : row + 1]
            middle = jnp.concatenate([edge[:, :LANES]] * (columns // LANES), axis=1)
            rows_out[out, line, :columns] = jnp.where(known, own_rows[j, line], middle)
            rows_out[out, line, columns:] = edge[:, LANES:]
        got = parted(edge_in[pairs_at + z, 0:1])[0]
        rows_out[2, line, :columns] = jnp.where(places[0][0], first_row(coef, places[0], z), got)
        rows_out[2, line, columns:] = ghosts[2, z, 0:1]
        if pairs > 1:
            continue
        own = ghost_columns(right, left, 0, 3, z, planes)
        ghost = ghost_columns(from_left, from_right, 0, 3, z, planes)
        for out, row, known in ((0, rows - 1, half == 0), (1, 0, half == 1)):
            edge = own[row : row + 1]
            middle = jnp.concatenate([edge] * (columns // LANES), axis=1)
            beyond_rows[out, line, :columns] = jnp.where(known, outer_rows[0, line], middle)
            beyond_rows[out, line, columns:] = ghost[row : row + 1]
        beyond_rows[2, line, :columns] = outer_rows[1, line]
        beyond_rows[2, line, columns:] = parted(ghost_columns(from_left, from_right, 3, 3, z, planes)[0:1])[0]
    if pairs > 1:
        beyond_rows[...] = jnp.zeros_like(beyond_rows)


def spread_kernel(
    ids, coef, edge_in, pairs, ghosts, own_rows, down, partial, middle, wide_yz, own_ax, gain, diagonal, middle_out
):
    planes, columns, rows = coef.shape[2], coef.shape[4], coef.shape[3] // 2
    places, pairs_at = units_of(ids, lax.axis_index("gy") % 2), beyond_at(planes, rows)[1]
    even = lax.axis_index("gy") % 2 == 0
    middle_out[...] = middle[...]
    for part in (0, 1):
        wide_yz[part, :, :, columns:] = ghosts[2 + part]
    for number, (part, k, z) in enumerate(pair_order(planes)):
        at = slice(k * rows, (k + 1) * rows)
        held = places[k][0]
        own = [coef_unit(coef, part + j, places[k], z) for j in (0, 1)]
        if part == 0:
            for j in (0, 1):
                own_ax[j, z, at] = jnp.where(held, own[j], 0.0)
            continue
        got = edge_in[pairs_at + number] if number < FIRST_PAIRS else pairs[number - FIRST_PAIRS]
        for j, value in enumerate(parted(got)):
            wide_yz[j, z, at, :columns] = jnp.where(held, own[j], value)
    rows *= 3
    unit_rows = rows // 3
    width = wide_yz.shape[3]
    row = row_of((rows, columns))
    inner = jnp.where(even, 2 * unit_rows, unit_rows)
    for z in range(planes):
        beta_y, beta_z, at = wide_yz[0, z], wide_yz[1, z], slice(z, z + 1)
        found = partial[z]
        if z == 0:
            found = found - (beta_z * down[0])[:, :columns]
        between = jnp.where(even, own_rows[2, at] - own_rows[1, at], own_rows[1, at] - own_rows[0, at])
        beta = jnp.where(even, beta_y[2 * unit_rows : 2 * unit_rows + 1], beta_y[unit_rows : unit_rows + 1])
        between = beta[:, :columns] * between
        found = found + jnp.where(row == inner, -between, jnp.where(row == inner - 1, between, 0.0))
        low = jnp.where(even, beta_y[0:1, :columns] * own_rows[0, at], 0.0)
        gain[z] = found - jnp.where(row == 0, low, 0.0)
        next_z = wide_yz[1, z + 1] if z + 1 < planes else 0.0
        next_y = jnp.where(row_of((rows, width)) == rows - 1, 0.0, pltpu.roll(beta_y, rows - 1, 0))
        diagonal[z] = beta_y + next_y + beta_z + next_z


def image_plane(value, lower_flux, upper_flux, alpha, beta_x, beta_y, rim_row):
    rows, width = value.shape
    flux_x = beta_x * (value - pltpu.roll(value, 1, 1))
    row = row_of(value.shape)
    before = jnp.where(row == 0, 0.0, pltpu.roll(value, 1, 0))
    flux_y = beta_y * (value - before)
    top = 0.0 if rim_row is None else -rim_row * value[rows - 1 : rows]
    after = jnp.where(row == rows - 1, top, pltpu.roll(flux_y, rows - 1, 0))
    return (
        alpha * value
        + (flux_x - pltpu.roll(flux_x, width - 1, 1))
        + (flux_y - after)
        + (lower_flux - upper_flux)
    )


def images(plane, coef, planes, rim_face, rim_row):
    (value, *others), beta_z = plane(0), coef(3, 0)
    lower = beta_z * value
    for z in range(planes):
        if z + 1 < planes:
            (following, *next_others), next_z = plane(z + 1), coef(3, z + 1)
            upper = next_z * (following - value)
        else:
            following, next_others, next_z = None, None, rim_face
            upper = 0.0 if rim_face is None else -rim_face * value
        image = image_plane(value, lower, upper, coef(0, z), coef(1, z), coef(2, z), rim_row(z))
        yield z, (value, *others), image
        value, others, lower, beta_z = following, next_others, upper, next_z


def edges(value):
    columns = value.shape[1] - LANES
    own = jnp.where(lane_of((value.shape[0], LANES)) < LANES // 2, value[:, :LANES], value[:, columns - LANES : columns])
    return jnp.concatenate([own, value[:, columns:]], axis=1)


def first_kernel(
    pairs, more_pairs, own_ax, ghosts, wide_yz, edge_start, rhs_ghost, gain, diagonal, wide_ax, extra, inverse
):
    planes, rows, width = extra.shape
    columns = width - LANES
    unit_rows = rows // 3
    for part in (0, 1):
        wide_ax[part, :, :, columns:] = ghosts[part]
    for number, (part, k, z) in enumerate(pair_order(planes)):
        if part:
            continue
        at, place_in = slice(k * unit_rows, (k + 1) * unit_rows), number - FIRST_PAIRS
        got = pairs[place_in] if place_in < pairs.shape[0] else more_pairs[place_in - pairs.shape[0]]
        for j, value in enumerate(parted(got)):
            wide_ax[j, z, at, :columns] = own_ax[j, z, at] + value

    def ring(part, z):
        return edges(wide_ax[part, z] if part < 2 else wide_yz[part - 2, z])

    lane = lane_of((rows, columns))
    for z, (value,), image in images(lambda z: (edge_start[z],), ring, planes, None, lambda z: None):
        flux = ring(1, z) * (value - pltpu.roll(value, 1, 1))
        near = jnp.where(lane == 0, -flux[:, :columns], 0.0)
        far = jnp.where(lane == columns - 1, pltpu.roll(flux, LANES - 1, 1)[:, :columns], 0.0)
        extra[z, :, :columns] = gain[z] + near + far
        extra[z, :, columns:] = rhs_ghost[z] - image[:, LANES:]
        beta_x = wide_ax[1, z]
        inverse[z] = 1.0 / (wide_ax[0, z] + beta_x + pltpu.roll(beta_x, width - 1, 1) + diagonal[z])


def start_rows(
    z, line, known, extra, part_inverse, wide_yz, own_up, own_last, low_face, high_face, ghost_rows
):
    planes, rows, width = extra.shape
    columns = known.shape[1]
    even = lax.axis_index("gy") % 2 == 0
    row = row_of((known.shape[0], width)) + line.start
    ghost = lane_of((1, width)) >= columns
    at = slice(z, z + 1)
    left = extra[z, line] + jnp.concatenate([known, jnp.zeros((known.shape[0], width - columns), jnp.float32)], axis=1)
    factor = part_inverse[z, line]
    if z == 0:
        left = left + wide_yz[1, 0, line] * low_face[line]
    if z == planes - 1:
        rim = high_face[1, line]
        left = left + rim * (high_face[0, line] - own_up[line])
        factor = factor / (1.0 + rim * factor)
    if line.start == 0:
        low = jnp.where(jnp.logical_or(ghost, even), wide_yz[0, z, 0:1] * ghost_rows[0, at], 0.0)
        left = left + jnp.where(row == 0, low, 0.0)
    if line.stop == rows:
        rim = ghost_rows[2, at]
        high = rim * (ghost_rows[1, at] - own_last[0, at])
        high = jnp.where(jnp.logical_and(jnp.logical_not(ghost), even), 0.0, high)
        left = left + jnp.where(row == rows - 1, high, 0.0)
        last = factor[factor.shape[0] - 1 :]
        factor = jnp.where(row == rows - 1, last / (1.0 + rim * last), factor)
    return left, factor


def partner_plane(z, planes, outer, middle=None, scales=None):
    if 0 < z < planes - 1:
        return jnp.concatenate(decoded((middle[2 * z - 2], middle[2 * z - 1]), scales, 3 * (z - 1)))
    return jnp.concatenate([outer[outer_at(planes) + 3 * (z > 0) + k] for k in range(3)])


def start_faces_kernel(second, outer, *refs):
    rest, (up, down, rows_out) = refs[:-3], refs[-3:]
    planes, rows, _ = rest[0].shape

    def step(z, line, known):
        left, factor = start_rows(z, line, known, *rest)
        return second * (factor * left)

    down[0] = step(0, slice(0, rows), partner_plane(0, planes, outer))
    up[...] = step(planes - 1, slice(0, rows), partner_plane(planes - 1, planes, outer))
    for z in range(planes):
        at = slice(z, z + 1)
        if z == 0:
            first, last = down[0, 0:1], down[0, rows - 1 : rows]
        elif z == planes - 1:
            first, last = up[0:1], up[rows - 1 : rows]
        else:
            lines = [outer[line_at(planes, outer.shape[1], edge, z)] for edge in range(2)]
            first, last = step(z, slice(0, 1), lines[0]), step(z, slice(rows - 1, rows), lines[1])
        rows_out[0, at], rows_out[1, at] = last, first


def start_kernel(second, outer, middle, start, *refs):
    own_down, *rest, inverse, residual, direction, total, start_scales = refs
    own_up = rest[3]
    planes, rows, _ = rest[0].shape
    columns = total.shape[2]
    scales = scales_of(middle[2 * (planes - 2)])
    start_scales[...] = scales[:, LANES:]
    for z in range(planes):
        known = partner_plane(z, planes, outer, middle, scales)
        left, factor = start_rows(z, slice(0, rows), known, *rest)
        step = second * (factor * left)
        inverse[z] = factor
        residual[z] = left
        direction[z] = step
        known = {0: own_down, planes - 1: own_up}.get(z)
        total[z] = (start[z] if known is None else known[:, :columns]) + step[:, :columns]


def halo_flux(z, wide_yz, rim_face, rim_rows, low_face, high_face, ghost_rows):
    _, planes, rows, width = wide_yz.shape
    at, row = slice(z, z + 1), row_of((rows, width))
    top = jnp.where(row == rows - 1, rim_rows[2, at] * ghost_rows[1, at], 0.0)
    flux = jnp.where(row == 0, wide_yz[0, z, 0:1] * ghost_rows[0, at], top)
    if z == 0:
        flux = flux + wide_yz[1, 0] * low_face[...]
    if z == planes - 1:
        flux = flux + rim_face[1] * high_face[0]
    return flux


def piecewise(source, target, sems):
    planes, pieces = source.shape[0], sems.shape[0]
    depth = planes // pieces
    copies = []
    for z in range(planes):
        if z % depth == depth - 1:
            at = pl.ds(z + 1 - depth, depth)
            copies.append(pltpu.make_async_copy(source.at[at], target.at[at], sems.at[z // depth]))
            copies[-1].start()
        yield
    for copy in copies:
        copy.wait()


def inner_kernel(weights, stage, wide_ax, wide_yz, rim_face, rim_rows, field, old, inverse, sum_in, *refs):
    before, first, second = weights
    rims = rim_face, rim_rows
    halo = refs[:3]
    if second:
        residual, direction, total = refs[-3:]
    else:
        residual, total = refs[-2:]
    planes, rows, columns = total.shape

    def plane(z):
        if not before:
            return field[z], old[z], sum_in[z]
        flux = halo_flux(z, wide_yz, *rims, *halo)
        step = before * (inverse[z] * flux)
        done = sum_in[z] + step[:, :columns]
        for place, number in enumerate(pieces_at(stage)):
            done = done + piece_rows(refs[4 + place], refs[3], number, z)
        return field[z] + step, old[z] + flux, done

    def coef(part, z):
        return wide_ax[part, z] if part < 2 else wide_yz[part - 2, z]

    for z, (value, left, done), image in images(
        plane, coef, planes, rim_face[1], lambda z: rim_rows[2, z : z + 1]
    ):
        left = left - image
        if second:
            step = first * value + second * (inverse[z] * left)
            residual[z] = left
            direction[z] = step
            total[z] = done + step[:, :columns]
        else:
            residual[z] = left[:, :columns]
            total[z] = done


def faces_kernel(second, wide_yz, rim_face, rim_rows, low_face, high_face, ghost_rows, inverse, direction, up, down, rows_out):
    halo = wide_yz, rim_face, rim_rows, low_face, high_face, ghost_rows
    planes, rows, _ = direction.shape
    for z, out in ((0, down.at[0]), (planes - 1, up)):
        out[...] = direction[z] + second * (inverse[z] * halo_flux(z, *halo))
    for z in range(planes):
        at = slice(z, z + 1)
        for edge, row, out in ((0, 0, 1), (1, rows - 1, 0)):
            line = slice(row, row + 1)
            if z == 0:
                rows_out[out, at] = down[0, line]
            elif z == planes - 1:
                rows_out[out, at] = up[line]
            else:
                beta = rim_rows[2, at] if edge else wide_yz[0, z, line]
                flux = beta * ghost_rows[edge, at]
                rows_out[out, at] = direction[z, line] + second * (inverse[z, line] * flux)


def last_kernel(wide_yz, rim_face, rim_rows, low_face, high_face, ghost_rows, partial, total, *refs):
    total_out, residual_out, whole, residual, total_sems, residual_sems = refs[-6:]
    planes, rows, columns = residual.shape
    copies = piecewise(whole, total_out, total_sems)
    for z in range(planes):
        done = total[z]
        for place, number in enumerate(pieces_at(SWEEPS + 1)):
            done = done + piece_rows(refs[1 + place], refs[0], number, z)
        whole[z] = done
        next(copies)
    more = piecewise(residual, residual_out, residual_sems)
    for z in range(planes):
        flux = halo_flux(z, wide_yz, rim_face, rim_rows, low_face, high_face, ghost_rows)
        residual[z] = partial[z] + flux[:, :columns]
        next(more)
    list(copies)
    list(more)


def local(old_fields, old_coef, held_slabs):
    _, slots, planes, rows, columns = old_fields.shape
    half = rows // 2
    rows = 3 * half
    width = columns + LANES
    full, own = f32(planes, rows, width), f32(planes, rows, columns)
    ids = held_slabs.reshape(2)
    vmem = pl.BlockSpec(memory_space=pltpu.VMEM)
    pairs = lax.axis_size("gy") // 2
    fields, coef, edge_out = pl.pallas_call(
        functools.partial(edge_kernel, pairs),
        out_shape=[
            f32(*old_fields.shape),
            jax.ShapeDtypeStruct(old_coef.shape, old_coef.dtype),
            f32(beyond_at(planes, half)[1] + FIRST_PAIRS, half, columns),
        ],
        in_specs=[pl.BlockSpec(memory_space=pltpu.HBM)] * 3,
        out_specs=[vmem] * 3,
        scratch_shapes=[pltpu.SMEM((2,), jnp.int32), pltpu.SemaphoreType.DMA((9,))],
        compiler_params=pltpu.CompilerParams(vmem_limit_bytes=VMEM_LIMIT),
    )(*(pltpu.with_memory_space_constraint(array, pltpu.HBM) for array in (ids, old_fields, old_coef)))
    edge_in = swapped(edge_out)
    (pairs_out,) = call(
        functools.partial(coef_kernel, FIRST_PAIRS), [f32(NEXT_PAIRS, half, columns)], ids, coef, edge_out, ids=True
    )
    pairs_in = swapped(pairs_out)
    outer_out, middle, partial, start_own, *start_out, _ = call(
        partial_kernel,
        [
            f32(outer_at(planes) + 6 + 2 * (planes // half), half, columns),
            jax.ShapeDtypeStruct((2 * (planes - 2) + 1, half, columns), jnp.int32),
            own,
            own,
            *(
                jax.ShapeDtypeStruct((2 * (end - start), half, columns), jnp.int32)
                for start, end in zip(PIECES, PIECES[1:])
            ),
            f32(slots, planes, 2 * half, columns),
        ],
        ids,
        fields,
        coef,
        pairs_out,
        ids=True,
    )
    outer_in = swapped(outer_out)
    strip = f32(STRIPS_AT[-1], half, LANES)
    left, right, outer_rows = call(
        functools.partial(strip_kernel, pairs),
        [strip, strip, f32(2, planes, columns)],
        ids,
        fields,
        coef,
        edge_in,
        ids=True,
    )
    from_left, from_right = shifted(right, "gx", 1), shifted(left, "gx", -1)
    coef_full = f32(2, planes, rows, width)
    edge_start, rhs_ghost, ghosts, own_rows, up, down, rows_out, rim_rows = call(
        functools.partial(gather_kernel, pairs),
        [
            f32(planes, rows, 2 * LANES),
            f32(planes, rows, LANES),
            f32(4, planes, rows, LANES),
            f32(3, planes, columns),
            f32(rows, width),
            f32(2, rows, width),
            f32(3, planes, width),
            f32(3, planes, width),
        ],
        ids,
        fields,
        coef,
        edge_in,
        left,
        right,
        outer_rows,
        from_left,
        from_right,
        ids=True,
    )
    low_face, rim_face = shifted(up, "gz", 1), shifted(down, "gz", -1)
    if pairs > 1:
        rim_rows = row_ghosts(rows_out)
    wide_yz, own_ax, gain, diagonal, middle = call(
        spread_kernel,
        [
            coef_full,
            f32(2, planes, rows, columns),
            own,
            full,
            jax.ShapeDtypeStruct(middle.shape, middle.dtype),
        ],
        ids,
        coef,
        edge_in,
        pairs_in,
        ghosts,
        own_rows,
        down,
        partial,
        middle,
        ids=True,
    )
    middle_in = swapped(middle)
    wide_ax, extra, part_inverse = call(
        first_kernel,
        [coef_full, full, full],
        pairs_in,
        outer_in,
        own_ax,
        ghosts,
        wide_yz,
        edge_start,
        rhs_ghost,
        gain,
        diagonal,
    )
    first_list, second_list = chebyshev_weights(SWEEPS)
    faces = [f32(rows, width), f32(1, rows, width), f32(2, planes, width)]
    down_start = down[0]
    rest = extra, part_inverse, wide_yz, up, rows_out, low_face, rim_face, rim_rows
    up, down, rows_out = call(functools.partial(start_faces_kernel, second_list[0]), faces, outer_in, *rest)
    inverse, residual, direction, total, scales = call(
        functools.partial(start_kernel, second_list[0]), [full, full, full, own, f32(half, LANES)], outer_in, middle_in, start_own, down_start, *rest
    )
    rims, halo, pieces = (rim_face, rim_rows), (), [swapped(units) for units in start_out]
    for stage in range(1, SWEEPS + 1):
        before = second_list[stage - 1] if halo else 0.0
        last = stage == SWEEPS
        weights = (before, 0.0, 0.0) if last else (before, first_list[stage], second_list[stage])
        arrived = (*halo, scales, *(pieces[number] for number in pieces_at(stage))) if halo else ()
        halo = shifted(up, "gz", 1), shifted(down, "gz", -1), row_ghosts(rows_out)
        residual, *state = call(
            functools.partial(inner_kernel, weights, stage),
            [own, own] if last else [full, full, own],
            wide_ax,
            wide_yz,
            *rims,
            direction,
            residual,
            inverse,
            total,
            *arrived,
        )
        if last:
            more = (pieces[number] for number in pieces_at(SWEEPS + 1))
            return tuple(call(last_kernel, [own, own], wide_yz, *rims, *halo, residual, *state, scales, *more, sent=True))
        direction, total = state
        up, down, rows_out = call(
            functools.partial(faces_kernel, second_list[stage]), faces, wide_yz, *rims, *halo, inverse, direction
        )


def solution(mesh):
    in_specs = (
        P(None, "gy", "gz", None, "gx"),
        P(None, "gy", "gz", None, "gx"),
        P("gy", "gz", "gx"),
    )
    out_specs = (P("gz", "gy", "gx"), P("gz", "gy", "gx"))
    return jax.shard_map(local, mesh=mesh, in_specs=in_specs, out_specs=out_specs, check_vma=False)
```

```python
import functools

import jax
import jax.numpy as jnp
from jax import lax
from jax.experimental import pallas as pl
from jax.experimental.pallas import tpu as pltpu
from jax.sharding import PartitionSpec as P

SWEEPS = 4
LANES = 128
STRIP = SWEEPS + 1
STRIPS_AT = (0, 3, 5, 7, 10)
SHIFT = 4096.0
VMEM_LIMIT = 24 * 1024 * 1024


def chebyshev_weights(count):
    low_bound = 0.25
    high_bound = 2.0
    centre_value = 0.5 * (high_bound + low_bound)
    half_width = 0.5 * (high_bound - low_bound)
    ratio_value = centre_value / half_width
    damping = 1.0 / ratio_value
    first_list = [0.0]
    second_list = [1.0 / centre_value]
    for step_index in range(1, count):
        damping_next = 1.0 / (2.0 * ratio_value - damping)
        first_list.append(damping_next * damping)
        second_list.append(2.0 * damping_next / half_width)
        damping = damping_next
    return (first_list, second_list)


def shifted(value, axis, steps):
    count = lax.axis_size(axis)
    return lax.ppermute(value, axis, [(i, (i + steps) % count) for i in range(count)])


def swapped(value):
    return lax.ppermute(value, "gy", [(i, i ^ 1) for i in range(lax.axis_size("gy"))])


def row_ghosts(rows):
    if lax.axis_size("gy") == 2:
        return swapped(rows)
    return jnp.concatenate([shifted(rows[:1], "gy", 1), shifted(rows[1:], "gy", -1)])


def f32(*shape):
    return jax.ShapeDtypeStruct(shape, jnp.float32)


def call(kernel, outs, *operands, ids=False, sent=False):
    out_specs = [pl.BlockSpec(memory_space=pltpu.VMEM) for _ in outs]
    scratch = []
    if sent:
        out_specs = [pl.BlockSpec(memory_space=pltpu.HBM) for _ in outs]
        scratch = [pltpu.VMEM(out.shape, out.dtype) for out in outs] + [pltpu.SemaphoreType.DMA((4,)) for _ in outs]
    specs = [pl.BlockSpec(memory_space=pltpu.VMEM) for _ in operands]
    if ids:
        specs[0] = pl.BlockSpec(memory_space=pltpu.SMEM)
    return pl.pallas_call(
        kernel,
        out_shape=outs,
        in_specs=specs,
        out_specs=out_specs,
        scratch_shapes=scratch,
        compiler_params=pltpu.CompilerParams(vmem_limit_bytes=VMEM_LIMIT),
    )(*operands)


def lane_of(shape):
    return lax.broadcasted_iota(jnp.int32, shape, 1)


def row_of(shape):
    return lax.broadcasted_iota(jnp.int32, shape, 0)


def units_of(ids, half, numbers=(0, 1, 2)):
    first = 3 * (lax.axis_index("gy") // 2)
    a, b = ids[0] - first, ids[1] - first
    found = []
    for k in numbers:
        unit = (3 * half + k) % 6
        slab = unit // 2
        found.append((jnp.logical_or(a == slab, b == slab), jnp.where(a == slab, 0, 1), unit % 2))
    return found


def field_unit(fields, item, place, z):
    rows = fields.shape[3] // 2
    _, slot, part = place
    return fields[item, slot, z, pl.ds(pl.multiple_of(part * rows, rows), rows), :]


def coef_unit(coef, item, place, z):
    rows = coef.shape[3] // 2
    _, slot, part = place
    both = coef[item, slot, z].astype(jnp.float32)
    return jnp.where(part == 0, both[:rows], both[rows:])


def strip_at(item, k, z, planes):
    group = k * planes + z
    return STRIPS_AT[item] + group // (LANES // STRIP), STRIP * (group % (LANES // STRIP))


def strips(fields, coef, item, ids, half, pairs, store):
    planes, columns, rows = fields.shape[2], fields.shape[4], fields.shape[3] // 2
    lane, row = lane_of((rows, LANES)), row_of((rows, columns))
    numbers = (0, 1, 2, 3, 5) if pairs == 1 and item in (0, 3) else (0, 1, 2)
    places = units_of(ids, half, numbers)

    def cells(place, z):
        if item < 2:
            found = field_unit(fields, item, place, z)
        else:
            found = coef_unit(coef, 2 * item - 4, place, z) + SHIFT * coef_unit(coef, 2 * item - 3, place, z)
        return jnp.where(place[0], found, 0.0)

    tiles = {at: [jnp.zeros((rows, LANES), jnp.float32)] * 2 for at in range(STRIPS_AT[item], STRIPS_AT[item + 1])}
    for k in range(min(len(places), 4)):
        for z in range(planes):
            value = cells(places[k], z)
            if k == 3:
                value = jnp.where(row < rows // 2, value, cells(places[4], z))
            at, first = strip_at(item, k, z, planes)
            inside = jnp.logical_and(lane >= first, lane < first + STRIP)
            for side, start, turn in ((0, 0, first), (1, columns - LANES, (first + STRIP) % LANES)):
                part = value[:, start : start + LANES]
                part = pltpu.roll(part, turn, 1) if turn else part
                tiles[at][side] = jnp.where(inside, part, tiles[at][side])
    for at, (low, high) in tiles.items():
        store(at, low, high)


def outer_row(fields, ids, half, z):
    last = fields.shape[3] - 1
    (above_held, above_slot, _), (below_held, below_slot, _) = units_of(ids, half, (3, 5))
    above = jnp.where(above_held, fields[0, above_slot, z, 0:1], 0.0)
    below = jnp.where(below_held, fields[0, below_slot, z, last : last + 1], 0.0)
    return jnp.where(half == 0, below, above)


def brick_rows(ids, half, unit_rows):
    first = 3 * (lax.axis_index("gy") // 2)
    a, b = ids[0] - first, ids[1] - first
    found = []
    for j in range(3):
        slab = jnp.where(half == 0, j // 2, 1 + (j + 1) // 2)
        row = jnp.where((j + half) % 2 == 0, 0, 2 * unit_rows - 1)
        found.append((jnp.logical_or(a == slab, b == slab), jnp.where(a == slab, 0, 1), row))
    return found


def field_row(fields, place, z):
    last = fields.shape[3] - 1
    _, slot, row = place
    return jnp.where(row == 0, fields[0, slot, z, 0:1], fields[0, slot, z, last : last + 1])


PLANES_AT, ROWS_AT = 10, 16
FIRST_PAIRS = 20
NEXT_PAIRS = 43
PIECES = (1, 4, 11, 15)
CODE_BITS = 20
ADDED_AT = (2, 4, 5)


def pieces_at(stage):
    return [number for number, at in enumerate(ADDED_AT) if at == stage]


def power_of_two(number):
    size, result = jnp.abs(number), jnp.ones(number.shape, jnp.float32)
    for bit in range(7):
        factor = jnp.where(number < 0, 2.0 ** -(1 << bit), 2.0 ** (1 << bit))
        result = result * jnp.where((size >> bit) & 1 == 1, factor, 1.0)
    return result


def exponents_of(tops):
    return (jnp.floor(jnp.log2(jnp.maximum(tops, 1e-30)) + 0.001) + 1.0).astype(jnp.int32)


def encoded(tiles, factors, first):
    codes, limit = [], float((1 << CODE_BITS) - 1)
    for j, tile in enumerate(tiles):
        scaled = jnp.floor(tile * factors[:, first + j : first + j + 1] + 0.5)
        codes.append(jnp.clip(scaled, -limit, limit).astype(jnp.int32) + (1 << CODE_BITS))
    a, b, c = codes
    return a | (c & 0x7FF) << 21, b | (c >> 11) << 21


def decoded(words, scales, first):
    a, b = (word & 0x1FFFFF for word in words)
    c = lax.shift_right_logical(words[0], 21) | (lax.shift_right_logical(words[1], 21) << 11)
    tiles = []
    for j, code in enumerate((a, b, c)):
        tiles.append((code - (1 << CODE_BITS)).astype(jnp.float32) * scales[:, first + j : first + j + 1])
    return tiles


def scales_of(exponents):
    return power_of_two(exponents - CODE_BITS)


def piece_rows(piece, scales, number, z):
    at = 2 * (z - PIECES[number])
    if not 0 <= at < piece.shape[0]:
        return 0.0
    return jnp.concatenate(decoded((piece[at], piece[at + 1]), scales, 3 * (z - 1)))


def pair_order(planes):
    rest = [(2, k, z) for k in (1, 2) for z in range(1, planes)]
    return (
        [(2, 0, z) for z in range(planes)]
        + [(2, 1, 0), (2, 2, 0)]
        + rest
        + [(0, k, z) for k in range(3) for z in range(planes)]
    )


def pair_tile(ids, coef, half, number):
    part, k, z = pair_order(coef.shape[2])[number]
    place = units_of(ids, half)[k]
    return jnp.where(place[0], coef_unit(coef, part, place, z) + SHIFT * coef_unit(coef, part + 1, place, z), 0.0)


def beyond_at(planes, unit_rows):
    start = ROWS_AT + 3 * (planes // unit_rows)
    return start, start + 2 * (planes // unit_rows)


def beyond(fields, coef, ids, half, pairs, row_out):
    if pairs > 1:
        return
    (above,) = units_of(ids, half, (3,))
    for z in range(fields.shape[2]):
        row_out(0, z, outer_row(fields, ids, half, z))
        row_out(1, z, jnp.where(above[0], first_row(coef, above, z), 0.0))


def first_row(coef, place, z):
    rows = coef.shape[3] // 2
    both = coef[2, place[1], z].astype(jnp.float32)
    return jnp.where(place[2] == 0, both[0:1], both[rows : rows + 1])


def edge_kernel(pairs, ids_in, fields_in, coef_in, fields, coef, out, ids, sems):
    copies = [pltpu.make_async_copy(ids_in, ids, sems.at[0])]
    for item in range(2):
        for slot in range(2):
            at = len(copies)
            copies.append(pltpu.make_async_copy(fields_in.at[item, slot], fields.at[item, slot], sems.at[at]))
    for part in range(4):
        at = len(copies)
        copies.append(pltpu.make_async_copy(coef_in.at[part], coef.at[part], sems.at[at]))
    for copy in copies:
        copy.start()
    planes, unit_rows = fields.shape[2], fields.shape[3] // 2
    half = 1 - lax.axis_index("gy") % 2
    for copy in copies[:5]:
        copy.wait()
    def strip_out(at, low, high):
        out[at] = jnp.concatenate([low, high], axis=1)

    for item in range(4):
        if item == 2:
            for copy in copies[5:]:
                copy.wait()
        strips(fields, coef, item, ids, half, pairs, strip_out)
        if item < 2:
            for k, place in enumerate(units_of(ids, half)):
                out[PLANES_AT + 3 * item + k] = field_unit(fields, 0, place, item * (planes - 1))
    for j, place in enumerate(brick_rows(ids, half, unit_rows)):
        for z in range(planes):
            at = ROWS_AT + j * (planes // unit_rows) + z // unit_rows
            line = z % unit_rows
            out[at, line : line + 1] = field_row(fields, place, z)
    rows_at, pairs_at = beyond_at(planes, unit_rows)

    def row_out(j, z, value):
        line = z % unit_rows
        out[rows_at + j * (planes // unit_rows) + z // unit_rows, line : line + 1] = value

    beyond(fields, coef, ids, half, pairs, row_out)
    for number in range(FIRST_PAIRS):
        out[pairs_at + number] = pair_tile(ids, coef, half, number)


def coef_kernel(first, ids, coef, _, out):
    for number in range(out.shape[0]):
        out[number] = pair_tile(ids, coef, 1 - lax.axis_index("gy") % 2, first + number)


def outer_at(planes):
    return 6 * planes - FIRST_PAIRS - NEXT_PAIRS


def line_at(planes, unit_rows, edge, z):
    at = outer_at(planes) + 6 + edge * (planes // unit_rows) + z // unit_rows
    return at, slice(z % unit_rows, z % unit_rows + 1)


def partial_kernel(ids, fields, coef, _, out, middle, own, start_own, *refs):
    start_out, partial = refs[:-1], refs[-1]
    _, slots, planes, rows, columns = fields.shape
    lane, row = lane_of((rows, columns)), row_of((rows, columns))
    for slot in range(slots):
        value, lower = fields[0, slot, 0], 0.0
        for z in range(planes):
            alpha, beta_x, beta_y = (coef[part, slot, z].astype(jnp.float32) for part in range(3))
            flux_x = jnp.where(lane == 0, 0.0, beta_x * (value - pltpu.roll(value, 1, 1)))
            flux_y = jnp.where(row == 0, 0.0, beta_y * (value - pltpu.roll(value, 1, 0)))
            image = (
                alpha * value
                + (flux_x - pltpu.roll(flux_x, columns - 1, 1))
                + (flux_y - pltpu.roll(flux_y, rows - 1, 0))
                + lower
            )
            if z + 1 < planes:
                following = fields[0, slot, z + 1]
                lower = coef[3, slot, z + 1].astype(jnp.float32) * (following - value)
                image = image - lower
                value = following
            partial[slot, z] = fields[1, slot, z] - image
    half_rows = rows // 2
    half = lax.axis_index("gy") % 2
    for number in range(outer_at(planes)):
        out[number] = pair_tile(ids, coef, 1 - half, FIRST_PAIRS + NEXT_PAIRS + number)
    places = units_of(ids, half)
    for z in range(planes):
        for k, place in enumerate(places):
            held, slot, part = place
            at = pl.ds(pl.multiple_of(part * half_rows, half_rows), half_rows)
            line = slice(k * half_rows, (k + 1) * half_rows)
            own[z, line] = jnp.where(held, partial[slot, z, at, :], 0.0)
            start_own[z, line] = jnp.where(held, field_unit(fields, 0, place, z), 0.0)
    lane = lane_of((half_rows, columns))
    places = units_of(ids, 1 - half)
    tops = jnp.zeros((half_rows, columns), jnp.float32)
    shares = []
    for z in range(planes):
        lefts, starts = [], []
        for k, place in enumerate(places):
            held, slot, part = place
            at = pl.ds(pl.multiple_of(part * half_rows, half_rows), half_rows)
            lefts.append(jnp.where(held, partial[slot, z, at, :], 0.0))
            starts.append(jnp.where(held, field_unit(fields, 0, place, z), 0.0))
            if k != 1:
                row = 0 if k == 0 else half_rows - 1
                at_line, line_in = line_at(planes, half_rows, k // 2, z)
                out[at_line, line_in] = lefts[k][row : row + 1]
            if z % (planes - 1) == 0:
                out[outer_at(planes) + 3 * (z > 0) + k] = lefts[k]
        if z % (planes - 1) == 0:
            continue
        piece = sum(z >= end for end in PIECES[1:])
        shares.append((lefts, 3 * (z - 1), middle, 2 * (z - 1)))
        shares.append((starts, LANES + 3 * (z - 1), start_out[piece], 2 * (z - PIECES[piece])))
        for tiles, first, _, _ in shares[-2:]:
            for j, tile in enumerate(tiles):
                tops = jnp.where(lane == first + j, jnp.max(jnp.abs(tile), axis=1, keepdims=True), tops)
    exponents = exponents_of(tops)
    factors = power_of_two(CODE_BITS - exponents)
    for tiles, first, target, at in shares:
        target[at], target[at + 1] = encoded(tiles, factors, first)
    middle[2 * (planes - 2)] = exponents


def strip_kernel(pairs, ids, fields, coef, edge_in, left, right, outer_rows):
    planes, unit_rows = fields.shape[2], fields.shape[3] // 2
    half = lax.axis_index("gy") % 2

    def strip_out(at, low, high):
        got = edge_in[at]
        left[at], right[at] = low + got[:, :LANES], high + got[:, LANES:]

    for item in range(4):
        strips(fields, coef, item, ids, half, pairs, strip_out)
    rows_at, _ = beyond_at(planes, unit_rows)

    def row_out(j, z, value):
        line = z % unit_rows
        got = edge_in[rows_at + j * (planes // unit_rows) + z // unit_rows, line : line + 1]
        outer_rows[j, z : z + 1] = value + got

    if pairs > 1:
        outer_rows[...] = jnp.zeros_like(outer_rows)
    beyond(fields, coef, ids, half, pairs, row_out)


def parted(both):
    second = jnp.floor(both * 0.125) * (8.0 / SHIFT)
    return both - SHIFT * second, second


def ghost_columns(from_left, from_right, item, k, z, planes):
    at, first = strip_at(item, k, z, planes)
    low, high = from_left[at], from_right[at]
    turn = (LANES - first) % LANES
    right = pltpu.roll(high, turn, 1) if turn else high
    turn = (LANES - STRIP - first) % LANES
    left = pltpu.roll(low, turn, 1) if turn else low
    lane = lane_of(low.shape)
    return jnp.where(lane < STRIP, right, jnp.where(lane >= LANES - STRIP, left, 1.0))


def gather_kernel(
    pairs, ids, fields, coef, edge_in, left, right, outer_rows, from_left, from_right,
    edge_start, rhs_ghost, ghosts, own_rows, up, down, rows_out, beyond_rows,
):
    _, _, planes, rows, columns = fields.shape
    rows //= 2
    half = lax.axis_index("gy") % 2
    for k, place in enumerate(units_of(ids, half)):
        at = slice(k * rows, (k + 1) * rows)
        for z in range(planes):
            edge_start[z, at, :LANES] = ghost_columns(right, left, 0, k, z, planes)
            edge_start[z, at, LANES:] = ghost_columns(from_left, from_right, 0, k, z, planes)
            rhs_ghost[z, at] = ghost_columns(from_left, from_right, 1, k, z, planes)
            for item in (2, 3):
                both = ghost_columns(from_left, from_right, item, k, z, planes)
                part = 2 * item - 4
                ghosts[part, z, at], ghosts[part + 1, z, at] = parted(both)
        for e, (z, out) in enumerate(((0, down.at[0]), (planes - 1, up))):
            own = field_unit(fields, 0, place, z)
            out[at, :columns] = jnp.where(place[0], own, edge_in[PLANES_AT + 3 * e + k])
            out[at, columns:] = edge_start[z, at, LANES:]
    _, pairs_at = beyond_at(planes, rows)
    places = units_of(ids, half)
    for k, place in enumerate(places):
        at = slice(k * rows, (k + 1) * rows)
        down[1, at, :columns] = jnp.where(
            place[0], coef_unit(coef, 3, place, 0), parted(edge_in[pairs_at + (planes - 1 + k if k else 0)])[1]
        )
    down[1, :, columns:] = ghosts[3, 0]
    for j, place in enumerate(brick_rows(ids, half, rows)):
        for z in range(planes):
            at = ROWS_AT + j * (planes // rows) + z // rows
            line = z % rows
            own_rows[j, z : z + 1] = jnp.where(place[0], field_row(fields, place, z), edge_in[at, line : line + 1])
    last = 3 * rows - 1
    for z in range(planes):
        line = slice(z, z + 1)
        for out, row, j, known in ((0, last, 2, half == 1), (1, 0, 0, half == 0)):
            edge = edge_start[z, row : row + 1]
            middle = jnp.concatenate([edge[:, :LANES]] * (columns // LANES), axis=1)
            rows_out[out, line, :columns] = jnp.where(known, own_rows[j, line], middle)
            rows_out[out, line, columns:] = edge[:, LANES:]
        got = parted(edge_in[pairs_at + z, 0:1])[0]
        rows_out[2, line, :columns] = jnp.where(places[0][0], first_row(coef, places[0], z), got)
        rows_out[2, line, columns:] = ghosts[2, z, 0:1]
        if pairs > 1:
            continue
        own = ghost_columns(right, left, 0, 3, z, planes)
        ghost = ghost_columns(from_left, from_right, 0, 3, z, planes)
        for out, row, known in ((0, rows - 1, half == 0), (1, 0, half == 1)):
            edge = own[row : row + 1]
            middle = jnp.concatenate([edge] * (columns // LANES), axis=1)
            beyond_rows[out, line, :columns] = jnp.where(known, outer_rows[0, line], middle)
            beyond_rows[out, line, columns:] = ghost[row : row + 1]
        beyond_rows[2, line, :columns] = outer_rows[1, line]
        beyond_rows[2, line, columns:] = parted(ghost_columns(from_left, from_right, 3, 3, z, planes)[0:1])[0]
    if pairs > 1:
        beyond_rows[...] = jnp.zeros_like(beyond_rows)


def spread_kernel(
    ids, coef, edge_in, pairs, ghosts, own_rows, down, partial, middle, wide_yz, own_ax, gain, diagonal, middle_out
):
    planes, columns, rows = coef.shape[2], coef.shape[4], coef.shape[3] // 2
    places, pairs_at = units_of(ids, lax.axis_index("gy") % 2), beyond_at(planes, rows)[1]
    even = lax.axis_index("gy") % 2 == 0
    middle_out[...] = middle[...]
    for part in (0, 1):
        wide_yz[part, :, :, columns:] = ghosts[2 + part]
    for number, (part, k, z) in enumerate(pair_order(planes)):
        at = slice(k * rows, (k + 1) * rows)
        held = places[k][0]
        own = [coef_unit(coef, part + j, places[k], z) for j in (0, 1)]
        if part == 0:
            for j in (0, 1):
                own_ax[j, z, at] = jnp.where(held, own[j], 0.0)
            continue
        got = edge_in[pairs_at + number] if number < FIRST_PAIRS else pairs[number - FIRST_PAIRS]
        for j, value in enumerate(parted(got)):
            wide_yz[j, z, at, :columns] = jnp.where(held, own[j], value)
    rows *= 3
    unit_rows = rows // 3
    width = wide_yz.shape[3]
    row = row_of((rows, columns))
    inner = jnp.where(even, 2 * unit_rows, unit_rows)
    for z in range(planes):
        beta_y, beta_z, at = wide_yz[0, z], wide_yz[1, z], slice(z, z + 1)
        found = partial[z]
        if z == 0:
            found = found - (beta_z * down[0])[:, :columns]
        between = jnp.where(even, own_rows[2, at] - own_rows[1, at], own_rows[1, at] - own_rows[0, at])
        beta = jnp.where(even, beta_y[2 * unit_rows : 2 * unit_rows + 1], beta_y[unit_rows : unit_rows + 1])
        between = beta[:, :columns] * between
        found = found + jnp.where(row == inner, -between, jnp.where(row == inner - 1, between, 0.0))
        low = jnp.where(even, beta_y[0:1, :columns] * own_rows[0, at], 0.0)
        gain[z] = found - jnp.where(row == 0, low, 0.0)
        next_z = wide_yz[1, z + 1] if z + 1 < planes else 0.0
        next_y = jnp.where(row_of((rows, width)) == rows - 1, 0.0, pltpu.roll(beta_y, rows - 1, 0))
        diagonal[z] = beta_y + next_y + beta_z + next_z


def image_plane(value, lower_flux, upper_flux, alpha, beta_x, beta_y, rim_row):
    rows, width = value.shape
    flux_x = beta_x * (value - pltpu.roll(value, 1, 1))
    row = row_of(value.shape)
    before = jnp.where(row == 0, 0.0, pltpu.roll(value, 1, 0))
    flux_y = beta_y * (value - before)
    top = 0.0 if rim_row is None else -rim_row * value[rows - 1 : rows]
    after = jnp.where(row == rows - 1, top, pltpu.roll(flux_y, rows - 1, 0))
    return (
        alpha * value
        + (flux_x - pltpu.roll(flux_x, width - 1, 1))
        + (flux_y - after)
        + (lower_flux - upper_flux)
    )


def images(plane, coef, planes, rim_face, rim_row):
    (value, *others), beta_z = plane(0), coef(3, 0)
    lower = beta_z * value
    for z in range(planes):
        if z + 1 < planes:
            (following, *next_others), next_z = plane(z + 1), coef(3, z + 1)
            upper = next_z * (following - value)
        else:
            following, next_others, next_z = None, None, rim_face
            upper = 0.0 if rim_face is None else -rim_face * value
        image = image_plane(value, lower, upper, coef(0, z), coef(1, z), coef(2, z), rim_row(z))
        yield z, (value, *others), image
        value, others, lower, beta_z = following, next_others, upper, next_z


def edges(value):
    columns = value.shape[1] - LANES
    own = jnp.where(lane_of((value.shape[0], LANES)) < LANES // 2, value[:, :LANES], value[:, columns - LANES : columns])
    return jnp.concatenate([own, value[:, columns:]], axis=1)


def first_kernel(
    pairs, more_pairs, own_ax, ghosts, wide_yz, edge_start, rhs_ghost, gain, diagonal, wide_ax, extra, inverse
):
    planes, rows, width = extra.shape
    columns = width - LANES
    unit_rows = rows // 3
    for part in (0, 1):
        wide_ax[part, :, :, columns:] = ghosts[part]
    for number, (part, k, z) in enumerate(pair_order(planes)):
        if part:
            continue
        at, place_in = slice(k * unit_rows, (k + 1) * unit_rows), number - FIRST_PAIRS
        got = pairs[place_in] if place_in < pairs.shape[0] else more_pairs[place_in - pairs.shape[0]]
        for j, value in enumerate(parted(got)):
            wide_ax[j, z, at, :columns] = own_ax[j, z, at] + value

    def ring(part, z):
        return edges(wide_ax[part, z] if part < 2 else wide_yz[part - 2, z])

    lane = lane_of((rows, columns))
    for z, (value,), image in images(lambda z: (edge_start[z],), ring, planes, None, lambda z: None):
        flux = ring(1, z) * (value - pltpu.roll(value, 1, 1))
        near = jnp.where(lane == 0, -flux[:, :columns], 0.0)
        far = jnp.where(lane == columns - 1, pltpu.roll(flux, LANES - 1, 1)[:, :columns], 0.0)
        extra[z, :, :columns] = gain[z] + near + far
        extra[z, :, columns:] = rhs_ghost[z] - image[:, LANES:]
        beta_x = wide_ax[1, z]
        inverse[z] = 1.0 / (wide_ax[0, z] + beta_x + pltpu.roll(beta_x, width - 1, 1) + diagonal[z])


def start_rows(
    z, line, known, extra, part_inverse, wide_yz, own_up, own_last, low_face, high_face, ghost_rows
):
    planes, rows, width = extra.shape
    columns = known.shape[1]
    even = lax.axis_index("gy") % 2 == 0
    row = row_of((known.shape[0], width)) + line.start
    ghost = lane_of((1, width)) >= columns
    at = slice(z, z + 1)
    left = extra[z, line] + jnp.concatenate([known, jnp.zeros((known.shape[0], width - columns), jnp.float32)], axis=1)
    factor = part_inverse[z, line]
    if z == 0:
        left = left + wide_yz[1, 0, line] * low_face[line]
    if z == planes - 1:
        rim = high_face[1, line]
        left = left + rim * (high_face[0, line] - own_up[line])
        factor = factor / (1.0 + rim * factor)
    if line.start == 0:
        low = jnp.where(jnp.logical_or(ghost, even), wide_yz[0, z, 0:1] * ghost_rows[0, at], 0.0)
        left = left + jnp.where(row == 0, low, 0.0)
    if line.stop == rows:
        rim = ghost_rows[2, at]
        high = rim * (ghost_rows[1, at] - own_last[0, at])
        high = jnp.where(jnp.logical_and(jnp.logical_not(ghost), even), 0.0, high)
        left = left + jnp.where(row == rows - 1, high, 0.0)
        last = factor[factor.shape[0] - 1 :]
        factor = jnp.where(row == rows - 1, last / (1.0 + rim * last), factor)
    return left, factor


def partner_plane(z, planes, outer, middle=None, scales=None):
    if 0 < z < planes - 1:
        return jnp.concatenate(decoded((middle[2 * z - 2], middle[2 * z - 1]), scales, 3 * (z - 1)))
    return jnp.concatenate([outer[outer_at(planes) + 3 * (z > 0) + k] for k in range(3)])


def start_faces_kernel(second, outer, *refs):
    rest, (up, down, rows_out) = refs[:-3], refs[-3:]
    planes, rows, _ = rest[0].shape

    def step(z, line, known):
        left, factor = start_rows(z, line, known, *rest)
        return second * (factor * left)

    down[0] = step(0, slice(0, rows), partner_plane(0, planes, outer))
    up[...] = step(planes - 1, slice(0, rows), partner_plane(planes - 1, planes, outer))
    for z in range(planes):
        at = slice(z, z + 1)
        if z == 0:
            first, last = down[0, 0:1], down[0, rows - 1 : rows]
        elif z == planes - 1:
            first, last = up[0:1], up[rows - 1 : rows]
        else:
            lines = [outer[line_at(planes, outer.shape[1], edge, z)] for edge in range(2)]
            first, last = step(z, slice(0, 1), lines[0]), step(z, slice(rows - 1, rows), lines[1])
        rows_out[0, at], rows_out[1, at] = last, first


def start_kernel(second, outer, middle, start, *refs):
    own_down, *rest, inverse, residual, direction, total, start_scales = refs
    own_up = rest[3]
    planes, rows, _ = rest[0].shape
    columns = total.shape[2]
    scales = scales_of(middle[2 * (planes - 2)])
    start_scales[...] = scales[:, LANES:]
    for z in range(planes):
        known = partner_plane(z, planes, outer, middle, scales)
        left, factor = start_rows(z, slice(0, rows), known, *rest)
        step = second * (factor * left)
        inverse[z] = factor
        residual[z] = left
        direction[z] = step
        known = {0: own_down, planes - 1: own_up}.get(z)
        total[z] = (start[z] if known is None else known[:, :columns]) + step[:, :columns]


def halo_flux(z, wide_yz, rim_face, rim_rows, low_face, high_face, ghost_rows):
    planes, (rows, width) = wide_yz.shape[1], low_face.shape
    at, row, wide = slice(z, z + 1), row_of((rows, width)), slice(0, width)
    top = jnp.where(row == rows - 1, rim_rows[2, at, wide] * ghost_rows[1, at], 0.0)
    flux = jnp.where(row == 0, wide_yz[0, z, 0:1, wide] * ghost_rows[0, at], top)
    if z == 0:
        flux = flux + wide_yz[1, 0, :, wide] * low_face[...]
    if z == planes - 1:
        flux = flux + rim_face[1, :, wide] * high_face[0]
    return flux


def piecewise(source, target, sems):
    planes, pieces = source.shape[0], sems.shape[0]
    depth = planes // pieces
    copies = []
    for z in range(planes):
        if z % depth == depth - 1:
            at = pl.ds(z + 1 - depth, depth)
            copies.append(pltpu.make_async_copy(source.at[at], target.at[at], sems.at[z // depth]))
            copies[-1].start()
        yield
    for copy in copies:
        copy.wait()


def inner_kernel(weights, stage, wide_ax, wide_yz, rim_face, rim_rows, field, old, inverse, sum_in, *refs):
    before, first, second = weights
    rims = rim_face, rim_rows
    halo = refs[:3]
    if second:
        residual, direction, total = refs[-3:]
    else:
        residual, total = refs[-2:]
    planes, rows, columns = total.shape

    def plane(z):
        if not before:
            return field[z], old[z], sum_in[z]
        flux = halo_flux(z, wide_yz, *rims, *halo)
        step = before * (inverse[z] * flux)
        done = sum_in[z] + step[:, :columns]
        for place, number in enumerate(pieces_at(stage)):
            done = done + piece_rows(refs[4 + place], refs[3], number, z)
        return field[z] + step, old[z] + flux, done

    def coef(part, z):
        return wide_ax[part, z] if part < 2 else wide_yz[part - 2, z]

    for z, (value, left, done), image in images(
        plane, coef, planes, rim_face[1], lambda z: rim_rows[2, z : z + 1]
    ):
        left = left - image
        if second:
            step = first * value + second * (inverse[z] * left)
            residual[z] = left
            direction[z] = step
            total[z] = done + step[:, :columns]
        else:
            residual[z] = left[:, :columns]
            total[z] = done


def faces_kernel(second, wide_yz, rim_face, rim_rows, low_face, high_face, ghost_rows, inverse, direction, up, down, rows_out):
    halo = wide_yz, rim_face, rim_rows, low_face, high_face, ghost_rows
    planes, rows, _ = direction.shape
    wide = slice(0, up.shape[1])
    for z, out in ((0, down.at[0]), (planes - 1, up)):
        out[...] = (direction[z] + second * (inverse[z] * halo_flux(z, *halo)))[:, wide]
    for z in range(planes):
        at = slice(z, z + 1)
        for edge, row, out in ((0, 0, 1), (1, rows - 1, 0)):
            line = slice(row, row + 1)
            if z == 0:
                rows_out[out, at] = down[0, line]
            elif z == planes - 1:
                rows_out[out, at] = up[line]
            else:
                beta = rim_rows[2, at, wide] if edge else wide_yz[0, z, line, wide]
                flux = beta * ghost_rows[edge, at, wide]
                rows_out[out, at] = direction[z, line, wide] + second * (inverse[z, line, wide] * flux)


def last_kernel(wide_yz, rim_face, rim_rows, low_face, high_face, ghost_rows, partial, total, *refs):
    total_out, residual_out, whole, residual, total_sems, residual_sems = refs[-6:]
    planes, rows, columns = residual.shape
    copies = piecewise(whole, total_out, total_sems)
    for z in range(planes):
        done = total[z]
        for place, number in enumerate(pieces_at(SWEEPS + 1)):
            done = done + piece_rows(refs[1 + place], refs[0], number, z)
        whole[z] = done
        next(copies)
    more = piecewise(residual, residual_out, residual_sems)
    for z in range(planes):
        flux = halo_flux(z, wide_yz, rim_face, rim_rows, low_face, high_face, ghost_rows)
        residual[z] = partial[z] + flux[:, :columns]
        next(more)
    list(copies)
    list(more)


def local(old_fields, old_coef, held_slabs):
    _, slots, planes, rows, columns = old_fields.shape
    half = rows // 2
    rows = 3 * half
    width = columns + LANES
    full, own = f32(planes, rows, width), f32(planes, rows, columns)
    ids = held_slabs.reshape(2)
    vmem = pl.BlockSpec(memory_space=pltpu.VMEM)
    pairs = lax.axis_size("gy") // 2
    fields, coef, edge_out = pl.pallas_call(
        functools.partial(edge_kernel, pairs),
        out_shape=[
            f32(*old_fields.shape),
            jax.ShapeDtypeStruct(old_coef.shape, old_coef.dtype),
            f32(beyond_at(planes, half)[1] + FIRST_PAIRS, half, columns),
        ],
        in_specs=[pl.BlockSpec(memory_space=pltpu.HBM)] * 3,
        out_specs=[vmem] * 3,
        scratch_shapes=[pltpu.SMEM((2,), jnp.int32), pltpu.SemaphoreType.DMA((9,))],
        compiler_params=pltpu.CompilerParams(vmem_limit_bytes=VMEM_LIMIT),
    )(*(pltpu.with_memory_space_constraint(array, pltpu.HBM) for array in (ids, old_fields, old_coef)))
    edge_in = swapped(edge_out)
    (pairs_out,) = call(
        functools.partial(coef_kernel, FIRST_PAIRS), [f32(NEXT_PAIRS, half, columns)], ids, coef, edge_out, ids=True
    )
    pairs_in = swapped(pairs_out)
    outer_out, middle, partial, start_own, *start_out, _ = call(
        partial_kernel,
        [
            f32(outer_at(planes) + 6 + 2 * (planes // half), half, columns),
            jax.ShapeDtypeStruct((2 * (planes - 2) + 1, half, columns), jnp.int32),
            own,
            own,
            *(
                jax.ShapeDtypeStruct((2 * (end - start), half, columns), jnp.int32)
                for start, end in zip(PIECES, PIECES[1:])
            ),
            f32(slots, planes, 2 * half, columns),
        ],
        ids,
        fields,
        coef,
        pairs_out,
        ids=True,
    )
    outer_in = swapped(outer_out)
    strip = f32(STRIPS_AT[-1], half, LANES)
    left, right, outer_rows = call(
        functools.partial(strip_kernel, pairs),
        [strip, strip, f32(2, planes, columns)],
        ids,
        fields,
        coef,
        edge_in,
        ids=True,
    )
    from_left, from_right = shifted(right, "gx", 1), shifted(left, "gx", -1)
    coef_full = f32(2, planes, rows, width)
    edge_start, rhs_ghost, ghosts, own_rows, up, down, rows_out, rim_rows = call(
        functools.partial(gather_kernel, pairs),
        [
            f32(planes, rows, 2 * LANES),
            f32(planes, rows, LANES),
            f32(4, planes, rows, LANES),
            f32(3, planes, columns),
            f32(rows, width),
            f32(2, rows, width),
            f32(3, planes, width),
            f32(3, planes, width),
        ],
        ids,
        fields,
        coef,
        edge_in,
        left,
        right,
        outer_rows,
        from_left,
        from_right,
        ids=True,
    )
    low_face, rim_face = shifted(up, "gz", 1), shifted(down, "gz", -1)
    if pairs > 1:
        rim_rows = row_ghosts(rows_out)
    wide_yz, own_ax, gain, diagonal, middle = call(
        spread_kernel,
        [
            coef_full,
            f32(2, planes, rows, columns),
            own,
            full,
            jax.ShapeDtypeStruct(middle.shape, middle.dtype),
        ],
        ids,
        coef,
        edge_in,
        pairs_in,
        ghosts,
        own_rows,
        down,
        partial,
        middle,
        ids=True,
    )
    middle_in = swapped(middle)
    wide_ax, extra, part_inverse = call(
        first_kernel,
        [coef_full, full, full],
        pairs_in,
        outer_in,
        own_ax,
        ghosts,
        wide_yz,
        edge_start,
        rhs_ghost,
        gain,
        diagonal,
    )
    first_list, second_list = chebyshev_weights(SWEEPS)
    faces = [f32(rows, width), f32(1, rows, width), f32(2, planes, width)]
    down_start = down[0]
    rest = extra, part_inverse, wide_yz, up, rows_out, low_face, rim_face, rim_rows
    up, down, rows_out = call(functools.partial(start_faces_kernel, second_list[0]), faces, outer_in, *rest)
    inverse, residual, direction, total, scales = call(
        functools.partial(start_kernel, second_list[0]), [full, full, full, own, f32(half, LANES)], outer_in, middle_in, start_own, down_start, *rest
    )
    rims, halo, pieces = (rim_face, rim_rows), (), [swapped(units) for units in start_out]
    for stage in range(1, SWEEPS + 1):
        before = second_list[stage - 1] if halo else 0.0
        last = stage == SWEEPS
        weights = (before, 0.0, 0.0) if last else (before, first_list[stage], second_list[stage])
        arrived = (*halo, scales, *(pieces[number] for number in pieces_at(stage))) if halo else ()
        halo = shifted(up, "gz", 1), shifted(down, "gz", -1), row_ghosts(rows_out)
        residual, *state = call(
            functools.partial(inner_kernel, weights, stage),
            [own, own] if last else [full, full, own],
            wide_ax,
            wide_yz,
            *rims,
            direction,
            residual,
            inverse,
            total,
            *arrived,
        )
        if last:
            more = (pieces[number] for number in pieces_at(SWEEPS + 1))
            return tuple(call(last_kernel, [own, own], wide_yz, *rims, *halo, residual, *state, scales, *more, sent=True))
        direction, total = state
        wide = columns if stage == SWEEPS - 1 else width
        faces = [f32(rows, wide), f32(1, rows, wide), f32(2, planes, wide)]
        up, down, rows_out = call(
            functools.partial(faces_kernel, second_list[stage]), faces, wide_yz, *rims, *halo, inverse, direction
        )


def solution(mesh):
    in_specs = (
        P(None, "gy", "gz", None, "gx"),
        P(None, "gy", "gz", None, "gx"),
        P("gy", "gz", "gx"),
    )
    out_specs = (P("gz", "gy", "gx"), P("gz", "gy", "gx"))
    return jax.shard_map(local, mesh=mesh, in_specs=in_specs, out_specs=out_specs, check_vma=False)
```
